32 devices in a mesh: ep: 16 (over z, y, x), rep: 2 (over core).
Axes of the slice: x: 2, y: 2, z: 4, core: 2. Of those that a mesh axis runs over, the one named last changes fastest.
Arguments:
- dy: bfloat16 [512, 2048], P('ep'), may hold values from -6 to 6
- probs: float32 [512, 8], P('ep'), may hold values from 0.02 to 0.5
- expert_ids: int32 [512, 8], P('ep'), may hold values from 0 to 15, as said below
- copy_choice: int32 [512, 8], P('ep'), may hold values from 0 to 1, as said below
- saved_inputs: bfloat16 [16, 2, 16, 16, 2048], P('ep', 'rep'), may hold values from -24 to 24
- saved_gate: bfloat16 [16, 2, 16, 16, 768], P('ep', 'rep'), may hold values from -4 to 4
- saved_up: bfloat16 [16, 2, 16, 16, 768], P('ep', 'rep'), may hold values from -12 to 12
- down_weight: bfloat16 [16, 768, 2048], P('ep', None, 'rep'), may hold values from -4 to 4
- gate_weight: bfloat16 [16, 2048, 768], P('ep', 'rep'), may hold values from -4 to 4
- up_weight: bfloat16 [16, 2048, 768], P('ep', 'rep'), may hold values from -4 to 4
- new_owner: int32 [16], replicated, may hold values from 0 to 15, each once
Outputs:
- new_gate: bfloat16 [16, 2048, 768], P('ep', 'rep')
- new_up: bfloat16 [16, 2048, 768], P('ep', 'rep')
The draws below stay inside these ranges and needn't reach their ends.
Inputs may be any that keep to these rules, and one draw needn't show every extreme that they name: `expert_ids`: each row names 8 different experts; the rows of one index of ep name each expert at most 2 * 16 times. `copy_choice`: of the pairs of the rows of one index of ep that name one expert, at most 16 take each copy; some take exactly 16 in every draw. `new_owner`: each expert has exactly one owner.
All inputs are finite; a program needn't handle non-finite values.
Results may differ from the reference program's by a relative error of at most 0.0056.
Values may be sent and summed in bfloat16 or wider, within the bound.
No kernel may reach another device: no remote copies, remote signals or barrier semaphores. Data moves between devices by JAX's collectives and lax.ppermute only.
A program may use at most 64 MiB of HBM per device.

```python
import math
import jax
import jax.numpy as jnp
from jax import lax

D = 2048
F = 768
TOP = 8
EXPERTS = 16
COPIES = 2
TOK_EP = 32
TOKENS = 512
MC = 16
ITERS = 2
N_EP = 16


def make_routing(key):
    base_key = jax.random.fold_in(key, 5)
    pair_key, shift_key, parity_key, token_key = jax.random.split(base_key, 4)
    block_count = TOKENS // TOK_EP
    halfway = EXPERTS // 2
    pair_block = TOK_EP * TOP
    order = jax.random.permutation(pair_key, EXPERTS)
    shifts = jax.random.randint(shift_key, (block_count, halfway), 0, MC + 1)
    forced = jnp.arange(halfway)[None, :] == (jnp.arange(block_count) % halfway)[:, None]
    shifts = jnp.where(forced, MC, shifts)
    delta = jnp.zeros((block_count, EXPERTS), jnp.int32)
    delta = delta.at[:, order[:halfway]].set(shifts).at[:, order[halfway:]].set(-shifts)
    counts = MC + delta
    ends = jnp.cumsum(counts, axis=1)
    starts = ends - counts
    position = jnp.arange(pair_block, dtype=jnp.int32)
    expert_at = jnp.sum((ends[:, None, :] <= position[None, :, None]).astype(jnp.int32), axis=2)
    start_at = jnp.take_along_axis(starts, expert_at, axis=1)
    parity = jax.random.randint(parity_key, (block_count, EXPERTS), 0, 2)
    copy_at = (position[None, :] - start_at + jnp.take_along_axis(parity, expert_at, axis=1)) % 2
    ids_grid = expert_at.reshape(block_count, TOP, TOK_EP).transpose(0, 2, 1)
    copy_grid = copy_at.reshape(block_count, TOP, TOK_EP).transpose(0, 2, 1)
    shuffles = jax.vmap(lambda block_key: jax.random.permutation(block_key, TOK_EP))(jax.random.split(token_key, block_count))
    index = jnp.broadcast_to(shuffles[:, :, None], ids_grid.shape)
    ids_grid = jnp.take_along_axis(ids_grid, index, axis=1)
    copy_grid = jnp.take_along_axis(copy_grid, index, axis=1)
    return (ids_grid.reshape(TOKENS, TOP).astype(jnp.int32), copy_grid.reshape(TOKENS, TOP).astype(jnp.int32))


def draw_expert_ids(key, part):
    return make_routing(key)[0]


def draw_copy_choice(key, part):
    return make_routing(key)[1]


def draw_saved_inputs(key, part):
    first_key, column_key, row_key = jax.random.split(jax.random.fold_in(key, 11), 3)
    shape = (EXPERTS, COPIES, EXPERTS, MC, D)
    column_scale = jnp.exp(jax.random.uniform(column_key, (D,), minval=math.log(0.3), maxval=math.log(3.0)))
    row_scale = jnp.exp(jax.random.uniform(row_key, (EXPERTS, COPIES, EXPERTS, MC, 1), minval=math.log(0.5), maxval=math.log(2.0)))
    values = jax.random.truncated_normal(first_key, -4.0, 4.0, shape)
    return (values * column_scale * row_scale).astype(jnp.bfloat16)


def draw_saved_up(key, part):
    first_key, column_key = jax.random.split(jax.random.fold_in(key, 13), 2)
    shape = (EXPERTS, COPIES, EXPERTS, MC, F)
    column_scale = jnp.exp(jax.random.uniform(column_key, (F,), minval=math.log(0.3), maxval=math.log(3.0)))
    values = jax.random.truncated_normal(first_key, -4.0, 4.0, shape)
    return (values * column_scale).astype(jnp.bfloat16)


def steps_of(rng, extent, pieces, least, high):
    level = 1.0
    for dim, blocks in pieces:
        heights = jax.random.uniform(jax.random.fold_in(jax.random.fold_in(rng, 6), dim), (blocks,), jnp.float32, least / len(pieces), high / len(pieces))
        level = level * jnp.repeat(jnp.exp(heights), extent[dim] // blocks).reshape((-1,) + (1,) * (len(extent) - 1 - dim))
    return level


def bell_draw(stream_key, extent, deviation, reach, pieces=(), kind=jnp.bfloat16):
    array = deviation * jax.random.normal(stream_key, extent, jnp.float32)
    if pieces:
        array = array * steps_of(stream_key, extent, pieces, -0.22, 0.18)
    return jnp.clip(array, -reach, reach).astype(kind)


def setup_inputs(seed: int = 0) -> dict:
    key_of = jax.random.split(jax.random.key(seed), 12)
    dy = bell_draw(key_of[0], (TOKENS, D), 1.0, 6.0, ((0, 16),))
    probs = jnp.clip(jnp.exp(math.log(0.5) - 3.218876 * jax.random.uniform(key_of[1], (TOKENS, TOP), jnp.float32) ** steps_of(key_of[1], (TOKENS, TOP), ((0, 16),), -0.2, 0.2)), 0.02, 0.5)
    expert_ids = draw_expert_ids(jax.random.fold_in(key_of[11], 71), 0)
    copy_choice = draw_copy_choice(jax.random.fold_in(key_of[11], 71), 0)
    saved_inputs = draw_saved_inputs(jax.random.fold_in(key_of[11], 71), 0)
    saved_gate = bell_draw(key_of[5], (EXPERTS, COPIES, N_EP, MC, F), 1.0, 4.0, ((0, 16), (1, 2)))
    saved_up = draw_saved_up(jax.random.fold_in(key_of[11], 71), 0)
    down_weight = bell_draw(key_of[7], (EXPERTS, F, D), 1.0, 4.0, ((0, 16), (2, 2)))
    gate_weight = bell_draw(key_of[8], (EXPERTS, D, F), 1.0, 4.0, ((0, 16), (1, 2)))
    up_weight = bell_draw(key_of[9], (EXPERTS, D, F), 1.0, 4.0, ((0, 16), (1, 2)))
    new_owner = jax.random.permutation(key_of[10], EXPERTS).astype(jnp.int32)
    return dict(dy=dy, probs=probs, expert_ids=expert_ids, copy_choice=copy_choice, saved_inputs=saved_inputs, saved_gate=saved_gate, saved_up=saved_up, down_weight=down_weight, gate_weight=gate_weight, up_weight=up_weight, new_owner=new_owner)


quintic_first = 3.4445
quintic_second = -4.775
quintic_third = 2.0315
step_scale = 2.0
epsilon = 1e-07

def contract_rows(left, right):
    return lax.dot_general(left, right, (((0,), (0,)), ((), ())), preferred_element_type=jnp.float32)

def orthogonalize(gradient):
    total = jnp.sqrt(jnp.sum(gradient * gradient))
    iterate = lax.optimization_barrier((gradient / (total + epsilon)).astype(jnp.bfloat16))
    for repeat in range(ITERS):
        gram = lax.optimization_barrier(contract_rows(iterate, iterate).astype(jnp.bfloat16))
        square = jnp.dot(gram, gram, preferred_element_type=jnp.float32)
        poly = (quintic_second * gram.astype(jnp.float32) + quintic_third * square).astype(jnp.bfloat16)
        mixed = quintic_first * iterate.astype(jnp.float32) + jnp.dot(iterate, poly, preferred_element_type=jnp.float32)
        iterate = lax.optimization_barrier(mixed.astype(jnp.bfloat16))
    return iterate

def slot_numbers(expert_ids, copy_choice):
    pair_block = TOK_EP * TOP
    block_count = expert_ids.shape[0] // TOK_EP
    keyed = (expert_ids * COPIES + copy_choice).reshape(block_count, pair_block)
    matches = (keyed[:, :, None] == jnp.arange(EXPERTS * COPIES, dtype=jnp.int32)[None, None, :]).astype(jnp.int32)
    return (lax.optimization_barrier(jnp.sum(jnp.cumsum(matches, axis=1) * matches, axis=2)) - 1).reshape(-1).astype(jnp.int32)

def expert_update(operands):
    routed_rows, inputs, pre_gate, pre_up, down_matrix, gate_matrix, up_matrix = operands
    hidden_grad = lax.dot_general(routed_rows, down_matrix, (((1,), (1,)), ((), ())), preferred_element_type=jnp.float32) / math.sqrt(F)
    gate_value = pre_gate.astype(jnp.float32)
    up_value = pre_up.astype(jnp.float32)
    sigmoid = jax.nn.sigmoid(gate_value)
    gate_rows = (hidden_grad * up_value * sigmoid * (1.0 + gate_value * (1.0 - sigmoid))).astype(jnp.bfloat16)
    up_rows = (hidden_grad * gate_value * sigmoid).astype(jnp.bfloat16)
    grad_gate = contract_rows(inputs, gate_rows)
    grad_up = contract_rows(inputs, up_rows)
    factor = step_scale * math.sqrt(D)
    new_gate = (gate_matrix.astype(jnp.float32) - factor * orthogonalize(grad_gate).astype(jnp.float32)).astype(jnp.bfloat16)
    new_up = (up_matrix.astype(jnp.float32) - factor * orthogonalize(grad_up).astype(jnp.float32)).astype(jnp.bfloat16)
    return (new_gate, new_up)

def reference(dy, probs, expert_ids, copy_choice, saved_inputs, saved_gate, saved_up, down_weight, gate_weight, up_weight, new_owner):
    pair_total = TOKENS * TOP
    slots = slot_numbers(expert_ids, copy_choice)
    flat_ids = expert_ids.reshape(-1).astype(jnp.int32)
    flat_copy = copy_choice.reshape(-1).astype(jnp.int32)
    source = jnp.arange(pair_total, dtype=jnp.int32) // (TOK_EP * TOP)
    target = ((flat_ids * COPIES + flat_copy) * N_EP + source) * MC + slots
    scaled = (probs[:, :, None] * dy.astype(jnp.float32)[:, None, :]).astype(jnp.bfloat16).reshape(pair_total, D)
    routed = jnp.zeros((EXPERTS * COPIES * N_EP * MC, D), jnp.bfloat16).at[target].set(scaled)
    routed = routed.reshape(EXPERTS, COPIES * N_EP * MC, D)
    gate_moved, up_moved = lax.map(expert_update, (routed, saved_inputs.reshape(EXPERTS, -1, D), saved_gate.reshape(EXPERTS, -1, F), saved_up.reshape(EXPERTS, -1, F), down_weight, gate_weight, up_weight))
    new_gate = jnp.zeros_like(gate_weight).at[new_owner].set(gate_moved)
    new_up = jnp.zeros_like(up_weight).at[new_owner].set(up_moved)
    return (new_gate, new_up)
```

```python
import functools
import math

import jax
import jax.numpy as jnp
from jax import lax
from jax.experimental import pallas as pl
from jax.experimental.pallas import tpu as pltpu
from jax.sharding import PartitionSpec as P

ITERS = 2

quintic_first = 3.4445
quintic_second = -4.775
quintic_third = 2.0315
step_scale = 2.0
epsilon = 1e-07

VMEM = pl.BlockSpec(memory_space=pltpu.VMEM)
SMEM = pl.BlockSpec(memory_space=pltpu.SMEM)
ANY = pl.BlockSpec(memory_space=pl.ANY)
MIB = 1 << 20


def from_partner(block):
    return lax.ppermute(block, "rep", [(0, 1), (1, 0)])


def mm(left, right, dims=((1,), (0,))):
    return lax.dot_general(left, right, (dims, ((), ())), preferred_element_type=jnp.float32)


def call(kernel, outs, in_specs, args, flops, nbytes, scratch=(), limit=40):
    return pl.pallas_call(
        kernel,
        out_shape=outs,
        in_specs=in_specs,
        out_specs=jax.tree.map(lambda _: VMEM, outs),
        scratch_shapes=list(scratch),
        compiler_params=pltpu.CompilerParams(vmem_limit_bytes=limit * MIB),
        cost_estimate=pl.CostEstimate(flops=flops, bytes_accessed=nbytes, transcendentals=0),
    )(*args)


def dispatch_kernel(capacity, rep_ref, ids_ref, copy_ref, probs_ref, dy_ref, out_ref):
    rows, tokens = out_ref.shape[0], dy_ref.shape[0]
    own = rep_ref[0]
    expert = lax.broadcasted_iota(jnp.int32, (rows, tokens), 0) // capacity
    slot = lax.broadcasted_iota(jnp.int32, (rows, tokens), 0) % capacity
    mask = jnp.zeros((rows, tokens), jnp.float32)
    weight = jnp.zeros((rows, tokens), jnp.float32)
    for k in range(ids_ref.shape[0]):
        here = (ids_ref[k : k + 1, :] == expert) & (copy_ref[k : k + 1, :] == own)
        mask = jnp.where(here, 1.0, mask)
        weight = jnp.where(here, probs_ref[k : k + 1, :], weight)
    before = lax.broadcasted_iota(jnp.int32, (tokens, tokens), 0) < lax.broadcasted_iota(
        jnp.int32, (tokens, tokens), 1
    )
    rank = mm(mask.astype(jnp.bfloat16), jnp.where(before, 1.0, 0.0).astype(jnp.bfloat16))
    hot = (mask > 0.5) & (rank.astype(jnp.int32) == slot)
    scale = jnp.sum(jnp.where(hot, weight, 0.0), axis=1, keepdims=True)
    picked = mm(jnp.where(hot, 1.0, 0.0).astype(jnp.bfloat16), dy_ref[...])
    out_ref[...] = (picked * scale).astype(jnp.bfloat16)


def inputs_kernel(rep_ref, own_ref, other_ref, high_ref, low_ref, xt_ref):
    half = xt_ref.shape[0]
    rows = own_ref.shape[0]
    own, other = own_ref[...], other_ref[...]

    def store(first, second, block):
        high = block.astype(jnp.bfloat16)
        high_ref[first, second] = high
        low_ref[first, second] = (block - high.astype(jnp.float32)).astype(jnp.bfloat16)

    begin, end = slice(0, rows), slice(rows, None)
    store(begin, begin, mm(own, own, ((1,), (1,))))
    store(end, end, mm(other, other, ((1,), (1,))))
    cross = mm(own, other, ((1,), (1,)))
    store(begin, end, cross)
    store(end, begin, cross.T)
    start = pl.multiple_of(rep_ref[0] * half, half)
    xt_ref[:, :rows] = own_ref[:, pl.ds(start, half)].T
    xt_ref[:, rows:] = other_ref[:, pl.ds(start, half)].T


def rows_kernel(
    rep_ref, routed_ref, own_down_ref, other_down_ref, gate_ref, up_ref, own_ref, partner_ref
):
    half = own_down_ref.shape[1]
    inner = own_down_ref.shape[0]
    rep = rep_ref[0]
    first = pl.multiple_of(rep * half, half)
    second = pl.multiple_of((1 - rep) * half, half)
    hidden = mm(routed_ref[:, pl.ds(first, half)], own_down_ref[...], ((1,), (1,)))
    hidden += mm(routed_ref[:, pl.ds(second, half)], other_down_ref[...], ((1,), (1,)))
    hidden = hidden / math.sqrt(inner)
    gate = gate_ref[...].astype(jnp.float32)
    up = up_ref[...].astype(jnp.float32)
    sigmoid = 1.0 / (1.0 + jnp.exp(-gate))
    gate_rows = (hidden * up * sigmoid * (1.0 + gate * (1.0 - sigmoid))).astype(jnp.bfloat16)
    up_rows = (hidden * gate * sigmoid).astype(jnp.bfloat16)

    @pl.when(rep == 0)
    def _():
        own_ref[...] = gate_rows
        partner_ref[...] = up_rows

    @pl.when(rep == 1)
    def _():
        own_ref[...] = up_rows
        partner_ref[...] = gate_rows


def schulz_kernel(own_ref, other_ref, high_ref, low_ref, b_ref, r_ref, gram_ref, poly_ref):
    rows = own_ref.shape[0]
    r_ref[:rows] = own_ref[...]
    r_ref[rows:] = other_ref[...]
    size = None
    for repeat in range(ITERS):
        base = r_ref[...]
        mapped = mm(high_ref[...], base) + mm(low_ref[...], base)
        if repeat == 0:
            squares = jnp.sum(base.astype(jnp.float32) * mapped)
            total = jnp.sqrt(jnp.maximum(squares, 0.0)) + epsilon
            size = 1.0 / total
        gram = mm(base, mapped.astype(jnp.bfloat16), ((0,), (0,)))
        if repeat == 0:
            gram = gram * (size * size)
        gram_ref[...] = gram.astype(jnp.bfloat16)
        square = mm(gram_ref[...], gram_ref[...])
        poly_ref[...] = (
            quintic_second * gram_ref[...].astype(jnp.float32) + quintic_third * square
        ).astype(jnp.bfloat16)
        mixed = quintic_first * base.astype(jnp.float32) + mm(base, poly_ref[...])
        if repeat == 0:
            mixed = mixed * size
        if repeat == ITERS - 1:
            b_ref[...] = mixed.astype(jnp.bfloat16)
        else:
            r_ref[...] = mixed.astype(jnp.bfloat16)


def update_kernel(factor, rep_ref, own_ref, other_ref, xt_ref, gate_ref, up_ref, gate_out, up_out):
    rows = own_ref.shape[0] // 2
    rep = rep_ref[0]

    def update(weight_ref, out_ref, swapped):
        b_ref = other_ref if swapped else own_ref
        first, second = (slice(rows, None), slice(0, rows)) if swapped else (slice(0, rows), slice(rows, None))
        ortho = mm(xt_ref[:, :rows], b_ref[first]) + mm(xt_ref[:, rows:], b_ref[second])
        out_ref[...] = (weight_ref[...].astype(jnp.float32) - factor * ortho).astype(jnp.bfloat16)

    @pl.when(rep == 0)
    def _():
        update(gate_ref, gate_out, False)
        update(up_ref, up_out, True)

    @pl.when(rep == 1)
    def _():
        update(gate_ref, gate_out, True)
        update(up_ref, up_out, False)


def arrange_kernel(index_ref, in_ref, out_ref, sems):
    count = in_ref.shape[0]
    copies = [
        pltpu.make_async_copy(in_ref.at[index_ref[i]], out_ref.at[i], sems.at[i])
        for i in range(count)
    ]
    for copy in copies:
        copy.start()
    for copy in copies:
        copy.wait()


def arrange(blocks, index):
    return pl.pallas_call(
        arrange_kernel,
        out_shape=jax.ShapeDtypeStruct(blocks.shape, blocks.dtype),
        in_specs=[SMEM, ANY],
        out_specs=ANY,
        scratch_shapes=[pltpu.SemaphoreType.DMA((blocks.shape[0],))],
        cost_estimate=pl.CostEstimate(
            flops=0, bytes_accessed=4 * blocks.size, transcendentals=0
        ),
    )(index, blocks)


def exchange(blocks):
    return lax.all_to_all(blocks, "ep", split_axis=0, concat_axis=0, tiled=True)


def shards(
    dy,
    probs,
    expert_ids,
    copy_choice,
    saved_inputs,
    saved_gate,
    saved_up,
    down_weight,
    gate_weight,
    up_weight,
    new_owner,
):
    experts = lax.axis_size("ep")
    capacity = saved_inputs.shape[3]
    width = dy.shape[1]
    inner = saved_gate.shape[4]
    half = width // 2
    rows = experts * capacity
    bf16 = jnp.bfloat16
    shape = lambda *dims: jax.ShapeDtypeStruct(dims, bf16)
    rep = lax.axis_index("rep").astype(jnp.int32).reshape(1)

    outgoing = call(
        functools.partial(dispatch_kernel, capacity),
        shape(rows, width),
        [SMEM, VMEM, VMEM, VMEM, VMEM],
        (rep, expert_ids.T, copy_choice.T, probs.T, dy),
        2 * rows * dy.shape[0] * width,
        2 * rows * width,
    )
    routed = exchange(outgoing.reshape(experts, capacity, width)).reshape(rows, width)

    inputs = saved_inputs.reshape(rows, width)
    down = down_weight[0]
    other_inputs = from_partner(inputs)
    other_down = from_partner(down)
    high, low, transposed = call(
        inputs_kernel,
        (shape(2 * rows, 2 * rows), shape(2 * rows, 2 * rows), shape(half, 2 * rows)),
        [SMEM, VMEM, VMEM],
        (rep, inputs, other_inputs),
        2 * 3 * rows * rows * width,
        8 * rows * width,
    )
    own_rows, partner_rows = call(
        rows_kernel,
        (shape(rows, inner), shape(rows, inner)),
        [SMEM] + [VMEM] * 5,
        (rep, routed, down, other_down, saved_gate.reshape(rows, inner), saved_up.reshape(rows, inner)),
        2 * rows * width * inner,
        2 * inner * width,
    )
    other_rows = from_partner(partner_rows)
    own_b = call(
        schulz_kernel,
        shape(2 * rows, inner),
        [VMEM] * 4,
        (own_rows, other_rows, high, low),
        ITERS * 2 * inner * inner * (inner + 6 * rows),
        8 * rows * inner,
        scratch=(
            pltpu.VMEM((2 * rows, inner), bf16),
            pltpu.VMEM((inner, inner), bf16),
            pltpu.VMEM((inner, inner), bf16),
        ),
    )
    other_b = from_partner(own_b)
    gate, up = call(
        functools.partial(update_kernel, step_scale * math.sqrt(width)),
        (shape(half, inner), shape(half, inner)),
        [SMEM] + [VMEM] * 5,
        (rep, own_b, other_b, transposed, gate_weight[0], up_weight[0]),
        2 * 2 * half * 2 * rows * inner,
        8 * half * inner,
    )
    place = jnp.arange(experts, dtype=jnp.int32)
    source = jnp.sum(
        jnp.where(new_owner[None, :] == place[:, None], place[None, :], 0), axis=1, dtype=jnp.int32
    )
    pieces = (experts, half // experts, inner)
    results = []
    for matrix in (gate, up):
        spread = exchange(matrix.reshape(pieces))
        results.append(spread)
    results = [exchange(arrange(spread, source)).reshape(1, half, inner) for spread in results]
    return tuple(results)


def solution(mesh):
    in_specs = (
        P("ep", None),
        P("ep", None),
        P("ep", None),
        P("ep", None),
        P("ep", "rep", None, None, None),
        P("ep", "rep", None, None, None),
        P("ep", "rep", None, None, None),
        P("ep", None, "rep"),
        P("ep", "rep", None),
        P("ep", "rep", None),
        P(),
    )
    out_specs = (P("ep", "rep", None), P("ep", "rep", None))
    return jax.shard_map(shards, mesh=mesh, in_specs=in_specs, out_specs=out_specs, check_vma=False)
```

```python
import functools
import math

import jax
import jax.numpy as jnp
from jax import lax
from jax.experimental import pallas as pl
from jax.experimental.pallas import tpu as pltpu
from jax.sharding import PartitionSpec as P

ITERS = 2

quintic_first = 3.4445
quintic_second = -4.775
quintic_third = 2.0315
step_scale = 2.0
epsilon = 1e-07

VMEM = pl.BlockSpec(memory_space=pltpu.VMEM)
SMEM = pl.BlockSpec(memory_space=pltpu.SMEM)
MIB = 1 << 20


def from_partner(block):
    return lax.ppermute(block, "rep", [(0, 1), (1, 0)])


def mm(left, right, dims=((1,), (0,))):
    return lax.dot_general(left, right, (dims, ((), ())), preferred_element_type=jnp.float32)


def call(kernel, outs, in_specs, args, flops, nbytes, scratch=(), limit=40):
    return pl.pallas_call(
        kernel,
        out_shape=outs,
        in_specs=in_specs,
        out_specs=jax.tree.map(lambda _: VMEM, outs),
        scratch_shapes=list(scratch),
        compiler_params=pltpu.CompilerParams(vmem_limit_bytes=limit * MIB),
        cost_estimate=pl.CostEstimate(flops=flops, bytes_accessed=nbytes, transcendentals=0),
    )(*args)


def dispatch_kernel(capacity, rep_ref, ids_ref, copy_ref, probs_ref, dy_ref, out_ref):
    rows, tokens = out_ref.shape[0], dy_ref.shape[0]
    own = rep_ref[0]
    expert = lax.broadcasted_iota(jnp.int32, (rows, tokens), 0) // capacity
    slot = lax.broadcasted_iota(jnp.int32, (rows, tokens), 0) % capacity
    mask = jnp.zeros((rows, tokens), jnp.float32)
    weight = jnp.zeros((rows, tokens), jnp.float32)
    for k in range(ids_ref.shape[0]):
        here = (ids_ref[k : k + 1, :] == expert) & (copy_ref[k : k + 1, :] == own)
        mask = jnp.where(here, 1.0, mask)
        weight = jnp.where(here, probs_ref[k : k + 1, :], weight)
    before = lax.broadcasted_iota(jnp.int32, (tokens, tokens), 0) < lax.broadcasted_iota(
        jnp.int32, (tokens, tokens), 1
    )
    rank = mm(mask.astype(jnp.bfloat16), jnp.where(before, 1.0, 0.0).astype(jnp.bfloat16))
    hot = (mask > 0.5) & (rank.astype(jnp.int32) == slot)
    scale = jnp.sum(jnp.where(hot, weight, 0.0), axis=1, keepdims=True)
    picked = mm(jnp.where(hot, 1.0, 0.0).astype(jnp.bfloat16), dy_ref[...])
    out_ref[...] = (picked * scale).astype(jnp.bfloat16)


def inputs_kernel(rep_ref, own_ref, other_ref, high_ref, low_ref, xt_ref):
    half = xt_ref.shape[0]
    rows = own_ref.shape[0]
    own, other = own_ref[...], other_ref[...]

    def store(first, second, block):
        high = block.astype(jnp.bfloat16)
        high_ref[first, second] = high
        low_ref[first, second] = (block - high.astype(jnp.float32)).astype(jnp.bfloat16)

    begin, end = slice(0, rows), slice(rows, None)
    store(begin, begin, mm(own, own, ((1,), (1,))))
    store(end, end, mm(other, other, ((1,), (1,))))
    cross = mm(own, other, ((1,), (1,)))
    store(begin, end, cross)
    store(end, begin, cross.T)
    start = pl.multiple_of(rep_ref[0] * half, half)
    xt_ref[:, :rows] = own_ref[:, pl.ds(start, half)].T
    xt_ref[:, rows:] = other_ref[:, pl.ds(start, half)].T


def rows_kernel(
    rep_ref, routed_ref, own_down_ref, other_down_ref, gate_ref, up_ref, own_ref, partner_ref
):
    half = own_down_ref.shape[1]
    inner = own_down_ref.shape[0]
    rep = rep_ref[0]
    first = pl.multiple_of(rep * half, half)
    second = pl.multiple_of((1 - rep) * half, half)
    hidden = mm(routed_ref[:, pl.ds(first, half)], own_down_ref[...], ((1,), (1,)))
    hidden += mm(routed_ref[:, pl.ds(second, half)], other_down_ref[...], ((1,), (1,)))
    hidden = hidden / math.sqrt(inner)
    gate = gate_ref[...].astype(jnp.float32)
    up = up_ref[...].astype(jnp.float32)
    sigmoid = 1.0 / (1.0 + jnp.exp(-gate))
    gate_rows = (hidden * up * sigmoid * (1.0 + gate * (1.0 - sigmoid))).astype(jnp.bfloat16)
    up_rows = (hidden * gate * sigmoid).astype(jnp.bfloat16)

    @pl.when(rep == 0)
    def _():
        own_ref[...] = gate_rows
        partner_ref[...] = up_rows

    @pl.when(rep == 1)
    def _():
        own_ref[...] = up_rows
        partner_ref[...] = gate_rows


def schulz_kernel(own_ref, other_ref, high_ref, low_ref, b_ref, r_ref, gram_ref, poly_ref):
    rows = own_ref.shape[0]
    r_ref[:rows] = own_ref[...]
    r_ref[rows:] = other_ref[...]
    size = None
    for repeat in range(ITERS):
        base = r_ref[...]
        mapped = mm(high_ref[...], base) + mm(low_ref[...], base)
        if repeat == 0:
            squares = jnp.sum(base.astype(jnp.float32) * mapped)
            total = jnp.sqrt(jnp.maximum(squares, 0.0)) + epsilon
            size = 1.0 / total
        gram = mm(base, mapped.astype(jnp.bfloat16), ((0,), (0,)))
        if repeat == 0:
            gram = gram * (size * size)
        gram_ref[...] = gram.astype(jnp.bfloat16)
        square = mm(gram_ref[...], gram_ref[...])
        poly_ref[...] = (
            quintic_second * gram_ref[...].astype(jnp.float32) + quintic_third * square
        ).astype(jnp.bfloat16)
        mixed = quintic_first * base.astype(jnp.float32) + mm(base, poly_ref[...])
        if repeat == 0:
            mixed = mixed * size
        if repeat == ITERS - 1:
            b_ref[...] = mixed.astype(jnp.bfloat16)
        else:
            r_ref[...] = mixed.astype(jnp.bfloat16)


def update_kernel(factor, rep_ref, own_ref, other_ref, xt_ref, gate_ref, up_ref, gate_out, up_out):
    rows = own_ref.shape[0] // 2
    rep = rep_ref[0]

    def update(weight_ref, out_ref, swapped):
        b_ref = other_ref if swapped else own_ref
        first, second = (slice(rows, None), slice(0, rows)) if swapped else (slice(0, rows), slice(rows, None))
        ortho = mm(xt_ref[:, :rows], b_ref[first]) + mm(xt_ref[:, rows:], b_ref[second])
        out_ref[...] = (weight_ref[...].astype(jnp.float32) - factor * ortho).astype(jnp.bfloat16)

    @pl.when(rep == 0)
    def _():
        update(gate_ref, gate_out, False)
        update(up_ref, up_out, True)

    @pl.when(rep == 1)
    def _():
        update(gate_ref, gate_out, True)
        update(up_ref, up_out, False)


def arrange_kernel(index_ref, in_ref, out_ref):
    for i in range(in_ref.shape[0]):
        out_ref[i] = in_ref[index_ref[i]]


def arrange(blocks, index):
    return call(
        arrange_kernel,
        jax.ShapeDtypeStruct(blocks.shape, blocks.dtype),
        [SMEM, VMEM],
        (index, blocks),
        0,
        4 * blocks.size,
        limit=16,
    )


def exchange(blocks):
    return lax.all_to_all(blocks, "ep", split_axis=0, concat_axis=0, tiled=True)


def shards(
    dy,
    probs,
    expert_ids,
    copy_choice,
    saved_inputs,
    saved_gate,
    saved_up,
    down_weight,
    gate_weight,
    up_weight,
    new_owner,
):
    experts = lax.axis_size("ep")
    capacity = saved_inputs.shape[3]
    width = dy.shape[1]
    inner = saved_gate.shape[4]
    half = width // 2
    rows = experts * capacity
    bf16 = jnp.bfloat16
    shape = lambda *dims: jax.ShapeDtypeStruct(dims, bf16)
    rep = lax.axis_index("rep").astype(jnp.int32).reshape(1)

    outgoing = pl.pallas_call(
        functools.partial(dispatch_kernel, capacity),
        out_shape=shape(rows, width),
        grid=(1,),
        in_specs=[SMEM]
        + [pl.BlockSpec(a.shape, lambda i: (0, 0)) for a in (expert_ids.T, copy_choice.T, probs.T, dy)],
        out_specs=pl.BlockSpec((rows, width), lambda i: (0, 0)),
        compiler_params=pltpu.CompilerParams(vmem_limit_bytes=16 * MIB),
    )(rep, expert_ids.T, copy_choice.T, probs.T, dy)
    routed = exchange(outgoing.reshape(experts, capacity, width)).reshape(rows, width)

    inputs = saved_inputs.reshape(rows, width)
    down = down_weight[0]
    other_inputs = from_partner(inputs)
    other_down = from_partner(down)
    high, low, transposed = call(
        inputs_kernel,
        (shape(2 * rows, 2 * rows), shape(2 * rows, 2 * rows), shape(half, 2 * rows)),
        [SMEM, VMEM, VMEM],
        (rep, inputs, other_inputs),
        2 * 3 * rows * rows * width,
        8 * rows * width,
    )
    own_rows, partner_rows = call(
        rows_kernel,
        (shape(rows, inner), shape(rows, inner)),
        [SMEM] + [VMEM] * 5,
        (rep, routed, down, other_down, saved_gate.reshape(rows, inner), saved_up.reshape(rows, inner)),
        2 * rows * width * inner,
        2 * inner * width,
    )
    other_rows = from_partner(partner_rows)
    own_b = call(
        schulz_kernel,
        shape(2 * rows, inner),
        [VMEM] * 4,
        (own_rows, other_rows, high, low),
        ITERS * 2 * inner * inner * (inner + 6 * rows),
        8 * rows * inner,
        scratch=(
            pltpu.VMEM((2 * rows, inner), bf16),
            pltpu.VMEM((inner, inner), bf16),
            pltpu.VMEM((inner, inner), bf16),
        ),
    )
    other_b = from_partner(own_b)
    gate, up = call(
        functools.partial(update_kernel, step_scale * math.sqrt(width)),
        (shape(half, inner), shape(half, inner)),
        [SMEM] + [VMEM] * 5,
        (rep, own_b, other_b, transposed, gate_weight[0], up_weight[0]),
        2 * 2 * half * 2 * rows * inner,
        8 * half * inner,
    )
    place = jnp.arange(experts, dtype=jnp.int32)
    source = jnp.sum(
        jnp.where(new_owner[None, :] == place[:, None], place[None, :], 0), axis=1, dtype=jnp.int32
    )
    pieces = (experts, half // experts, inner)
    results = []
    for matrix in (gate, up):
        spread = exchange(matrix.reshape(pieces))
        results.append(spread)
    results = [exchange(arrange(spread, source)).reshape(1, half, inner) for spread in results]
    return tuple(results)


def solution(mesh):
    in_specs = (
        P("ep", None),
        P("ep", None),
        P("ep", None),
        P("ep", None),
        P("ep", "rep", None, None, None),
        P("ep", "rep", None, None, None),
        P("ep", "rep", None, None, None),
        P("ep", None, "rep"),
        P("ep", "rep", None),
        P("ep", "rep", None),
        P(),
    )
    out_specs = (P("ep", "rep", None), P("ep", "rep", None))
    return jax.shard_map(shards, mesh=mesh, in_specs=in_specs, out_specs=out_specs, check_vma=False)
```

```python
import functools
import math

import jax
import jax.numpy as jnp
from jax import lax
from jax.experimental import pallas as pl
from jax.experimental.pallas import tpu as pltpu
from jax.sharding import PartitionSpec as P

ITERS = 2

quintic_first = 3.4445
quintic_second = -4.775
quintic_third = 2.0315
step_scale = 2.0
epsilon = 1e-07

VMEM = pl.BlockSpec(memory_space=pltpu.VMEM)
SMEM = pl.BlockSpec(memory_space=pltpu.SMEM)
MIB = 1 << 20


def from_partner(block):
    return lax.ppermute(block, "rep", [(0, 1), (1, 0)])


def mm(left, right, dims=((1,), (0,))):
    return lax.dot_general(left, right, (dims, ((), ())), preferred_element_type=jnp.float32)


def call(kernel, outs, in_specs, args, flops, nbytes, scratch=(), limit=40):
    return pl.pallas_call(
        kernel,
        out_shape=outs,
        in_specs=in_specs,
        out_specs=jax.tree.map(lambda _: VMEM, outs),
        scratch_shapes=list(scratch),
        compiler_params=pltpu.CompilerParams(vmem_limit_bytes=limit * MIB),
        cost_estimate=pl.CostEstimate(flops=flops, bytes_accessed=nbytes, transcendentals=0),
    )(*args)


def dispatch_kernel(capacity, rep_ref, ids_ref, copy_ref, probs_ref, dy_ref, out_ref):
    rows, tokens = out_ref.shape[0], dy_ref.shape[0]
    own = rep_ref[0]
    expert = lax.broadcasted_iota(jnp.int32, (rows, tokens), 0) // capacity
    slot = lax.broadcasted_iota(jnp.int32, (rows, tokens), 0) % capacity
    mask = jnp.zeros((rows, tokens), jnp.float32)
    weight = jnp.zeros((rows, tokens), jnp.float32)
    for k in range(ids_ref.shape[0]):
        here = (ids_ref[k : k + 1, :] == expert) & (copy_ref[k : k + 1, :] == own)
        mask = jnp.where(here, 1.0, mask)
        weight = jnp.where(here, probs_ref[k : k + 1, :], weight)
    before = lax.broadcasted_iota(jnp.int32, (tokens, tokens), 0) < lax.broadcasted_iota(
        jnp.int32, (tokens, tokens), 1
    )
    rank = mm(mask.astype(jnp.bfloat16), jnp.where(before, 1.0, 0.0).astype(jnp.bfloat16))
    hot = (mask > 0.5) & (rank.astype(jnp.int32) == slot)
    scale = jnp.sum(jnp.where(hot, weight, 0.0), axis=1, keepdims=True)
    picked = mm(jnp.where(hot, 1.0, 0.0).astype(jnp.bfloat16), dy_ref[...])
    out_ref[...] = (picked * scale).astype(jnp.bfloat16)


def inputs_kernel(rep_ref, own_ref, other_ref, high_ref, low_ref, xt_ref):
    half = xt_ref.shape[0]
    rows = own_ref.shape[0]
    own, other = own_ref[...], other_ref[...]

    def store(first, second, block):
        high = block.astype(jnp.bfloat16)
        high_ref[first, second] = high
        low_ref[first, second] = (block - high.astype(jnp.float32)).astype(jnp.bfloat16)

    begin, end = slice(0, rows), slice(rows, None)
    store(begin, begin, mm(own, own, ((1,), (1,))))
    store(end, end, mm(other, other, ((1,), (1,))))
    cross = mm(own, other, ((1,), (1,)))
    store(begin, end, cross)
    store(end, begin, cross.T)
    start = pl.multiple_of(rep_ref[0] * half, half)
    xt_ref[:, :rows] = own_ref[:, pl.ds(start, half)].T
    xt_ref[:, rows:] = other_ref[:, pl.ds(start, half)].T


def rows_kernel(
    rep_ref, routed_ref, own_down_ref, other_down_ref, gate_ref, up_ref, own_ref, partner_ref
):
    half = own_down_ref.shape[1]
    inner = own_down_ref.shape[0]
    rep = rep_ref[0]
    first = pl.multiple_of(rep * half, half)
    second = pl.multiple_of((1 - rep) * half, half)
    hidden = mm(routed_ref[:, pl.ds(first, half)], own_down_ref[...], ((1,), (1,)))
    hidden += mm(routed_ref[:, pl.ds(second, half)], other_down_ref[...], ((1,), (1,)))
    hidden = hidden / math.sqrt(inner)
    gate = gate_ref[...].astype(jnp.float32)
    up = up_ref[...].astype(jnp.float32)
    sigmoid = 1.0 / (1.0 + jnp.exp(-gate))
    gate_rows = (hidden * up * sigmoid * (1.0 + gate * (1.0 - sigmoid))).astype(jnp.bfloat16)
    up_rows = (hidden * gate * sigmoid).astype(jnp.bfloat16)

    @pl.when(rep == 0)
    def _():
        own_ref[...] = gate_rows
        partner_ref[...] = up_rows

    @pl.when(rep == 1)
    def _():
        own_ref[...] = up_rows
        partner_ref[...] = gate_rows


def schulz_kernel(own_ref, other_ref, high_ref, low_ref, b_ref, r_ref, gram_ref, poly_ref):
    rows = own_ref.shape[0]
    r_ref[:rows] = own_ref[...]
    r_ref[rows:] = other_ref[...]
    size = None
    for repeat in range(ITERS):
        base = r_ref[...]
        mapped = mm(high_ref[...], base) + mm(low_ref[...], base)
        if repeat == 0:
            squares = jnp.sum(base.astype(jnp.float32) * mapped)
            total = jnp.sqrt(jnp.maximum(squares, 0.0)) + epsilon
            size = 1.0 / total
        gram = mm(base, mapped.astype(jnp.bfloat16), ((0,), (0,)))
        if repeat == 0:
            gram = gram * (size * size)
        gram_ref[...] = gram.astype(jnp.bfloat16)
        square = mm(gram_ref[...], gram_ref[...])
        poly_ref[...] = (
            quintic_second * gram_ref[...].astype(jnp.float32) + quintic_third * square
        ).astype(jnp.bfloat16)
        mixed = quintic_first * base.astype(jnp.float32) + mm(base, poly_ref[...])
        if repeat == 0:
            mixed = mixed * size
        if repeat == ITERS - 1:
            b_ref[...] = mixed.astype(jnp.bfloat16)
        else:
            r_ref[...] = mixed.astype(jnp.bfloat16)


def update_kernel(factor, halves, plane, rep_ref, me_ref, own_ref, other_ref, xt_ref, *refs):
    weights, outs = refs[:2], refs[2:]
    rows = own_ref.shape[0] // 2
    size = outs[0].shape[0]
    rep = rep_ref[0]

    def update(matrix, swapped):
        b_ref = other_ref if swapped else own_ref
        begin, end = slice(0, rows), slice(rows, None)
        first, second = (end, begin) if swapped else (begin, end)
        for h in range(halves):
            for d in range(plane):
                start = pl.multiple_of((h * plane + (me_ref[0] ^ d)) * size, size)
                x = xt_ref[pl.ds(start, size), :]
                ortho = mm(x[:, :rows], b_ref[first]) + mm(x[:, rows:], b_ref[second])
                weight = weights[matrix][pl.ds(start, size), :].astype(jnp.float32)
                outs[(matrix * halves + h) * plane + d][...] = (weight - factor * ortho).astype(
                    jnp.bfloat16
                )

    @pl.when(rep == 0)
    def _():
        update(0, False)
        update(1, True)

    @pl.when(rep == 1)
    def _():
        update(0, True)
        update(1, False)


def route_kernel(line, plane, limit, owner_ref, place_ref, pick_ref, last_ref, count_ref, at, slot, right, left):
    items = line * plane
    mine, me = place_ref[0] // plane, place_ref[0] % plane

    def begin(i, carry):
        at[i] = i // plane
        slot[i] = (i % plane) ^ me
        return carry

    lax.fori_loop(0, items, begin, 0)
    count_ref[0] = 0
    for step in range(limit):
        for z in range(line):
            right[z] = -1
            left[z] = -1

        def choose(i, carry):
            place, target = at[i], owner_ref[i] // plane

            @pl.when(target > place)
            def _():
                best = right[place]
                reach = jnp.where(best >= 0, owner_ref[jnp.maximum(best, 0)] // plane, -1)
                right[place] = jnp.where(target > reach, i, best)

            @pl.when(target < place)
            def _():
                best = left[place]
                reach = jnp.where(best >= 0, owner_ref[jnp.maximum(best, 0)] // plane, line)
                left[place] = jnp.where(target < reach, i, best)

            return carry + jnp.where(target != place, 1, 0)

        waiting = lax.fori_loop(0, items, choose, jnp.int32(0))
        count_ref[0] = jnp.where(waiting > 0, step + 1, count_ref[0])
        go, back = right[mine], left[mine]
        pick_ref[step] = jnp.where(go >= 0, slot[jnp.maximum(go, 0)], 0)
        pick_ref[limit + step] = jnp.where(back >= 0, slot[jnp.maximum(back, 0)], 0)
        for z in range(line):
            for chosen, move in ((right, 1), (left, -1)):

                @pl.when(chosen[z] >= 0)
                def _():
                    at[chosen[z]] = z + move
                    slot[chosen[z]] = plane + step

    def finish(i, carry):
        target = owner_ref[i] // plane

        @pl.when(target == mine)
        def _():
            late = (slot[i] >= plane) & (target < i // plane)
            last_ref[(owner_ref[i] % plane) ^ me] = slot[i] + jnp.where(late, limit, 0)

        return carry + jnp.where(target != at[i], 1, 0)

    rest = lax.fori_loop(0, items, finish, jnp.int32(0))
    count_ref[0] = jnp.where(rest > 0, limit + 1, count_ref[0])


def route(line, plane, limit, owner, place):
    table = lambda n: jax.ShapeDtypeStruct((n,), jnp.int32)
    return pl.pallas_call(
        functools.partial(route_kernel, line, plane, limit),
        out_shape=(table(2 * limit), table(plane), table(1)),
        in_specs=[SMEM, SMEM],
        out_specs=(SMEM, SMEM, SMEM),
        scratch_shapes=[pltpu.SMEM((n,), jnp.int32) for n in (line * plane, line * plane, line, line)],
    )(owner, place)


def pick_kernel(entries, groups, table_ref, *refs):
    outs = refs[len(refs) - len(entries) :]
    for entry, group, out in zip(entries, groups, outs):
        for number, index in group:

            @pl.when(table_ref[entry] == number)
            def _():
                out[...] = refs[index][...]


def pick(table, blocks, entries, groups):
    shape = jax.ShapeDtypeStruct(blocks[0].shape, blocks[0].dtype)
    return call(
        functools.partial(pick_kernel, entries, groups),
        (shape,) * len(entries),
        [SMEM] + [VMEM] * len(blocks),
        (table, *blocks),
        0,
        4 * blocks[0].size * len(entries),
        limit=16,
    )


def assemble_kernel(halves, plane, me_ref, *refs):
    out_ref = refs[-1]
    size = refs[0].shape[0]
    for h in range(halves):
        for d in range(plane):
            start = pl.multiple_of((h * plane + (me_ref[0] ^ d)) * size, size)
            out_ref[pl.ds(start, size), :] = refs[h * plane + d][...]


def assemble(halves, plane, me, pieces):
    rows, columns = pieces[0].shape
    return call(
        functools.partial(assemble_kernel, halves, plane),
        jax.ShapeDtypeStruct((halves * plane * rows, columns), pieces[0].dtype),
        [SMEM] + [VMEM] * len(pieces),
        (me, *pieces),
        0,
        4 * halves * plane * rows * columns,
        limit=16,
    )


def direct(steps, limit, line, plane, halves, me, pick_table, last_table, pieces):
    items = line * plane

    def across(block, d):
        return lax.ppermute(block, "ep", [(i, i ^ d) for i in range(items)])

    def along(block, move):
        low, high = (0, items - plane) if move > 0 else (plane, items)
        return lax.ppermute(block, "ep", [(i, i + move * plane) for i in range(low, high)])

    chunks = [
        [piece if d == 0 else across(piece, d) for d, piece in enumerate(pieces[c : c + plane])]
        for c in range(0, len(pieces), plane)
    ]
    rights = [[] for _ in chunks]
    lefts = [[] for _ in chunks]
    base = [(s, s) for s in range(plane)]
    for step in range(steps):
        came = [(plane + s, plane + s) for s in range(step)]
        back = [(plane + s, plane + step + s) for s in range(step)]
        for c, chunk in enumerate(chunks):
            go, ret = pick(
                pick_table,
                (*chunk, *rights[c], *lefts[c]),
                (step, limit + step),
                (base + came, base + back),
            )
            rights[c].append(along(go, 1))
            lefts[c].append(along(ret, -1))
    came = [(plane + s, plane + s) for s in range(steps)]
    back = [(plane + limit + s, plane + steps + s) for s in range(steps)]
    done = []
    for c, chunk in enumerate(chunks):
        found = pick(
            last_table,
            (*chunk, *rights[c], *lefts[c]),
            tuple(range(plane)),
            (base + came + back,) * plane,
        )
        done += [block if d == 0 else across(block, d) for d, block in enumerate(found)]
    count = halves * plane
    return tuple(assemble(halves, plane, me, done[m : m + count]) for m in (0, count))


def indirect(experts, halves, plane, me, source, pieces):
    count = halves * plane
    results = []
    for m in (0, count):
        matrix = assemble(halves, plane, me, pieces[m : m + count])
        results.append(exchange(matrix.reshape(experts, -1, matrix.shape[1])))
    results = [exchange(arrange(spread, source)) for spread in results]
    return tuple(result.reshape(-1, result.shape[2]) for result in results)


def arrange_kernel(index_ref, in_ref, out_ref):
    for i in range(in_ref.shape[0]):
        out_ref[i] = in_ref[index_ref[i]]


def arrange(blocks, index):
    return call(
        arrange_kernel,
        jax.ShapeDtypeStruct(blocks.shape, blocks.dtype),
        [SMEM, VMEM],
        (index, blocks),
        0,
        4 * blocks.size,
        limit=16,
    )


def exchange(blocks):
    return lax.all_to_all(blocks, "ep", split_axis=0, concat_axis=0, tiled=True)


def shards(
    dy,
    probs,
    expert_ids,
    copy_choice,
    saved_inputs,
    saved_gate,
    saved_up,
    down_weight,
    gate_weight,
    up_weight,
    new_owner,
):
    experts = lax.axis_size("ep")
    capacity = saved_inputs.shape[3]
    width = dy.shape[1]
    inner = saved_gate.shape[4]
    half = width // 2
    rows = experts * capacity
    bf16 = jnp.bfloat16
    shape = lambda *dims: jax.ShapeDtypeStruct(dims, bf16)
    rep = lax.axis_index("rep").astype(jnp.int32).reshape(1)

    outgoing = pl.pallas_call(
        functools.partial(dispatch_kernel, capacity),
        out_shape=shape(rows, width),
        grid=(1,),
        in_specs=[SMEM]
        + [pl.BlockSpec(a.shape, lambda i: (0, 0)) for a in (expert_ids.T, copy_choice.T, probs.T, dy)],
        out_specs=pl.BlockSpec((rows, width), lambda i: (0, 0)),
        compiler_params=pltpu.CompilerParams(vmem_limit_bytes=16 * MIB),
    )(rep, expert_ids.T, copy_choice.T, probs.T, dy)
    routed = exchange(outgoing.reshape(experts, capacity, width)).reshape(rows, width)

    inputs = saved_inputs.reshape(rows, width)
    down = down_weight[0]
    other_inputs = from_partner(inputs)
    other_down = from_partner(down)
    high, low, transposed = call(
        inputs_kernel,
        (shape(2 * rows, 2 * rows), shape(2 * rows, 2 * rows), shape(half, 2 * rows)),
        [SMEM, VMEM, VMEM],
        (rep, inputs, other_inputs),
        2 * 3 * rows * rows * width,
        8 * rows * width,
    )
    own_rows, partner_rows = call(
        rows_kernel,
        (shape(rows, inner), shape(rows, inner)),
        [SMEM] + [VMEM] * 5,
        (rep, routed, down, other_down, saved_gate.reshape(rows, inner), saved_up.reshape(rows, inner)),
        2 * rows * width * inner,
        2 * inner * width,
    )
    other_rows = from_partner(partner_rows)
    own_b = call(
        schulz_kernel,
        shape(2 * rows, inner),
        [VMEM] * 4,
        (own_rows, other_rows, high, low),
        ITERS * 2 * inner * inner * (inner + 6 * rows),
        8 * rows * inner,
        scratch=(
            pltpu.VMEM((2 * rows, inner), bf16),
            pltpu.VMEM((inner, inner), bf16),
            pltpu.VMEM((inner, inner), bf16),
        ),
    )
    other_b = from_partner(own_b)
    halves = 2
    plane = 1
    while 4 * plane * plane <= experts:
        plane *= 2
    line = experts // plane
    place = lax.axis_index("ep").astype(jnp.int32).reshape(1)
    me = place % plane
    order = jnp.arange(experts, dtype=jnp.int32)
    source = jnp.sum(
        jnp.where(new_owner[None, :] == order[:, None], order[None, :], 0), axis=1, dtype=jnp.int32
    )
    pieces = call(
        functools.partial(update_kernel, step_scale * math.sqrt(width), halves, plane),
        (shape(half // (halves * plane), inner),) * (2 * halves * plane),
        [SMEM, SMEM] + [VMEM] * 5,
        (rep, me, own_b, other_b, transposed, gate_weight[0], up_weight[0]),
        2 * 2 * half * 2 * rows * inner,
        8 * half * inner,
    )
    if line == plane:
        least, limit = plane - 1, plane + 2
        pick_table, last_table, count = route(line, plane, limit, new_owner, place)
        branches = [
            functools.partial(direct, steps, limit, line, plane, halves)
            for steps in range(least, limit + 1)
        ]

        def other(me, pick_table, last_table, pieces):
            return indirect(experts, halves, plane, me, source, pieces)

        gate, up = lax.switch(
            jnp.maximum(count[0] - least, 0),
            branches + [other],
            me,
            pick_table,
            last_table,
            pieces,
        )
    else:
        gate, up = indirect(experts, halves, plane, me, source, pieces)
    return (gate[None], up[None])


def solution(mesh):
    in_specs = (
        P("ep", None),
        P("ep", None),
        P("ep", None),
        P("ep", None),
        P("ep", "rep", None, None, None),
        P("ep", "rep", None, None, None),
        P("ep", "rep", None, None, None),
        P("ep", None, "rep"),
        P("ep", "rep", None),
        P("ep", "rep", None),
        P(),
    )
    out_specs = (P("ep", "rep", None), P("ep", "rep", None))
    return jax.shard_map(shards, mesh=mesh, in_specs=in_specs, out_specs=out_specs, check_vma=False)
```

```python
import functools
import math

import jax
import jax.numpy as jnp
from jax import lax
from jax.experimental import pallas as pl
from jax.experimental.pallas import tpu as pltpu
from jax.sharding import PartitionSpec as P

ITERS = 2

quintic_first = 3.4445
quintic_second = -4.775
quintic_third = 2.0315
step_scale = 2.0
epsilon = 1e-07

VMEM = pl.BlockSpec(memory_space=pltpu.VMEM)
SMEM = pl.BlockSpec(memory_space=pltpu.SMEM)
ANY = pl.BlockSpec(memory_space=pl.ANY)
MIB = 1 << 20


def from_partner(block):
    return lax.ppermute(block, "rep", [(0, 1), (1, 0)])


def mm(left, right, dims=((1,), (0,))):
    return lax.dot_general(left, right, (dims, ((), ())), preferred_element_type=jnp.float32)


def call(kernel, outs, in_specs, args, flops, nbytes, scratch=(), limit=24):
    return pl.pallas_call(
        kernel,
        out_shape=outs,
        in_specs=in_specs,
        out_specs=jax.tree.map(lambda _: VMEM, outs),
        scratch_shapes=list(scratch),
        compiler_params=pltpu.CompilerParams(vmem_limit_bytes=limit * MIB),
        cost_estimate=pl.CostEstimate(flops=flops, bytes_accessed=nbytes, transcendentals=0),
    )(*args)


def dispatch_kernel(capacity, rep_ref, ids_ref, copy_ref, probs_ref, dy_ref, out_ref):
    rows, tokens = out_ref.shape[0], dy_ref.shape[0]
    own = rep_ref[0]
    expert = lax.broadcasted_iota(jnp.int32, (rows, tokens), 0) // capacity
    slot = lax.broadcasted_iota(jnp.int32, (rows, tokens), 0) % capacity
    mask = jnp.zeros((rows, tokens), jnp.float32)
    weight = jnp.zeros((rows, tokens), jnp.float32)
    for k in range(ids_ref.shape[0]):
        here = (ids_ref[k : k + 1, :] == expert) & (copy_ref[k : k + 1, :] == own)
        mask = jnp.where(here, 1.0, mask)
        weight = jnp.where(here, probs_ref[k : k + 1, :], weight)
    before = lax.broadcasted_iota(jnp.int32, (tokens, tokens), 0) < lax.broadcasted_iota(
        jnp.int32, (tokens, tokens), 1
    )
    rank = mm(mask.astype(jnp.bfloat16), jnp.where(before, 1.0, 0.0).astype(jnp.bfloat16))
    hot = (mask > 0.5) & (rank.astype(jnp.int32) == slot)
    scale = jnp.sum(jnp.where(hot, weight, 0.0), axis=1, keepdims=True)
    picked = mm(jnp.where(hot, 1.0, 0.0).astype(jnp.bfloat16), dy_ref[...])
    out_ref[...] = (picked * scale).astype(jnp.bfloat16)


def inputs_kernel(rep_ref, own_ref, other_ref, high_ref, low_ref, xt_ref):
    half = xt_ref.shape[0]
    rows = own_ref.shape[0]
    own, other = own_ref[...], other_ref[...]

    def store(first, second, block):
        high = block.astype(jnp.bfloat16)
        high_ref[first, second] = high
        low_ref[first, second] = (block - high.astype(jnp.float32)).astype(jnp.bfloat16)

    begin, end = slice(0, rows), slice(rows, None)
    store(begin, begin, mm(own, own, ((1,), (1,))))
    store(end, end, mm(other, other, ((1,), (1,))))
    cross = mm(own, other, ((1,), (1,)))
    store(begin, end, cross)
    store(end, begin, cross.T)
    start = pl.multiple_of(rep_ref[0] * half, half)
    xt_ref[:, :rows] = own_ref[:, pl.ds(start, half)].T
    xt_ref[:, rows:] = other_ref[:, pl.ds(start, half)].T


def rows_kernel(rep_ref, routed_ref, own_down_ref, other_down_ref, gate_ref, up_ref, *refs):
    own_ref, partner_ref = refs[-2:]
    half = own_down_ref.shape[1]
    inner = own_down_ref.shape[0]
    rep = rep_ref[0]
    first = pl.multiple_of(rep * half, half)
    second = pl.multiple_of((1 - rep) * half, half)
    hidden = mm(routed_ref[:, pl.ds(first, half)], own_down_ref[...], ((1,), (1,)))
    hidden += mm(routed_ref[:, pl.ds(second, half)], other_down_ref[...], ((1,), (1,)))
    hidden = hidden / math.sqrt(inner)
    gate = gate_ref[...].astype(jnp.float32)
    up = up_ref[...].astype(jnp.float32)
    sigmoid = 1.0 / (1.0 + jnp.exp(-gate))
    gate_rows = (hidden * up * sigmoid * (1.0 + gate * (1.0 - sigmoid))).astype(jnp.bfloat16)
    up_rows = (hidden * gate * sigmoid).astype(jnp.bfloat16)

    @pl.when(rep == 0)
    def _():
        own_ref[...] = gate_rows
        partner_ref[...] = up_rows

    @pl.when(rep == 1)
    def _():
        own_ref[...] = up_rows
        partner_ref[...] = gate_rows


def schulz_kernel(own_ref, other_ref, high_ref, low_ref, b_ref, r_ref, gram_ref, poly_ref):
    rows = own_ref.shape[0]
    r_ref[:rows] = own_ref[...]
    r_ref[rows:] = other_ref[...]
    size = None
    for repeat in range(ITERS):
        base = r_ref[...]
        mapped = mm(high_ref[...], base) + mm(low_ref[...], base)
        if repeat == 0:
            squares = jnp.sum(base.astype(jnp.float32) * mapped)
            total = jnp.sqrt(jnp.maximum(squares, 0.0)) + epsilon
            size = 1.0 / total
        gram = mm(base, mapped.astype(jnp.bfloat16), ((0,), (0,)))
        if repeat == 0:
            gram = gram * (size * size)
        gram_ref[...] = gram.astype(jnp.bfloat16)
        square = mm(gram_ref[...], gram_ref[...])
        poly_ref[...] = (
            quintic_second * gram_ref[...].astype(jnp.float32) + quintic_third * square
        ).astype(jnp.bfloat16)
        mixed = quintic_first * base.astype(jnp.float32) + mm(base, poly_ref[...])
        if repeat == 0:
            mixed = mixed * size
        if repeat == ITERS - 1:
            b_ref[...] = mixed.astype(jnp.bfloat16)
        else:
            r_ref[...] = mixed.astype(jnp.bfloat16)


def update_kernel(factor, halves, plane, rep_ref, me_ref, own_ref, other_ref, xt_ref, *refs):
    weights, outs = refs[:2], refs[2:]
    rows = own_ref.shape[0] // 2
    size = outs[0].shape[0]
    rep = rep_ref[0]

    def update(matrix, swapped):
        b_ref = other_ref if swapped else own_ref
        begin, end = slice(0, rows), slice(rows, None)
        first, second = (end, begin) if swapped else (begin, end)
        for h in range(halves):
            for d in range(plane):
                start = pl.multiple_of((h * plane + (me_ref[0] ^ d)) * size, size)
                x = xt_ref[pl.ds(start, size), :]
                ortho = mm(x[:, :rows], b_ref[first]) + mm(x[:, rows:], b_ref[second])
                weight = weights[matrix][pl.ds(start, size), :].astype(jnp.float32)
                outs[(matrix * halves + h) * plane + d][...] = (weight - factor * ortho).astype(
                    jnp.bfloat16
                )

    @pl.when(rep == 0)
    def _():
        update(0, False)
        update(1, True)

    @pl.when(rep == 1)
    def _():
        update(0, True)
        update(1, False)


def route_kernel(line, plane, least, limit, owner_ref, place_ref, pick_ref, last_ref, branch_ref, at, slot, right, left):
    items = line * plane
    mine, me = place_ref[0] // plane, place_ref[0] % plane

    def begin(i, carry):
        at[i] = i // plane
        slot[i] = (i % plane) ^ me
        return carry

    lax.fori_loop(0, items, begin, 0)
    count = jnp.int32(0)
    for step in range(limit):
        for z in range(line):
            right[z] = -1
            left[z] = -1

        def choose(i, carry):
            place, target = at[i], owner_ref[i] // plane

            @pl.when(target > place)
            def _():
                best = right[place]
                reach = jnp.where(best >= 0, owner_ref[jnp.maximum(best, 0)] // plane, -1)
                right[place] = jnp.where(target > reach, i, best)

            @pl.when(target < place)
            def _():
                best = left[place]
                reach = jnp.where(best >= 0, owner_ref[jnp.maximum(best, 0)] // plane, line)
                left[place] = jnp.where(target < reach, i, best)

            return carry + jnp.where(target != place, 1, 0)

        waiting = lax.fori_loop(0, items, choose, jnp.int32(0))
        count = jnp.where(waiting > 0, step + 1, count)
        go, back = right[mine], left[mine]
        go = jnp.where(go >= 0, slot[jnp.maximum(go, 0)], 0)
        back = jnp.where(back >= 0, slot[jnp.maximum(back, 0)], 0)
        pick_ref[step] = jnp.where(mine % 2 == 0, go, back)
        pick_ref[limit + step] = jnp.where(mine % 2 == 0, back, go)
        for z in range(line):
            for chosen, move in ((right, 1), (left, -1)):

                @pl.when(chosen[z] >= 0)
                def _():
                    at[chosen[z]] = z + move
                    slot[chosen[z]] = plane + step

    def finish(i, carry):
        target = owner_ref[i] // plane

        @pl.when(target == mine)
        def _():
            link = jnp.where(target < i // plane, mine, mine + 1)
            second = (slot[i] >= plane) & (link % 2 == 1)
            last_ref[(owner_ref[i] % plane) ^ me] = slot[i] + jnp.where(second, limit, 0)

        return carry + jnp.where(target != at[i], 1, 0)

    rest = lax.fori_loop(0, items, finish, jnp.int32(0))
    branch_ref[0] = jnp.where(rest > 0, 0, jnp.maximum(count - least, 0) + 1)


def route(line, plane, least, limit, owner, place):
    table = lambda n: jax.ShapeDtypeStruct((n,), jnp.int32)
    return pl.pallas_call(
        functools.partial(route_kernel, line, plane, least, limit),
        out_shape=(table(2 * limit), table(plane), table(1)),
        in_specs=[SMEM, SMEM],
        out_specs=(SMEM, SMEM, SMEM),
        scratch_shapes=[pltpu.SMEM((n,), jnp.int32) for n in (line * plane, line * plane, line, line)],
        compiler_params=pltpu.CompilerParams(vmem_limit_bytes=MIB),
    )(owner, place)


def pick_kernel(entries, groups, table_ref, *refs):
    outs = refs[len(refs) - len(entries) :]
    for entry, group, out in zip(entries, groups, outs):
        for number, index in group:

            @pl.when(table_ref[entry] == number)
            def _():
                def copy(i, carry):
                    place = pl.ds(pl.multiple_of(i * 16, 16), 16)
                    out[place, :] = refs[index][place, :]
                    return carry

                lax.fori_loop(0, out.shape[0] // 16, copy, 0, unroll=4)


def pick(table, blocks, entries, groups, after):
    shape = jax.ShapeDtypeStruct(blocks[0].shape, blocks[0].dtype)
    return call(
        functools.partial(pick_kernel, entries, groups),
        (shape,) * len(entries),
        [SMEM] + [VMEM] * len(blocks) + [ANY] * len(after),
        (table, *blocks, *after),
        0,
        4 * blocks[0].size * len(entries),
        limit=6,
    )


def hold_kernel(*refs):
    pass


def hold(blocks, after):
    return pl.pallas_call(
        hold_kernel,
        out_shape=tuple(jax.ShapeDtypeStruct(b.shape, b.dtype) for b in blocks),
        in_specs=[ANY] * (len(blocks) + 1),
        out_specs=(ANY,) * len(blocks),
        input_output_aliases={i: i for i in range(len(blocks))},
        compiler_params=pltpu.CompilerParams(vmem_limit_bytes=MIB),
    )(*blocks, after)


def assemble_kernel(halves, plane, me_ref, *refs):
    per = halves * plane
    count = (len(refs) - 1) // (per + 1)
    pieces, outs, sems = refs[: count * per], refs[count * per : -1], refs[-1]
    size = pieces[0].shape[0]
    copies = []
    for n, piece in enumerate(pieces):
        h, d = n % per // plane, n % plane
        start = pl.multiple_of((h * plane + (me_ref[0] ^ d)) * size, size)
        copies.append(
            pltpu.make_async_copy(piece, outs[n // per].at[pl.ds(start, size), :], sems.at[n])
        )
    for copy in copies:
        copy.start()
    for copy in copies:
        copy.wait()


def assemble(halves, plane, me, pieces):
    rows, columns = pieces[0].shape
    per = halves * plane
    count = len(pieces) // per
    shape = jax.ShapeDtypeStruct((per * rows, columns), pieces[0].dtype)
    return pl.pallas_call(
        functools.partial(assemble_kernel, halves, plane),
        out_shape=(shape,) * count,
        in_specs=[SMEM] + [VMEM] * len(pieces),
        out_specs=(pl.BlockSpec(memory_space=pl.ANY),) * count,
        scratch_shapes=[pltpu.SemaphoreType.DMA((len(pieces),))],
        compiler_params=pltpu.CompilerParams(vmem_limit_bytes=8 * MIB),
        cost_estimate=pl.CostEstimate(
            flops=0, bytes_accessed=4 * per * rows * columns * count, transcendentals=0
        ),
    )(me, *pieces)


def direct(steps, limit, line, plane, me, owner, pick_table, last_table, pieces):
    items = line * plane

    def across(block, d):
        return lax.ppermute(block, "ep", [(i, i ^ d) for i in range(items)])

    def along(block, stream):
        pairs = []
        for z in range(stream, line - 1, 2):
            for i in range(z * plane, (z + 1) * plane):
                pairs += [(i, i + plane), (i + plane, i)]
        return lax.ppermute(block, "ep", pairs)

    def spread(chunk):
        return [piece if d == 0 else across(piece, d) for d, piece in enumerate(chunk)]

    groups = [pieces[c : c + plane] for c in range(0, len(pieces), plane)]
    chunks = [spread(groups[0])]
    came = [([], []) for _ in groups]
    base = [(s, s) for s in range(plane)]
    order = sorted((c + step, c, step) for c in range(len(groups)) for step in range(steps + 1))
    after = ()
    waits = {}
    collected = [None] * len(groups)
    for position, (_, c, step) in enumerate(order):
        first, second = came[c]
        after += waits.pop(position, ())
        if step == steps:
            from_first = [(plane + s, plane + s) for s in range(steps)]
            from_second = [(plane + limit + s, plane + steps + s) for s in range(steps)]
            found = pick(
                last_table,
                (*chunks[c], *first, *second),
                tuple(range(plane)),
                (base + from_first + from_second,) * plane,
                after,
            )
            after = found[:1]
            collected[c] = spread(found)
            waits[position + 4] = tuple(collected[c][1:])
            continue
        from_first = [(plane + s, plane + s) for s in range(step)]
        from_second = [(plane + s, plane + step + s) for s in range(step)]
        sent = pick(
            pick_table,
            (*chunks[c], *first, *second),
            (step, limit + step),
            (base + from_second, base + from_first),
            after,
        )
        after = sent[:1]
        if step == 0 and c + 1 < len(groups):
            chunks.append(spread(hold(groups[c + 1], sent[0])))
        first.append(along(sent[0], 0))
        second.append(along(sent[1], 1))
    return tuple(piece for chunk in collected for piece in chunk)


def indirect(experts, halves, plane, me, owner, pieces):
    order = jnp.arange(experts, dtype=jnp.int32)
    source = jnp.sum(
        jnp.where(owner[None, :] == order[:, None], order[None, :], 0), axis=1, dtype=jnp.int32
    )
    matrices = assemble(halves, plane, me, pieces)
    results = [exchange(m.reshape(experts, -1, m.shape[1])) for m in matrices]
    results = [exchange(arrange(spread, source)) for spread in results]
    return tuple(result.reshape(-1, result.shape[2]) for result in results)


def cut(halves, plane, me, matrix):
    size = matrix.shape[0] // (halves * plane)
    return [
        lax.dynamic_slice_in_dim(matrix, (h * plane + (me[0] ^ d)) * size, size)
        for h in range(halves)
        for d in range(plane)
    ]


def arrange_kernel(index_ref, in_ref, out_ref):
    for i in range(in_ref.shape[0]):
        out_ref[i] = in_ref[index_ref[i]]


def arrange(blocks, index):
    return call(
        arrange_kernel,
        jax.ShapeDtypeStruct(blocks.shape, blocks.dtype),
        [SMEM, VMEM],
        (index, blocks),
        0,
        4 * blocks.size,
        limit=8,
    )


def exchange(blocks):
    return lax.all_to_all(blocks, "ep", split_axis=0, concat_axis=0, tiled=True)


def shards(
    dy,
    probs,
    expert_ids,
    copy_choice,
    saved_inputs,
    saved_gate,
    saved_up,
    down_weight,
    gate_weight,
    up_weight,
    new_owner,
):
    experts = lax.axis_size("ep")
    capacity = saved_inputs.shape[3]
    width = dy.shape[1]
    inner = saved_gate.shape[4]
    half = width // 2
    rows = experts * capacity
    bf16 = jnp.bfloat16
    shape = lambda *dims: jax.ShapeDtypeStruct(dims, bf16)
    rep = lax.axis_index("rep").astype(jnp.int32).reshape(1)

    halves = 2
    plane = 1
    while 4 * plane * plane <= experts:
        plane *= 2
    line = experts // plane
    place = lax.axis_index("ep").astype(jnp.int32)
    me = (place & (plane - 1)).reshape(1)
    least, limit = plane - 1, plane + 1
    tables = ()
    if line == plane:
        pick_table, last_table, branch = route(
            line, plane, least, limit, new_owner, place.reshape(1)
        )
        tables = (pick_table,)
    outgoing = pl.pallas_call(
        functools.partial(dispatch_kernel, capacity),
        out_shape=shape(rows, width),
        grid=(1,),
        in_specs=[SMEM]
        + [pl.BlockSpec(a.shape, lambda i: (0, 0)) for a in (expert_ids.T, copy_choice.T, probs.T, dy)],
        out_specs=pl.BlockSpec((rows, width), lambda i: (0, 0)),
        compiler_params=pltpu.CompilerParams(vmem_limit_bytes=8 * MIB),
    )(rep, expert_ids.T, copy_choice.T, probs.T, dy)
    routed = exchange(outgoing.reshape(experts, capacity, width)).reshape(rows, width)

    inputs = saved_inputs.reshape(rows, width)
    down = down_weight[0]
    other_inputs = from_partner(inputs)
    other_down = from_partner(down)
    high, low, transposed = call(
        inputs_kernel,
        (shape(2 * rows, 2 * rows), shape(2 * rows, 2 * rows), shape(half, 2 * rows)),
        [SMEM, VMEM, VMEM],
        (rep, inputs, other_inputs),
        2 * 3 * rows * rows * width,
        8 * rows * width,
    )
    own_rows, partner_rows = call(
        rows_kernel,
        (shape(rows, inner), shape(rows, inner)),
        [SMEM] + [VMEM] * 5 + [SMEM] * len(tables),
        (
            rep,
            routed,
            down,
            other_down,
            saved_gate.reshape(rows, inner),
            saved_up.reshape(rows, inner),
            *tables,
        ),
        2 * rows * width * inner,
        2 * inner * width,
    )
    other_rows = from_partner(partner_rows)
    own_b = call(
        schulz_kernel,
        shape(2 * rows, inner),
        [VMEM] * 4,
        (own_rows, other_rows, high, low),
        ITERS * 2 * inner * inner * (inner + 6 * rows),
        8 * rows * inner,
        scratch=(
            pltpu.VMEM((2 * rows, inner), bf16),
            pltpu.VMEM((inner, inner), bf16),
            pltpu.VMEM((inner, inner), bf16),
        ),
    )
    other_b = from_partner(own_b)
    pieces = call(
        functools.partial(update_kernel, step_scale * math.sqrt(width), halves, plane),
        (shape(half // (halves * plane), inner),) * (2 * halves * plane),
        [SMEM, SMEM] + [VMEM] * 5,
        (rep, me, own_b, other_b, transposed, gate_weight[0], up_weight[0]),
        2 * 2 * half * 2 * rows * inner,
        8 * half * inner,
    )
    if line == plane:

        def other(me, owner, pick_table, last_table, pieces):
            matrices = indirect(experts, halves, plane, me, owner, pieces)
            return tuple(piece for m in matrices for piece in cut(halves, plane, me, m))

        branches = [
            functools.partial(direct, steps, limit, line, plane)
            for steps in range(least, limit + 1)
        ]
        pieces = lax.switch(branch[0], [other] + branches, me, new_owner, pick_table, last_table, pieces)
        gate, up = assemble(halves, plane, me, pieces)
    else:
        gate, up = indirect(experts, halves, plane, me, new_owner, pieces)
    return (gate[None], up[None])


def solution(mesh):
    in_specs = (
        P("ep", None),
        P("ep", None),
        P("ep", None),
        P("ep", None),
        P("ep", "rep", None, None, None),
        P("ep", "rep", None, None, None),
        P("ep", "rep", None, None, None),
        P("ep", None, "rep"),
        P("ep", "rep", None),
        P("ep", "rep", None),
        P(),
    )
    out_specs = (P("ep", "rep", None), P("ep", "rep", None))
    return jax.shard_map(shards, mesh=mesh, in_specs=in_specs, out_specs=out_specs, check_vma=False)
```

```python
import functools
import math

import jax
import jax.numpy as jnp
from jax import lax
from jax.experimental import pallas as pl
from jax.experimental.pallas import tpu as pltpu
from jax.sharding import PartitionSpec as P

ITERS = 2

quintic_first = 3.4445
quintic_second = -4.775
quintic_third = 2.0315
step_scale = 2.0
epsilon = 1e-07

VMEM = pl.BlockSpec(memory_space=pltpu.VMEM)
SMEM = pl.BlockSpec(memory_space=pltpu.SMEM)
ANY = pl.BlockSpec(memory_space=pl.ANY)
MIB = 1 << 20


def from_partner(block):
    return lax.ppermute(block, "rep", [(0, 1), (1, 0)])


def mm(left, right, dims=((1,), (0,))):
    return lax.dot_general(left, right, (dims, ((), ())), preferred_element_type=jnp.float32)


def call(kernel, outs, in_specs, args, flops, nbytes, scratch=(), limit=16):
    return pl.pallas_call(
        kernel,
        out_shape=outs,
        in_specs=in_specs,
        out_specs=jax.tree.map(lambda _: VMEM, outs),
        scratch_shapes=list(scratch),
        compiler_params=pltpu.CompilerParams(vmem_limit_bytes=limit * MIB),
        cost_estimate=pl.CostEstimate(flops=flops, bytes_accessed=nbytes, transcendentals=0),
    )(*args)


def dispatch_kernel(capacity, rep_ref, ids_ref, copy_ref, probs_ref, dy_ref, out_ref):
    rows, tokens = out_ref.shape[0], dy_ref.shape[0]
    own = rep_ref[0]
    expert = lax.broadcasted_iota(jnp.int32, (rows, tokens), 0) // capacity
    slot = lax.broadcasted_iota(jnp.int32, (rows, tokens), 0) % capacity
    mask = jnp.zeros((rows, tokens), jnp.float32)
    weight = jnp.zeros((rows, tokens), jnp.float32)
    for k in range(ids_ref.shape[0]):
        here = (ids_ref[k : k + 1, :] == expert) & (copy_ref[k : k + 1, :] == own)
        mask = jnp.where(here, 1.0, mask)
        weight = jnp.where(here, probs_ref[k : k + 1, :], weight)
    before = lax.broadcasted_iota(jnp.int32, (tokens, tokens), 0) < lax.broadcasted_iota(
        jnp.int32, (tokens, tokens), 1
    )
    rank = mm(mask.astype(jnp.bfloat16), jnp.where(before, 1.0, 0.0).astype(jnp.bfloat16))
    hot = (mask > 0.5) & (rank.astype(jnp.int32) == slot)
    scale = jnp.sum(jnp.where(hot, weight, 0.0), axis=1, keepdims=True)
    picked = mm(jnp.where(hot, 1.0, 0.0).astype(jnp.bfloat16), dy_ref[...])
    out_ref[...] = (picked * scale).astype(jnp.bfloat16)


def pack_kernel(rep_ref, choice_ref, dy_ref, out_ref, table):
    top, half = choice_ref.shape[0] // 3, dy_ref.shape[1] // 2
    tokens = dy_ref.shape[0]
    out_ref[:, :half] = dy_ref[:, pl.ds(pl.multiple_of(rep_ref[0] * half, half), half)]
    table[...] = jnp.zeros_like(table)
    table[: 2 * top, :tokens] = choice_ref[: 2 * top, :]
    rest = choice_ref[2 * top :, :]
    for part in range(3):
        rounded = rest.astype(jnp.bfloat16).astype(jnp.float32)
        table[(2 + part) * top : (3 + part) * top, :tokens] = rounded
        rest = rest - rounded
    out_ref[:, half:] = table[...].T[:tokens].astype(jnp.bfloat16)


def join_kernel(*refs):
    out_ref = refs[-1]
    rows = refs[0].shape[0]
    for n in range(out_ref.shape[0] // rows):
        out_ref[n * rows : (n + 1) * rows, :] = refs[n][...]


def join(blocks, after):
    rows, columns = blocks[0].shape
    return call(
        join_kernel,
        jax.ShapeDtypeStruct((len(blocks) * rows, columns), blocks[0].dtype),
        [VMEM] * len(blocks) + [ANY] * len(after),
        (*blocks, *after),
        0,
        4 * len(blocks) * rows * columns,
        limit=2,
    )


def gather_kernel(
    capacity,
    line,
    plane,
    top,
    rep_ref,
    place_ref,
    own_down_ref,
    other_down_ref,
    own_gate_ref,
    own_up_ref,
    other_gate_ref,
    other_up_ref,
    *refs,
):
    own_refs, other_refs = refs[:plane], refs[plane : 2 * plane]
    out_ref, own_dy, other_dy, table = refs[-4:]
    half, inner = own_down_ref.shape[1], own_down_ref.shape[0]
    block = own_refs[0].shape[0]
    tokens = block * plane
    rows = out_ref.shape[0] // 2
    per = block // line
    rep, place = rep_ref[0], place_ref[0]
    mine, me = place // plane, place % plane
    for d in range(plane):
        own_dy[d * block : (d + 1) * block, :] = own_refs[d][:, :half]
        other_dy[d * block : (d + 1) * block, :] = other_refs[d][:, :half]
        table[:, d * block : (d + 1) * block] = own_refs[d][:, half:].astype(jnp.float32).T
    ids = table[:top, :]
    copies = table[top : 2 * top, :]
    probs = table[2 * top : 3 * top, :] + table[3 * top : 4 * top, :] + table[4 * top : 5 * top, :]
    here = ids == place.astype(jnp.float32)
    prob = jnp.sum(jnp.where(here, probs, 0.0), axis=0, keepdims=True)
    chosen = [
        jnp.sum(
            jnp.where(here & (copies == copy.astype(jnp.float32)), 1.0, 0.0), axis=0, keepdims=True
        )
        for copy in (rep, 1 - rep)
    ]
    first = lax.broadcasted_iota(jnp.int32, (tokens, tokens), 0)
    second = lax.broadcasted_iota(jnp.int32, (tokens, tokens), 1)
    before = jnp.where((first // per == second // per) & (first < second), 1.0, 0.0)
    both = jnp.concatenate(chosen + [jnp.zeros((6, tokens), jnp.float32)], axis=0)
    rank = mm(both.astype(jnp.bfloat16), before.astype(jnp.bfloat16)).astype(jnp.int32)
    number = lax.broadcasted_iota(jnp.int32, (1, tokens), 1) // per
    source = ((number % line) ^ mine) * plane + ((number // line) ^ me)
    row = lax.broadcasted_iota(jnp.int32, (rows, tokens), 0)
    hot = jnp.concatenate(
        [
            (row == source * capacity + rank[c : c + 1]) & (chosen[c] > 0.5)
            for c in range(2)
        ],
        axis=0,
    )
    scale = jnp.sum(jnp.where(hot, prob, 0.0), axis=1, keepdims=True)
    hot = jnp.where(hot, 1.0, 0.0).astype(jnp.bfloat16)
    routed = (mm(hot, own_dy[...]) * scale).astype(jnp.bfloat16)
    hidden = mm(routed, own_down_ref[...], ((1,), (1,)))
    routed = (mm(hot, other_dy[...]) * scale).astype(jnp.bfloat16)
    hidden += mm(routed, other_down_ref[...], ((1,), (1,)))
    hidden = hidden / math.sqrt(inner)
    for c, (gate_ref, up_ref) in enumerate(
        ((own_gate_ref, own_up_ref), (other_gate_ref, other_up_ref))
    ):
        part = slice(c * rows, (c + 1) * rows)
        gate = gate_ref[...].astype(jnp.float32)
        sigmoid = 1.0 / (1.0 + jnp.exp(-gate))

        @pl.when(rep == 0)
        def _():
            up = up_ref[...].astype(jnp.float32)
            out_ref[part, :] = (
                hidden[part] * up * sigmoid * (1.0 + gate * (1.0 - sigmoid))
            ).astype(jnp.bfloat16)

        @pl.when(rep == 1)
        def _():
            out_ref[part, :] = (hidden[part] * gate * sigmoid).astype(jnp.bfloat16)


def inputs_kernel(rep_ref, own_ref, other_ref, high_ref, low_ref, xt_ref):
    half = xt_ref.shape[0]
    rows = own_ref.shape[0]
    own, other = own_ref[...], other_ref[...]

    def store(first, second, block):
        high = block.astype(jnp.bfloat16)
        high_ref[first, second] = high
        low_ref[first, second] = (block - high.astype(jnp.float32)).astype(jnp.bfloat16)

    begin, end = slice(0, rows), slice(rows, None)
    store(begin, begin, mm(own, own, ((1,), (1,))))
    store(end, end, mm(other, other, ((1,), (1,))))
    cross = mm(own, other, ((1,), (1,)))
    store(begin, end, cross)
    store(end, begin, cross.T)
    start = pl.multiple_of(rep_ref[0] * half, half)
    xt_ref[:, :rows] = own_ref[:, pl.ds(start, half)].T
    xt_ref[:, rows:] = other_ref[:, pl.ds(start, half)].T


def rows_kernel(rep_ref, routed_ref, own_down_ref, other_down_ref, gate_ref, up_ref, *refs):
    own_ref, partner_ref = refs[-2:]
    half = own_down_ref.shape[1]
    inner = own_down_ref.shape[0]
    rep = rep_ref[0]
    first = pl.multiple_of(rep * half, half)
    second = pl.multiple_of((1 - rep) * half, half)
    hidden = mm(routed_ref[:, pl.ds(first, half)], own_down_ref[...], ((1,), (1,)))
    hidden += mm(routed_ref[:, pl.ds(second, half)], other_down_ref[...], ((1,), (1,)))
    hidden = hidden / math.sqrt(inner)
    gate = gate_ref[...].astype(jnp.float32)
    up = up_ref[...].astype(jnp.float32)
    sigmoid = 1.0 / (1.0 + jnp.exp(-gate))
    gate_rows = (hidden * up * sigmoid * (1.0 + gate * (1.0 - sigmoid))).astype(jnp.bfloat16)
    up_rows = (hidden * gate * sigmoid).astype(jnp.bfloat16)

    @pl.when(rep == 0)
    def _():
        own_ref[...] = gate_rows
        partner_ref[...] = up_rows

    @pl.when(rep == 1)
    def _():
        own_ref[...] = up_rows
        partner_ref[...] = gate_rows


def schulz_kernel(high_ref, low_ref, xt_ref, *refs):
    row_refs, (b_ref, r_ref, gram_ref, poly_ref) = refs[:-4], refs[-4:]
    rows = row_refs[0].shape[0]
    for n, row_ref in enumerate(row_refs):
        r_ref[n * rows : (n + 1) * rows] = row_ref[...]
    size = None
    for repeat in range(ITERS):
        base = r_ref[...]
        mapped = mm(high_ref[...], base) + mm(low_ref[...], base)
        if repeat == 0:
            squares = jnp.sum(base.astype(jnp.float32) * mapped)
            total = jnp.sqrt(jnp.maximum(squares, 0.0)) + epsilon
            size = 1.0 / total
        gram = mm(base, mapped.astype(jnp.bfloat16), ((0,), (0,)))
        if repeat == 0:
            gram = gram * (size * size)
        gram_ref[...] = gram.astype(jnp.bfloat16)
        square = mm(gram_ref[...], gram_ref[...])
        poly_ref[...] = (
            quintic_second * gram_ref[...].astype(jnp.float32) + quintic_third * square
        ).astype(jnp.bfloat16)
        mixed = quintic_first * base.astype(jnp.float32) + mm(base, poly_ref[...])
        if repeat == 0:
            mixed = mixed * size
        if repeat == ITERS - 1:
            b_ref[...] = mixed.astype(jnp.bfloat16)
        else:
            r_ref[...] = mixed.astype(jnp.bfloat16)


LAYOUT = (((0, 0), (0, 1)), ((1, 0), (1, 1)))
HALVES = 2


def update_kernel(factor, plane, rep_ref, me_ref, own_ref, other_ref, xt_ref, *refs):
    weights, outs = refs[:2], refs[2:]
    rows = own_ref.shape[0] // 2
    size = weights[0].shape[0] // (HALVES * plane)
    rep = rep_ref[0]

    def update(swapped):
        for c, parts in enumerate(LAYOUT):
            for k, (matrix, h) in enumerate(parts):
                b_ref = other_ref if swapped[matrix] else own_ref
                begin, end = slice(0, rows), slice(rows, None)
                first, second = (end, begin) if swapped[matrix] else (begin, end)
                for d in range(plane):
                    start = pl.multiple_of((h * plane + (me_ref[0] ^ d)) * size, size)
                    x = xt_ref[pl.ds(start, size), :]
                    ortho = mm(x[:, :rows], b_ref[first]) + mm(x[:, rows:], b_ref[second])
                    weight = weights[matrix][pl.ds(start, size), :].astype(jnp.float32)
                    outs[c * plane + d][k * size : (k + 1) * size] = (
                        weight - factor * ortho
                    ).astype(jnp.bfloat16)

    @pl.when(rep == 0)
    def _():
        update((False, True))

    @pl.when(rep == 1)
    def _():
        update((True, False))


def route_kernel(line, plane, least, limit, owner_ref, place_ref, pick_ref, last_ref, branch_ref, at, slot, right, left):
    items = line * plane
    mine, me = place_ref[0] // plane, place_ref[0] % plane

    def begin(i, carry):
        at[i] = i // plane
        slot[i] = (i % plane) ^ me
        return carry

    lax.fori_loop(0, items, begin, 0)
    count = jnp.int32(0)
    for step in range(limit):
        for z in range(line):
            right[z] = -1
            left[z] = -1

        def choose(i, carry):
            place, target = at[i], owner_ref[i] // plane

            @pl.when(target > place)
            def _():
                best = right[place]
                reach = jnp.where(best >= 0, owner_ref[jnp.maximum(best, 0)] // plane, -1)
                right[place] = jnp.where(target > reach, i, best)

            @pl.when(target < place)
            def _():
                best = left[place]
                reach = jnp.where(best >= 0, owner_ref[jnp.maximum(best, 0)] // plane, line)
                left[place] = jnp.where(target < reach, i, best)

            return carry + jnp.where(target != place, 1, 0)

        waiting = lax.fori_loop(0, items, choose, jnp.int32(0))
        count = jnp.where(waiting > 0, step + 1, count)
        go, back = right[mine], left[mine]
        go = jnp.where(go >= 0, slot[jnp.maximum(go, 0)], 0)
        back = jnp.where(back >= 0, slot[jnp.maximum(back, 0)], 0)
        pick_ref[step] = jnp.where(mine % 2 == 0, go, back)
        pick_ref[limit + step] = jnp.where(mine % 2 == 0, back, go)
        for z in range(line):
            for chosen, move in ((right, 1), (left, -1)):

                @pl.when(chosen[z] >= 0)
                def _():
                    at[chosen[z]] = z + move
                    slot[chosen[z]] = plane + step

    def finish(i, carry):
        target = owner_ref[i] // plane

        @pl.when(target == mine)
        def _():
            link = jnp.where(target < i // plane, mine, mine + 1)
            second = (slot[i] >= plane) & (link % 2 == 1)
            last_ref[(owner_ref[i] % plane) ^ me] = slot[i] + jnp.where(second, limit, 0)

        return carry + jnp.where(target != at[i], 1, 0)

    rest = lax.fori_loop(0, items, finish, jnp.int32(0))
    branch_ref[0] = jnp.where(rest > 0, 0, jnp.maximum(count - least, 0) + 1)


def route(line, plane, least, limit, owner, place):
    table = lambda n: jax.ShapeDtypeStruct((n,), jnp.int32)
    return pl.pallas_call(
        functools.partial(route_kernel, line, plane, least, limit),
        out_shape=(table(2 * limit), table(plane), table(1)),
        in_specs=[SMEM, SMEM],
        out_specs=(SMEM, SMEM, SMEM),
        scratch_shapes=[pltpu.SMEM((n,), jnp.int32) for n in (line * plane, line * plane, line, line)],
        compiler_params=pltpu.CompilerParams(vmem_limit_bytes=MIB),
    )(owner, place)


def pick_kernel(entries, groups, table_ref, *refs):
    outs = refs[len(refs) - len(entries) :]
    for entry, group, out in zip(entries, groups, outs):
        for number, index in group:

            @pl.when(table_ref[entry] == number)
            def _():
                def copy(i, carry):
                    place = pl.ds(pl.multiple_of(i * 16, 16), 16)
                    out[place, :] = refs[index][place, :]
                    return carry

                lax.fori_loop(0, out.shape[0] // 16, copy, 0, unroll=1)


def pick(table, blocks, entries, groups, after):
    shape = jax.ShapeDtypeStruct(blocks[0].shape, blocks[0].dtype)
    return call(
        functools.partial(pick_kernel, entries, groups),
        (shape,) * len(entries),
        [SMEM] + [VMEM] * len(blocks) + [ANY] * len(after),
        (table, *blocks, *after),
        0,
        4 * blocks[0].size * len(entries),
        limit=6,
    )


def hold_kernel(*refs):
    pass


def hold(blocks, after):
    return pl.pallas_call(
        hold_kernel,
        out_shape=tuple(jax.ShapeDtypeStruct(b.shape, b.dtype) for b in blocks),
        in_specs=[ANY] * (len(blocks) + 1),
        out_specs=(ANY,) * len(blocks),
        input_output_aliases={i: i for i in range(len(blocks))},
        compiler_params=pltpu.CompilerParams(vmem_limit_bytes=MIB),
    )(*blocks, after)


def assemble_kernel(plane, me_ref, *refs):
    pieces, outs, sems = refs[: len(LAYOUT) * plane], refs[len(LAYOUT) * plane : -1], refs[-1]
    size = pieces[0].shape[0] // len(LAYOUT[0])
    copies = []
    for c, parts in enumerate(LAYOUT):
        for d in range(plane):
            for k, (matrix, h) in enumerate(parts):
                start = pl.multiple_of((h * plane + (me_ref[0] ^ d)) * size, size)
                copies.append(
                    pltpu.make_async_copy(
                        pieces[c * plane + d].at[pl.ds(k * size, size), :],
                        outs[matrix].at[pl.ds(start, size), :],
                        sems.at[len(copies)],
                    )
                )
    for copy in copies:
        copy.start()
    for copy in copies:
        copy.wait()


def assemble(plane, me, pieces):
    rows, columns = pieces[0].shape
    rows = rows // len(LAYOUT[0]) * plane * HALVES
    shape = jax.ShapeDtypeStruct((rows, columns), pieces[0].dtype)
    return pl.pallas_call(
        functools.partial(assemble_kernel, plane),
        out_shape=(shape,) * 2,
        in_specs=[SMEM] + [VMEM] * len(pieces),
        out_specs=(ANY,) * 2,
        scratch_shapes=[pltpu.SemaphoreType.DMA((2 * HALVES * plane,))],
        compiler_params=pltpu.CompilerParams(vmem_limit_bytes=8 * MIB),
        cost_estimate=pl.CostEstimate(
            flops=0, bytes_accessed=8 * rows * columns, transcendentals=0
        ),
    )(me, *pieces)


def direct(steps, limit, line, plane, me, owner, pick_table, last_table, pieces):
    items = line * plane

    def across(block, d):
        return lax.ppermute(block, "ep", [(i, i ^ d) for i in range(items)])

    def along(block, stream):
        pairs = []
        for z in range(stream, line - 1, 2):
            for i in range(z * plane, (z + 1) * plane):
                pairs += [(i, i + plane), (i + plane, i)]
        return lax.ppermute(block, "ep", pairs)

    def spread(chunk):
        return [piece if d == 0 else across(piece, d) for d, piece in enumerate(chunk)]

    groups = [pieces[c : c + plane] for c in range(0, len(pieces), plane)]
    chunks = [spread(groups[0])]
    came = [([], []) for _ in groups]
    base = [(s, s) for s in range(plane)]
    order = sorted((1.5 * c + step, c, step) for c in range(len(groups)) for step in range(steps + 1))
    after = ()
    waits = {}
    collected = [None] * len(groups)
    for position, (_, c, step) in enumerate(order):
        first, second = came[c]
        after += waits.pop(position, ())
        if step == steps:
            from_first = [(plane + s, plane + s) for s in range(steps)]
            from_second = [(plane + limit + s, plane + steps + s) for s in range(steps)]
            found = pick(
                last_table,
                (*chunks[c], *first, *second),
                tuple(range(plane)),
                (base + from_first + from_second,) * plane,
                after,
            )
            after = found[:1]
            collected[c] = spread(found)
            waits[position + 2] = tuple(collected[c][1:])
            continue
        from_first = [(plane + s, plane + s) for s in range(step)]
        from_second = [(plane + s, plane + step + s) for s in range(step)]
        sent = pick(
            pick_table,
            (*chunks[c], *first, *second),
            (step, limit + step),
            (base + from_second, base + from_first),
            after,
        )
        after = sent[:1]
        if step == 0 and c + 1 < len(groups):
            chunks.append(spread(hold(groups[c + 1], sent[0])))
        first.append(along(sent[0], 0))
        second.append(along(sent[1], 1))
    return tuple(piece for chunk in collected for piece in chunk)


def indirect(experts, plane, me, owner, pieces):
    order = jnp.arange(experts, dtype=jnp.int32)
    source = jnp.sum(
        jnp.where(owner[None, :] == order[:, None], order[None, :], 0), axis=1, dtype=jnp.int32
    )
    results = [exchange(m.reshape(experts, -1, m.shape[1])) for m in assemble(plane, me, pieces)]
    results = [exchange(arrange(spread, source)) for spread in results]
    return tuple(result.reshape(-1, result.shape[2]) for result in results)


def cut(plane, me, matrices):
    size = matrices[0].shape[0] // (HALVES * plane)
    return tuple(
        jnp.concatenate(
            [
                lax.dynamic_slice_in_dim(matrices[m], (h * plane + (me[0] ^ d)) * size, size)
                for m, h in parts
            ]
        )
        for parts in LAYOUT
        for d in range(plane)
    )


def arrange_kernel(index_ref, in_ref, out_ref):
    for i in range(in_ref.shape[0]):
        out_ref[i] = in_ref[index_ref[i]]


def arrange(blocks, index):
    return call(
        arrange_kernel,
        jax.ShapeDtypeStruct(blocks.shape, blocks.dtype),
        [SMEM, VMEM],
        (index, blocks),
        0,
        4 * blocks.size,
        limit=8,
    )


def exchange(blocks):
    return lax.all_to_all(blocks, "ep", split_axis=0, concat_axis=0, tiled=True)


def shards(
    dy,
    probs,
    expert_ids,
    copy_choice,
    saved_inputs,
    saved_gate,
    saved_up,
    down_weight,
    gate_weight,
    up_weight,
    new_owner,
):
    experts = lax.axis_size("ep")
    capacity = saved_inputs.shape[3]
    width = dy.shape[1]
    inner = saved_gate.shape[4]
    half = width // 2
    rows = experts * capacity
    bf16 = jnp.bfloat16
    shape = lambda *dims: jax.ShapeDtypeStruct(dims, bf16)
    rep = lax.axis_index("rep").astype(jnp.int32).reshape(1)

    plane = 1
    while 4 * plane * plane <= experts:
        plane *= 2
    line = experts // plane
    place = lax.axis_index("ep").astype(jnp.int32)
    me = (place & (plane - 1)).reshape(1)
    least, limit = plane - 1, plane + 1
    inputs = saved_inputs.reshape(rows, width)
    down = down_weight[0]
    other_inputs = from_partner(inputs)
    other_down = from_partner(down)
    high, low, transposed = call(
        inputs_kernel,
        (shape(2 * rows, 2 * rows), shape(2 * rows, 2 * rows), shape(half, 2 * rows)),
        [SMEM, VMEM, VMEM],
        (rep, inputs, other_inputs),
        2 * 3 * rows * rows * width,
        8 * rows * width,
    )
    gate_rows = saved_gate.reshape(rows, inner)
    up_rows = saved_up.reshape(rows, inner)
    if line == plane:
        pick_table, last_table, branch = route(
            line, plane, least, limit, new_owner, place.reshape(1)
        )
        tokens, top = expert_ids.shape
        choice = jnp.concatenate(
            [expert_ids.T.astype(jnp.float32), copy_choice.T.astype(jnp.float32), probs.T]
        )
        packed = call(
            pack_kernel,
            shape(tokens, half + 128),
            [SMEM, VMEM, VMEM],
            (rep, choice, dy),
            0,
            4 * tokens * width,
            scratch=(pltpu.VMEM((128, 128), jnp.float32),),
            limit=2,
        )
        along = lambda q: [
            (z * plane + i, (z ^ q) * plane + i) for z in range(line) for i in range(plane)
        ]
        column = join(
            [packed] + [lax.ppermute(packed, "ep", along(q)) for q in range(1, line)],
            (high,),
        )
        own_tokens = [column] + [
            lax.ppermute(column, "ep", [(i, i ^ d) for i in range(experts)])
            for d in range(1, plane)
        ]
        own_tokens[-1] = hold(own_tokens[-1:], pick_table)[0]
        other_tokens = [from_partner(block) for block in own_tokens]
        row_blocks = (
            call(
                functools.partial(gather_kernel, capacity, line, plane, top),
                shape(2 * rows, inner),
                [SMEM, SMEM] + [VMEM] * (6 + 2 * plane),
                (
                    rep,
                    place.reshape(1),
                    down,
                    other_down,
                    gate_rows,
                    up_rows,
                    from_partner(gate_rows),
                    from_partner(up_rows),
                    *own_tokens,
                    *other_tokens,
                ),
                2 * 2 * rows * width * (inner + experts * tokens),
                8 * rows * width,
                scratch=(
                    pltpu.VMEM((experts * tokens, half), bf16),
                    pltpu.VMEM((experts * tokens, half), bf16),
                    pltpu.VMEM((128, experts * tokens), jnp.float32),
                ),
                limit=24,
            ),
        )
    else:
        outgoing = pl.pallas_call(
            functools.partial(dispatch_kernel, capacity),
            out_shape=shape(rows, width),
            grid=(1,),
            in_specs=[SMEM]
            + [pl.BlockSpec(a.shape, lambda i: (0, 0)) for a in (expert_ids.T, copy_choice.T, probs.T, dy)],
            out_specs=pl.BlockSpec((rows, width), lambda i: (0, 0)),
            compiler_params=pltpu.CompilerParams(vmem_limit_bytes=8 * MIB),
        )(rep, expert_ids.T, copy_choice.T, probs.T, dy)
        routed = exchange(outgoing.reshape(experts, capacity, width)).reshape(rows, width)

        own_rows, partner_rows = call(
            rows_kernel,
            (shape(rows, inner), shape(rows, inner)),
            [SMEM] + [VMEM] * 5 + [ANY],
            (
                rep,
                routed,
                down,
                other_down,
                gate_rows,
                up_rows,
                high,
            ),
            2 * rows * width * inner,
            2 * inner * width,
        )
        row_blocks = (own_rows, from_partner(partner_rows))
    own_b = call(
        schulz_kernel,
        shape(2 * rows, inner),
        [VMEM, VMEM, ANY] + [VMEM] * len(row_blocks),
        (high, low, transposed, *row_blocks),
        ITERS * 2 * inner * inner * (inner + 6 * rows),
        8 * rows * inner,
        scratch=(
            pltpu.VMEM((2 * rows, inner), bf16),
            pltpu.VMEM((inner, inner), bf16),
            pltpu.VMEM((inner, inner), bf16),
        ),
    )
    other_b = from_partner(own_b)
    pieces = call(
        functools.partial(update_kernel, step_scale * math.sqrt(width), plane),
        tuple(
            shape(len(parts) * half // (HALVES * plane), inner)
            for parts in LAYOUT
            for _ in range(plane)
        ),
        [SMEM, SMEM] + [VMEM] * 5,
        (rep, me, own_b, other_b, transposed, gate_weight[0], up_weight[0]),
        2 * 2 * half * 2 * rows * inner,
        8 * half * inner,
    )
    if line == plane:

        def other(me, owner, pick_table, last_table, pieces):
            return cut(plane, me, indirect(experts, plane, me, owner, pieces))

        branches = [
            functools.partial(direct, steps, limit, line, plane)
            for steps in range(least, limit + 1)
        ]
        pieces = lax.switch(branch[0], [other] + branches, me, new_owner, pick_table, last_table, pieces)
        gate, up = assemble(plane, me, pieces)
    else:
        gate, up = indirect(experts, plane, me, new_owner, pieces)
    return (gate[None], up[None])


def solution(mesh):
    in_specs = (
        P("ep", None),
        P("ep", None),
        P("ep", None),
        P("ep", None),
        P("ep", "rep", None, None, None),
        P("ep", "rep", None, None, None),
        P("ep", "rep", None, None, None),
        P("ep", None, "rep"),
        P("ep", "rep", None),
        P("ep", "rep", None),
        P(),
    )
    out_specs = (P("ep", "rep", None), P("ep", "rep", None))
    return jax.shard_map(shards, mesh=mesh, in_specs=in_specs, out_specs=out_specs, check_vma=False)
```

```python
import functools
import math

import jax
import jax.numpy as jnp
from jax import lax
from jax.experimental import pallas as pl
from jax.experimental.pallas import tpu as pltpu
from jax.sharding import PartitionSpec as P

ITERS = 2

quintic_first = 3.4445
quintic_second = -4.775
quintic_third = 2.0315
step_scale = 2.0
epsilon = 1e-07

VMEM = pl.BlockSpec(memory_space=pltpu.VMEM)
SMEM = pl.BlockSpec(memory_space=pltpu.SMEM)
ANY = pl.BlockSpec(memory_space=pl.ANY)
MIB = 1 << 20


def from_partner(block):
    return lax.ppermute(block, "rep", [(0, 1), (1, 0)])


def mm(left, right, dims=((1,), (0,))):
    return lax.dot_general(left, right, (dims, ((), ())), preferred_element_type=jnp.float32)


def call(kernel, outs, in_specs, args, flops, nbytes, scratch=(), limit=16):
    return pl.pallas_call(
        kernel,
        out_shape=outs,
        in_specs=in_specs,
        out_specs=jax.tree.map(lambda _: VMEM, outs),
        scratch_shapes=list(scratch),
        compiler_params=pltpu.CompilerParams(vmem_limit_bytes=limit * MIB),
        cost_estimate=pl.CostEstimate(flops=flops, bytes_accessed=nbytes, transcendentals=0),
    )(*args)


def dispatch_kernel(capacity, rep_ref, ids_ref, copy_ref, probs_ref, dy_ref, out_ref):
    rows, tokens = out_ref.shape[0], dy_ref.shape[0]
    own = rep_ref[0]
    expert = lax.broadcasted_iota(jnp.int32, (rows, tokens), 0) // capacity
    slot = lax.broadcasted_iota(jnp.int32, (rows, tokens), 0) % capacity
    mask = jnp.zeros((rows, tokens), jnp.float32)
    weight = jnp.zeros((rows, tokens), jnp.float32)
    for k in range(ids_ref.shape[0]):
        here = (ids_ref[k : k + 1, :] == expert) & (copy_ref[k : k + 1, :] == own)
        mask = jnp.where(here, 1.0, mask)
        weight = jnp.where(here, probs_ref[k : k + 1, :], weight)
    before = lax.broadcasted_iota(jnp.int32, (tokens, tokens), 0) < lax.broadcasted_iota(
        jnp.int32, (tokens, tokens), 1
    )
    rank = mm(mask.astype(jnp.bfloat16), jnp.where(before, 1.0, 0.0).astype(jnp.bfloat16))
    hot = (mask > 0.5) & (rank.astype(jnp.int32) == slot)
    scale = jnp.sum(jnp.where(hot, weight, 0.0), axis=1, keepdims=True)
    picked = mm(jnp.where(hot, 1.0, 0.0).astype(jnp.bfloat16), dy_ref[...])
    out_ref[...] = (picked * scale).astype(jnp.bfloat16)


def pack_kernel(rep_ref, choice_ref, dy_ref, out_ref, table):
    top, half = choice_ref.shape[0] // 3, dy_ref.shape[1] // 2
    tokens = dy_ref.shape[0]
    out_ref[:, :half] = dy_ref[:, pl.ds(pl.multiple_of(rep_ref[0] * half, half), half)]
    table[...] = jnp.zeros_like(table)
    table[: 2 * top, :tokens] = choice_ref[: 2 * top, :]
    rest = choice_ref[2 * top :, :]
    for part in range(3):
        rounded = rest.astype(jnp.bfloat16).astype(jnp.float32)
        table[(2 + part) * top : (3 + part) * top, :tokens] = rounded
        rest = rest - rounded
    out_ref[:, half:] = table[...].T[:tokens].astype(jnp.bfloat16)


def join_kernel(*refs):
    out_ref = refs[-1]
    rows = refs[0].shape[0]
    for n in range(out_ref.shape[0] // rows):
        out_ref[n * rows : (n + 1) * rows, :] = refs[n][...]


def join(blocks, after):
    rows, columns = blocks[0].shape
    return call(
        join_kernel,
        jax.ShapeDtypeStruct((len(blocks) * rows, columns), blocks[0].dtype),
        [VMEM] * len(blocks) + [ANY] * len(after),
        (*blocks, *after),
        0,
        4 * len(blocks) * rows * columns,
        limit=2,
    )


def gather_kernel(
    capacity,
    line,
    plane,
    top,
    rep_ref,
    place_ref,
    own_down_ref,
    other_down_ref,
    own_gate_ref,
    own_up_ref,
    other_gate_ref,
    other_up_ref,
    *refs,
):
    own_refs, other_refs = refs[:plane], refs[plane : 2 * plane]
    out_ref, own_dy, other_dy, table = refs[-4:]
    half, inner = own_down_ref.shape[1], own_down_ref.shape[0]
    block = own_refs[0].shape[0]
    tokens = block * plane
    rows = out_ref.shape[0] // 2
    per = block // line
    rep, place = rep_ref[0], place_ref[0]
    mine, me = place // plane, place % plane
    for d in range(plane):
        own_dy[d * block : (d + 1) * block, :] = own_refs[d][:, :half]
        other_dy[d * block : (d + 1) * block, :] = other_refs[d][:, :half]
        table[:, d * block : (d + 1) * block] = own_refs[d][:, half:].astype(jnp.float32).T
    ids = table[:top, :]
    copies = table[top : 2 * top, :]
    probs = table[2 * top : 3 * top, :] + table[3 * top : 4 * top, :] + table[4 * top : 5 * top, :]
    here = ids == place.astype(jnp.float32)
    prob = jnp.sum(jnp.where(here, probs, 0.0), axis=0, keepdims=True)
    chosen = [
        jnp.sum(
            jnp.where(here & (copies == copy.astype(jnp.float32)), 1.0, 0.0), axis=0, keepdims=True
        )
        for copy in (rep, 1 - rep)
    ]
    first = lax.broadcasted_iota(jnp.int32, (tokens, tokens), 0)
    second = lax.broadcasted_iota(jnp.int32, (tokens, tokens), 1)
    before = jnp.where((first // per == second // per) & (first < second), 1.0, 0.0)
    both = jnp.concatenate(chosen + [jnp.zeros((6, tokens), jnp.float32)], axis=0)
    rank = mm(both.astype(jnp.bfloat16), before.astype(jnp.bfloat16)).astype(jnp.int32)
    number = lax.broadcasted_iota(jnp.int32, (1, tokens), 1) // per
    source = ((number % line) ^ mine) * plane + ((number // line) ^ me)
    row = lax.broadcasted_iota(jnp.int32, (rows, tokens), 0)
    hot = jnp.concatenate(
        [
            (row == source * capacity + rank[c : c + 1]) & (chosen[c] > 0.5)
            for c in range(2)
        ],
        axis=0,
    )
    scale = jnp.sum(jnp.where(hot, prob, 0.0), axis=1, keepdims=True)
    hot = jnp.where(hot, 1.0, 0.0).astype(jnp.bfloat16)
    routed = (mm(hot, own_dy[...]) * scale).astype(jnp.bfloat16)
    hidden = mm(routed, own_down_ref[...], ((1,), (1,)))
    routed = (mm(hot, other_dy[...]) * scale).astype(jnp.bfloat16)
    hidden += mm(routed, other_down_ref[...], ((1,), (1,)))
    hidden = hidden / math.sqrt(inner)
    for c, (gate_ref, up_ref) in enumerate(
        ((own_gate_ref, own_up_ref), (other_gate_ref, other_up_ref))
    ):
        part = slice(c * rows, (c + 1) * rows)
        gate = gate_ref[...].astype(jnp.float32)
        sigmoid = 1.0 / (1.0 + jnp.exp(-gate))

        @pl.when(rep == 0)
        def _():
            up = up_ref[...].astype(jnp.float32)
            out_ref[part, :] = (
                hidden[part] * up * sigmoid * (1.0 + gate * (1.0 - sigmoid))
            ).astype(jnp.bfloat16)

        @pl.when(rep == 1)
        def _():
            out_ref[part, :] = (hidden[part] * gate * sigmoid).astype(jnp.bfloat16)


def inputs_kernel(rep_ref, own_ref, other_ref, high_ref, low_ref, xt_ref):
    half = xt_ref.shape[0]
    rows = own_ref.shape[0]
    own, other = own_ref[...], other_ref[...]

    def store(first, second, block):
        high = block.astype(jnp.bfloat16)
        high_ref[first, second] = high
        low_ref[first, second] = (block - high.astype(jnp.float32)).astype(jnp.bfloat16)

    begin, end = slice(0, rows), slice(rows, None)
    store(begin, begin, mm(own, own, ((1,), (1,))))
    store(end, end, mm(other, other, ((1,), (1,))))
    cross = mm(own, other, ((1,), (1,)))
    store(begin, end, cross)
    store(end, begin, cross.T)
    start = pl.multiple_of(rep_ref[0] * half, half)
    xt_ref[:, :rows] = own_ref[:, pl.ds(start, half)].T
    xt_ref[:, rows:] = other_ref[:, pl.ds(start, half)].T


def rows_kernel(rep_ref, routed_ref, own_down_ref, other_down_ref, gate_ref, up_ref, *refs):
    own_ref, partner_ref = refs[-2:]
    half = own_down_ref.shape[1]
    inner = own_down_ref.shape[0]
    rep = rep_ref[0]
    first = pl.multiple_of(rep * half, half)
    second = pl.multiple_of((1 - rep) * half, half)
    hidden = mm(routed_ref[:, pl.ds(first, half)], own_down_ref[...], ((1,), (1,)))
    hidden += mm(routed_ref[:, pl.ds(second, half)], other_down_ref[...], ((1,), (1,)))
    hidden = hidden / math.sqrt(inner)
    gate = gate_ref[...].astype(jnp.float32)
    up = up_ref[...].astype(jnp.float32)
    sigmoid = 1.0 / (1.0 + jnp.exp(-gate))
    gate_rows = (hidden * up * sigmoid * (1.0 + gate * (1.0 - sigmoid))).astype(jnp.bfloat16)
    up_rows = (hidden * gate * sigmoid).astype(jnp.bfloat16)

    @pl.when(rep == 0)
    def _():
        own_ref[...] = gate_rows
        partner_ref[...] = up_rows

    @pl.when(rep == 1)
    def _():
        own_ref[...] = up_rows
        partner_ref[...] = gate_rows


def update_rows(factor, me, xt_ref, weight_ref, b_ref, swapped, outs):
    rows = b_ref.shape[0] // 2
    begin, end = slice(0, rows), slice(rows, None)
    first, second = (end, begin) if swapped else (begin, end)
    for d, out in enumerate(outs):
        size = out.shape[0]
        place = pl.ds(pl.multiple_of((me ^ d) * size, size), size)
        x = xt_ref[place, :]
        ortho = mm(x[:, :rows], b_ref[first]) + mm(x[:, rows:], b_ref[second])
        out[...] = (weight_ref[place, :].astype(jnp.float32) - factor * ortho).astype(jnp.bfloat16)


def schulz_kernel(factor, blocks, rep_ref, me_ref, high_ref, low_ref, xt_ref, gate_ref, up_ref, *refs):
    row_refs, b_ref, outs = refs[:blocks], refs[blocks], refs[blocks + 1 : -6]
    r_ref, gram_ref, poly_ref, x_ref, weight_ref, sems = refs[-6:]
    rows = row_refs[0].shape[0]
    rep = rep_ref[0]
    x_copy = pltpu.make_async_copy(xt_ref, x_ref, sems.at[0])
    gate_copy = pltpu.make_async_copy(gate_ref, weight_ref, sems.at[1])
    up_copy = pltpu.make_async_copy(up_ref, weight_ref, sems.at[2])
    x_copy.start()
    pl.when(rep == 0)(gate_copy.start)
    pl.when(rep == 1)(up_copy.start)
    for n, row_ref in enumerate(row_refs):
        r_ref[n * rows : (n + 1) * rows] = row_ref[...]
    size = None
    for repeat in range(ITERS):
        base = r_ref[...]
        mapped = mm(high_ref[...], base) + mm(low_ref[...], base)
        if repeat == 0:
            squares = jnp.sum(base.astype(jnp.float32) * mapped)
            total = jnp.sqrt(jnp.maximum(squares, 0.0)) + epsilon
            size = 1.0 / total
        gram = mm(base, mapped.astype(jnp.bfloat16), ((0,), (0,)))
        if repeat == 0:
            gram = gram * (size * size)
        gram_ref[...] = gram.astype(jnp.bfloat16)
        square = mm(gram_ref[...], gram_ref[...])
        poly_ref[...] = (
            quintic_second * gram_ref[...].astype(jnp.float32) + quintic_third * square
        ).astype(jnp.bfloat16)
        mixed = quintic_first * base.astype(jnp.float32) + mm(base, poly_ref[...])
        if repeat == 0:
            mixed = mixed * size
        if repeat == ITERS - 1:
            b_ref[...] = mixed.astype(jnp.bfloat16)
        else:
            r_ref[...] = mixed.astype(jnp.bfloat16)
    x_copy.wait()
    pl.when(rep == 0)(gate_copy.wait)
    pl.when(rep == 1)(up_copy.wait)
    update_rows(factor, me_ref[0], x_ref, weight_ref, b_ref, False, outs)


def update_kernel(factor, rep_ref, me_ref, xt_ref, gate_ref, up_ref, b_ref, *outs):
    for rep, weight_ref in ((0, up_ref), (1, gate_ref)):

        @pl.when(rep_ref[0] == rep)
        def _():
            update_rows(factor, me_ref[0], xt_ref, weight_ref, b_ref, True, outs)


def route_kernel(line, plane, least, limit, owner_ref, place_ref, pick_ref, last_ref, branch_ref, at, to, slot, right, left):
    items = line * plane
    shift = plane.bit_length() - 1
    mine, me = place_ref[0] >> shift, place_ref[0] & (plane - 1)
    for i in range(items):
        at[i] = i // plane
        to[i] = owner_ref[i] >> shift
        slot[i] = (i % plane) ^ me
    count = jnp.int32(0)
    even = mine & 1 == 0
    for step in range(limit):
        for z in range(line):
            right[z] = -1
            left[z] = -1
        waiting = jnp.int32(0)
        for i in range(items):
            place, target = at[i], to[i]
            key = target * items + items - 1 - i
            right[place] = jnp.maximum(right[place], jnp.where(target > place, key, -1))
            key = (line - 1 - target) * items + items - 1 - i
            left[place] = jnp.maximum(left[place], jnp.where(target < place, key, -1))
            waiting = waiting | (target ^ place)
        count = jnp.where(waiting > 0, step + 1, count)

        def chosen(key):
            return items - 1 - (jnp.maximum(key, 0) & (items - 1))

        go, back = right[mine], left[mine]
        go = jnp.where(go >= 0, slot[chosen(go)], 0)
        back = jnp.where(back >= 0, slot[chosen(back)], 0)
        pick_ref[step] = jnp.where(even, go, back)
        pick_ref[limit + step] = jnp.where(even, back, go)
        for z in range(line):
            for keys, move in ((right, 1), (left, -1)):
                key = keys[z]
                item = chosen(key)
                at[item] = jnp.where(key >= 0, z + move, at[item])
                slot[item] = jnp.where(key >= 0, plane + step, slot[item])
    rest = jnp.int32(0)
    for i in range(items):
        target = to[i]
        rest = rest | (target ^ at[i])

        @pl.when(target == mine)
        def _():
            link = jnp.where(target < i // plane, mine, mine + 1)
            second = (slot[i] >= plane) & (link & 1 == 1)
            last_ref[(owner_ref[i] & (plane - 1)) ^ me] = slot[i] + jnp.where(second, limit, 0)

    branch_ref[0] = jnp.where(rest > 0, 0, jnp.maximum(count - least, 0) + 1)


def route(line, plane, least, limit, owner, place):
    table = lambda n: jax.ShapeDtypeStruct((n,), jnp.int32)
    return pl.pallas_call(
        functools.partial(route_kernel, line, plane, least, limit),
        out_shape=(table(2 * limit), table(plane), table(1)),
        in_specs=[SMEM, SMEM],
        out_specs=(SMEM, SMEM, SMEM),
        scratch_shapes=[pltpu.SMEM((n,), jnp.int32) for n in (line * plane,) * 3 + (line,) * 2],
        compiler_params=pltpu.CompilerParams(vmem_limit_bytes=MIB),
    )(owner, place)


def pick_kernel(entries, groups, table_ref, *refs):
    outs = refs[len(refs) - len(entries) :]
    for entry, group, out in zip(entries, groups, outs):
        for number, index in group:

            @pl.when(table_ref[entry] == number)
            def _():
                def copy(i, carry):
                    place = pl.ds(pl.multiple_of(i * 16, 16), 16)
                    out[place, :] = refs[index][place, :]
                    return carry

                lax.fori_loop(0, out.shape[0] // 16, copy, 0, unroll=1)


def pick(table, blocks, entries, groups, after):
    shape = jax.ShapeDtypeStruct(blocks[0].shape, blocks[0].dtype)
    return call(
        functools.partial(pick_kernel, entries, groups),
        (shape,) * len(entries),
        [SMEM] + [VMEM] * len(blocks) + [ANY] * len(after),
        (table, *blocks, *after),
        0,
        4 * blocks[0].size * len(entries),
        limit=6,
    )


def hold_kernel(*refs):
    pass


def hold(blocks, after):
    return pl.pallas_call(
        hold_kernel,
        out_shape=tuple(jax.ShapeDtypeStruct(b.shape, b.dtype) for b in blocks),
        in_specs=[ANY] * (len(blocks) + 1),
        out_specs=(ANY,) * len(blocks),
        input_output_aliases={i: i for i in range(len(blocks))},
        compiler_params=pltpu.CompilerParams(vmem_limit_bytes=MIB),
    )(*blocks, after)


def assemble_kernel(plane, rep_ref, me_ref, *refs):
    pieces, gate_ref, up_ref, sems = refs[: 2 * plane], refs[-3], refs[-2], refs[-1]
    size = pieces[0].shape[0]

    def move(outs):
        copies = []
        for n, piece in enumerate(pieces):
            start = pl.multiple_of((me_ref[0] ^ (n % plane)) * size, size)
            out = outs[n // plane].at[pl.ds(start, size), :]
            copies.append(pltpu.make_async_copy(piece, out, sems.at[n]))
        for copy in copies:
            copy.start()
        for copy in copies:
            copy.wait()

    pl.when(rep_ref[0] == 0)(lambda: move((gate_ref, up_ref)))
    pl.when(rep_ref[0] == 1)(lambda: move((up_ref, gate_ref)))


def assemble(plane, rep, me, pieces):
    rows, columns = pieces[0].shape
    shape = jax.ShapeDtypeStruct((plane * rows, columns), pieces[0].dtype)
    return pl.pallas_call(
        functools.partial(assemble_kernel, plane),
        out_shape=(shape,) * 2,
        in_specs=[SMEM, SMEM] + [VMEM] * len(pieces),
        out_specs=(ANY,) * 2,
        scratch_shapes=[pltpu.SemaphoreType.DMA((len(pieces),))],
        compiler_params=pltpu.CompilerParams(vmem_limit_bytes=8 * MIB),
        cost_estimate=pl.CostEstimate(
            flops=0, bytes_accessed=8 * plane * rows * columns, transcendentals=0
        ),
    )(rep, me, *pieces)


def across(block, d, items):
    return block if d == 0 else lax.ppermute(block, "ep", [(i, i ^ d) for i in range(items)])


def direct(steps, limit, line, plane, rep, me, owner, pick_table, last_table, spread, own, other):
    items = line * plane

    def along(block, stream):
        pairs = []
        for z in range(stream, line - 1, 2):
            for i in range(z * plane, (z + 1) * plane):
                pairs += [(i, i + plane), (i + plane, i)]
        return lax.ppermute(block, "ep", pairs)

    groups = (own, other)
    chunks = [spread]
    came = [([], []) for _ in groups]
    base = [(s, s) for s in range(plane)]
    order = sorted((1.5 * c + step, c, step) for c in range(len(groups)) for step in range(steps + 1))
    after = ()
    waits = {}
    collected = [None] * len(groups)
    for position, (_, c, step) in enumerate(order):
        first, second = came[c]
        after += waits.pop(position, ())
        if step == steps:
            from_first = [(plane + s, plane + s) for s in range(steps)]
            from_second = [(plane + limit + s, plane + steps + s) for s in range(steps)]
            found = pick(
                last_table,
                (*chunks[c], *first, *second),
                tuple(range(plane)),
                (base + from_first + from_second,) * plane,
                after,
            )
            after = found[:1]
            collected[c] = [across(block, d, items) for d, block in enumerate(found)]
            waits[position + 2] = tuple(collected[c][1:])
            continue
        from_first = [(plane + s, plane + s) for s in range(step)]
        from_second = [(plane + s, plane + step + s) for s in range(step)]
        sent = pick(
            pick_table,
            (*chunks[c], *first, *second),
            (step, limit + step),
            (base + from_second, base + from_first),
            after,
        )
        after = sent[:1]
        if step == 0 and c + 1 < len(groups):
            chunks.append(
                [
                    across(block, d, items)
                    for d, block in enumerate(hold(groups[c + 1], sent[0]))
                ]
            )
        first.append(along(sent[0], 0))
        second.append(along(sent[1], 1))
    return tuple(piece for chunk in collected for piece in chunk)


def indirect(experts, plane, rep, me, owner, own, other):
    order = jnp.arange(experts, dtype=jnp.int32)
    source = jnp.sum(
        jnp.where(owner[None, :] == order[:, None], order[None, :], 0), axis=1, dtype=jnp.int32
    )
    matrices = assemble(plane, rep, me, (*own, *other))
    results = [exchange(m.reshape(experts, -1, m.shape[1])) for m in matrices]
    results = [exchange(arrange(spread, source)) for spread in results]
    return tuple(result.reshape(-1, result.shape[2]) for result in results)


def cut(plane, rep, me, matrices):
    size = matrices[0].shape[0] // plane
    gate, up = matrices
    return tuple(
        lax.dynamic_slice_in_dim(matrix, (me[0] ^ d) * size, size)
        for matrix in (jnp.where(rep[0] == 0, gate, up), jnp.where(rep[0] == 0, up, gate))
        for d in range(plane)
    )


def arrange_kernel(index_ref, in_ref, out_ref):
    for i in range(in_ref.shape[0]):
        out_ref[i] = in_ref[index_ref[i]]


def arrange(blocks, index):
    return call(
        arrange_kernel,
        jax.ShapeDtypeStruct(blocks.shape, blocks.dtype),
        [SMEM, VMEM],
        (index, blocks),
        0,
        4 * blocks.size,
        limit=8,
    )


def exchange(blocks):
    return lax.all_to_all(blocks, "ep", split_axis=0, concat_axis=0, tiled=True)


def shards(
    dy,
    probs,
    expert_ids,
    copy_choice,
    saved_inputs,
    saved_gate,
    saved_up,
    down_weight,
    gate_weight,
    up_weight,
    new_owner,
):
    experts = lax.axis_size("ep")
    capacity = saved_inputs.shape[3]
    width = dy.shape[1]
    inner = saved_gate.shape[4]
    half = width // 2
    rows = experts * capacity
    bf16 = jnp.bfloat16
    shape = lambda *dims: jax.ShapeDtypeStruct(dims, bf16)
    rep = lax.axis_index("rep").astype(jnp.int32).reshape(1)

    plane = 1
    while 4 * plane * plane <= experts:
        plane *= 2
    line = experts // plane
    place = lax.axis_index("ep").astype(jnp.int32)
    me = (place & (plane - 1)).reshape(1)
    least, limit = plane - 1, plane + 2
    inputs = saved_inputs.reshape(rows, width)
    down = down_weight[0]
    other_inputs = from_partner(inputs)
    other_down = from_partner(down)
    high, low, transposed = call(
        inputs_kernel,
        (shape(2 * rows, 2 * rows), shape(2 * rows, 2 * rows), shape(half, 2 * rows)),
        [SMEM, VMEM, VMEM],
        (rep, inputs, other_inputs),
        2 * 3 * rows * rows * width,
        8 * rows * width,
    )
    gate_rows = saved_gate.reshape(rows, inner)
    up_rows = saved_up.reshape(rows, inner)
    if line == plane:
        pick_table, last_table, branch = route(
            line, plane, least, limit, new_owner, place.reshape(1)
        )
        tokens, top = expert_ids.shape
        choice = jnp.concatenate(
            [expert_ids.T.astype(jnp.float32), copy_choice.T.astype(jnp.float32), probs.T]
        )
        packed = call(
            pack_kernel,
            shape(tokens, half + 128),
            [SMEM, VMEM, VMEM],
            (rep, choice, dy),
            0,
            4 * tokens * width,
            scratch=(pltpu.VMEM((128, 128), jnp.float32),),
            limit=2,
        )
        along = lambda q: [
            (z * plane + i, (z ^ q) * plane + i) for z in range(line) for i in range(plane)
        ]
        column = join(
            [packed] + [lax.ppermute(packed, "ep", along(q)) for q in range(1, line)],
            (high,),
        )
        own_tokens = [column] + [
            lax.ppermute(column, "ep", [(i, i ^ d) for i in range(experts)])
            for d in range(1, plane)
        ]
        own_tokens[-1] = hold(own_tokens[-1:], pick_table)[0]
        other_tokens = [from_partner(block) for block in own_tokens]
        row_blocks = (
            call(
                functools.partial(gather_kernel, capacity, line, plane, top),
                shape(2 * rows, inner),
                [SMEM, SMEM] + [VMEM] * (6 + 2 * plane),
                (
                    rep,
                    place.reshape(1),
                    down,
                    other_down,
                    gate_rows,
                    up_rows,
                    from_partner(gate_rows),
                    from_partner(up_rows),
                    *own_tokens,
                    *other_tokens,
                ),
                2 * 2 * rows * width * (inner + experts * tokens),
                8 * rows * width,
                scratch=(
                    pltpu.VMEM((experts * tokens, half), bf16),
                    pltpu.VMEM((experts * tokens, half), bf16),
                    pltpu.VMEM((128, experts * tokens), jnp.float32),
                ),
                limit=24,
            ),
        )
    else:
        outgoing = pl.pallas_call(
            functools.partial(dispatch_kernel, capacity),
            out_shape=shape(rows, width),
            grid=(1,),
            in_specs=[SMEM]
            + [pl.BlockSpec(a.shape, lambda i: (0, 0)) for a in (expert_ids.T, copy_choice.T, probs.T, dy)],
            out_specs=pl.BlockSpec((rows, width), lambda i: (0, 0)),
            compiler_params=pltpu.CompilerParams(vmem_limit_bytes=8 * MIB),
        )(rep, expert_ids.T, copy_choice.T, probs.T, dy)
        routed = exchange(outgoing.reshape(experts, capacity, width)).reshape(rows, width)

        own_rows, partner_rows = call(
            rows_kernel,
            (shape(rows, inner), shape(rows, inner)),
            [SMEM] + [VMEM] * 5 + [ANY],
            (
                rep,
                routed,
                down,
                other_down,
                gate_rows,
                up_rows,
                high,
            ),
            2 * rows * width * inner,
            2 * inner * width,
        )
        row_blocks = (own_rows, from_partner(partner_rows))
    factor = step_scale * math.sqrt(width)
    size = half // plane
    gate, up = gate_weight[0], up_weight[0]
    own_b, *own = call(
        functools.partial(schulz_kernel, factor, len(row_blocks)),
        (shape(2 * rows, inner),) + (shape(size, inner),) * plane,
        [SMEM, SMEM, VMEM, VMEM, ANY, ANY, ANY] + [VMEM] * len(row_blocks),
        (rep, me, high, low, transposed, gate, up, *row_blocks),
        ITERS * 2 * inner * inner * (inner + 6 * rows) + 2 * half * 2 * rows * inner,
        8 * rows * inner,
        scratch=(
            pltpu.VMEM((2 * rows, inner), bf16),
            pltpu.VMEM((inner, inner), bf16),
            pltpu.VMEM((inner, inner), bf16),
            pltpu.VMEM((half, 2 * rows), bf16),
            pltpu.VMEM((half, inner), bf16),
            pltpu.SemaphoreType.DMA((3,)),
        ),
        limit=22,
    )
    other = call(
        functools.partial(update_kernel, factor),
        (shape(size, inner),) * plane,
        [SMEM, SMEM] + [VMEM] * 4,
        (rep, me, transposed, gate, up, from_partner(own_b)),
        2 * half * 2 * rows * inner,
        8 * half * inner,
    )
    if line == plane:
        spread = [across(block, d, experts) for d, block in enumerate(own)]

        def otherwise(rep, me, owner, pick_table, last_table, spread, own, other):
            return cut(plane, rep, me, indirect(experts, plane, rep, me, owner, own, other))

        branches = [
            functools.partial(direct, steps, limit, line, plane)
            for steps in range(least, limit + 1)
        ]
        pieces = lax.switch(
            branch[0],
            [otherwise] + branches,
            rep,
            me,
            new_owner,
            pick_table,
            last_table,
            spread,
            own,
            other,
        )
        gate, up = assemble(plane, rep, me, pieces)
    else:
        gate, up = indirect(experts, plane, rep, me, new_owner, own, other)
    return (gate[None], up[None])


def solution(mesh):
    in_specs = (
        P("ep", None),
        P("ep", None),
        P("ep", None),
        P("ep", None),
        P("ep", "rep", None, None, None),
        P("ep", "rep", None, None, None),
        P("ep", "rep", None, None, None),
        P("ep", None, "rep"),
        P("ep", "rep", None),
        P("ep", "rep", None),
        P(),
    )
    out_specs = (P("ep", "rep", None), P("ep", "rep", None))
    return jax.shard_map(shards, mesh=mesh, in_specs=in_specs, out_specs=out_specs, check_vma=False)
```

```python
import functools
import math

import jax
import jax.numpy as jnp
from jax import lax
from jax.experimental import pallas as pl
from jax.experimental.pallas import tpu as pltpu
from jax.sharding import PartitionSpec as P

ITERS = 2

quintic_first = 3.4445
quintic_second = -4.775
quintic_third = 2.0315
step_scale = 2.0
epsilon = 1e-07

VMEM = pl.BlockSpec(memory_space=pltpu.VMEM)
SMEM = pl.BlockSpec(memory_space=pltpu.SMEM)
ANY = pl.BlockSpec(memory_space=pl.ANY)
MIB = 1 << 20


def from_partner(block):
    return lax.ppermute(block, "rep", [(0, 1), (1, 0)])


def mm(left, right, dims=((1,), (0,))):
    return lax.dot_general(left, right, (dims, ((), ())), preferred_element_type=jnp.float32)


def call(kernel, outs, in_specs, args, flops, nbytes, scratch=(), limit=16):
    return pl.pallas_call(
        kernel,
        out_shape=outs,
        in_specs=in_specs,
        out_specs=jax.tree.map(lambda _: VMEM, outs),
        scratch_shapes=list(scratch),
        compiler_params=pltpu.CompilerParams(vmem_limit_bytes=limit * MIB),
        cost_estimate=pl.CostEstimate(flops=flops, bytes_accessed=nbytes, transcendentals=0),
    )(*args)


def dispatch_kernel(capacity, rep_ref, ids_ref, copy_ref, probs_ref, dy_ref, out_ref):
    rows, tokens = out_ref.shape[0], dy_ref.shape[0]
    own = rep_ref[0]
    expert = lax.broadcasted_iota(jnp.int32, (rows, tokens), 0) // capacity
    slot = lax.broadcasted_iota(jnp.int32, (rows, tokens), 0) % capacity
    mask = jnp.zeros((rows, tokens), jnp.float32)
    weight = jnp.zeros((rows, tokens), jnp.float32)
    for k in range(ids_ref.shape[0]):
        here = (ids_ref[k : k + 1, :] == expert) & (copy_ref[k : k + 1, :] == own)
        mask = jnp.where(here, 1.0, mask)
        weight = jnp.where(here, probs_ref[k : k + 1, :], weight)
    before = lax.broadcasted_iota(jnp.int32, (tokens, tokens), 0) < lax.broadcasted_iota(
        jnp.int32, (tokens, tokens), 1
    )
    rank = mm(mask.astype(jnp.bfloat16), jnp.where(before, 1.0, 0.0).astype(jnp.bfloat16))
    hot = (mask > 0.5) & (rank.astype(jnp.int32) == slot)
    scale = jnp.sum(jnp.where(hot, weight, 0.0), axis=1, keepdims=True)
    picked = mm(jnp.where(hot, 1.0, 0.0).astype(jnp.bfloat16), dy_ref[...])
    out_ref[...] = (picked * scale).astype(jnp.bfloat16)


def pack_kernel(rep_ref, choice_ref, dy_ref, out_ref, table):
    top, half = choice_ref.shape[0] // 3, dy_ref.shape[1] // 2
    tokens = dy_ref.shape[0]
    out_ref[:, :half] = dy_ref[:, pl.ds(pl.multiple_of(rep_ref[0] * half, half), half)]
    table[...] = jnp.zeros_like(table)
    table[: 2 * top, :tokens] = choice_ref[: 2 * top, :]
    rest = choice_ref[2 * top :, :]
    for part in range(3):
        rounded = rest.astype(jnp.bfloat16).astype(jnp.float32)
        table[(2 + part) * top : (3 + part) * top, :tokens] = rounded
        rest = rest - rounded
    out_ref[:, half:] = table[...].T[:tokens].astype(jnp.bfloat16)


def join_kernel(*refs):
    out_ref = refs[-1]
    rows = refs[0].shape[0]
    for n in range(out_ref.shape[0] // rows):
        out_ref[n * rows : (n + 1) * rows, :] = refs[n][...]


def join(blocks, after):
    rows, columns = blocks[0].shape
    return call(
        join_kernel,
        jax.ShapeDtypeStruct((len(blocks) * rows, columns), blocks[0].dtype),
        [VMEM] * len(blocks) + [ANY] * len(after),
        (*blocks, *after),
        0,
        4 * len(blocks) * rows * columns,
        limit=2,
    )


def gather_kernel(
    capacity,
    line,
    plane,
    top,
    rep_ref,
    place_ref,
    own_down_ref,
    other_down_ref,
    own_gate_ref,
    own_up_ref,
    other_gate_ref,
    other_up_ref,
    *refs,
):
    own_refs, other_refs = refs[:plane], refs[plane : 2 * plane]
    out_ref, own_dy, other_dy, table = refs[-4:]
    half, inner = own_down_ref.shape[1], own_down_ref.shape[0]
    block = own_refs[0].shape[0]
    tokens = block * plane
    rows = out_ref.shape[0] // 2
    per = block // line
    rep, place = rep_ref[0], place_ref[0]
    mine, me = place // plane, place % plane
    for d in range(plane):
        own_dy[d * block : (d + 1) * block, :] = own_refs[d][:, :half]
        other_dy[d * block : (d + 1) * block, :] = other_refs[d][:, :half]
        table[:, d * block : (d + 1) * block] = own_refs[d][:, half:].astype(jnp.float32).T
    ids = table[:top, :]
    copies = table[top : 2 * top, :]
    probs = table[2 * top : 3 * top, :] + table[3 * top : 4 * top, :] + table[4 * top : 5 * top, :]
    here = ids == place.astype(jnp.float32)
    prob = jnp.sum(jnp.where(here, probs, 0.0), axis=0, keepdims=True)
    chosen = [
        jnp.sum(
            jnp.where(here & (copies == copy.astype(jnp.float32)), 1.0, 0.0), axis=0, keepdims=True
        )
        for copy in (rep, 1 - rep)
    ]
    first = lax.broadcasted_iota(jnp.int32, (tokens, tokens), 0)
    second = lax.broadcasted_iota(jnp.int32, (tokens, tokens), 1)
    before = jnp.where((first // per == second // per) & (first < second), 1.0, 0.0)
    both = jnp.concatenate(chosen + [jnp.zeros((6, tokens), jnp.float32)], axis=0)
    rank = mm(both.astype(jnp.bfloat16), before.astype(jnp.bfloat16)).astype(jnp.int32)
    number = lax.broadcasted_iota(jnp.int32, (1, tokens), 1) // per
    source = ((number % line) ^ mine) * plane + ((number // line) ^ me)
    row = lax.broadcasted_iota(jnp.int32, (rows, tokens), 0)
    hot = jnp.concatenate(
        [
            (row == source * capacity + rank[c : c + 1]) & (chosen[c] > 0.5)
            for c in range(2)
        ],
        axis=0,
    )
    scale = jnp.sum(jnp.where(hot, prob, 0.0), axis=1, keepdims=True)
    hot = jnp.where(hot, 1.0, 0.0).astype(jnp.bfloat16)
    routed = (mm(hot, own_dy[...]) * scale).astype(jnp.bfloat16)
    hidden = mm(routed, own_down_ref[...], ((1,), (1,)))
    routed = (mm(hot, other_dy[...]) * scale).astype(jnp.bfloat16)
    hidden += mm(routed, other_down_ref[...], ((1,), (1,)))
    hidden = hidden / math.sqrt(inner)
    for c, (gate_ref, up_ref) in enumerate(
        ((own_gate_ref, own_up_ref), (other_gate_ref, other_up_ref))
    ):
        part = slice(c * rows, (c + 1) * rows)
        gate = gate_ref[...].astype(jnp.float32)
        sigmoid = 1.0 / (1.0 + jnp.exp(-gate))

        @pl.when(rep == 0)
        def _():
            up = up_ref[...].astype(jnp.float32)
            out_ref[part, :] = (
                hidden[part] * up * sigmoid * (1.0 + gate * (1.0 - sigmoid))
            ).astype(jnp.bfloat16)

        @pl.when(rep == 1)
        def _():
            out_ref[part, :] = (hidden[part] * gate * sigmoid).astype(jnp.bfloat16)


def inputs_kernel(rep_ref, own_ref, other_ref, high_ref, low_ref, xt_ref):
    half = xt_ref.shape[0]
    rows = own_ref.shape[0]
    own, other = own_ref[...], other_ref[...]

    def store(first, second, block):
        high = block.astype(jnp.bfloat16)
        high_ref[first, second] = high
        low_ref[first, second] = (block - high.astype(jnp.float32)).astype(jnp.bfloat16)

    begin, end = slice(0, rows), slice(rows, None)
    store(begin, begin, mm(own, own, ((1,), (1,))))
    store(end, end, mm(other, other, ((1,), (1,))))
    cross = mm(own, other, ((1,), (1,)))
    store(begin, end, cross)
    store(end, begin, cross.T)
    start = pl.multiple_of(rep_ref[0] * half, half)
    xt_ref[:, :rows] = own_ref[:, pl.ds(start, half)].T
    xt_ref[:, rows:] = other_ref[:, pl.ds(start, half)].T


def rows_kernel(rep_ref, routed_ref, own_down_ref, other_down_ref, gate_ref, up_ref, *refs):
    own_ref, partner_ref = refs[-2:]
    half = own_down_ref.shape[1]
    inner = own_down_ref.shape[0]
    rep = rep_ref[0]
    first = pl.multiple_of(rep * half, half)
    second = pl.multiple_of((1 - rep) * half, half)
    hidden = mm(routed_ref[:, pl.ds(first, half)], own_down_ref[...], ((1,), (1,)))
    hidden += mm(routed_ref[:, pl.ds(second, half)], other_down_ref[...], ((1,), (1,)))
    hidden = hidden / math.sqrt(inner)
    gate = gate_ref[...].astype(jnp.float32)
    up = up_ref[...].astype(jnp.float32)
    sigmoid = 1.0 / (1.0 + jnp.exp(-gate))
    gate_rows = (hidden * up * sigmoid * (1.0 + gate * (1.0 - sigmoid))).astype(jnp.bfloat16)
    up_rows = (hidden * gate * sigmoid).astype(jnp.bfloat16)

    @pl.when(rep == 0)
    def _():
        own_ref[...] = gate_rows
        partner_ref[...] = up_rows

    @pl.when(rep == 1)
    def _():
        own_ref[...] = up_rows
        partner_ref[...] = gate_rows


def update_rows(factor, me, xt_ref, weight_ref, b_ref, swapped, outs):
    rows = b_ref.shape[0] // 2
    begin, end = slice(0, rows), slice(rows, None)
    first, second = (end, begin) if swapped else (begin, end)
    for d, out in enumerate(outs):
        size = out.shape[0]
        place = pl.ds(pl.multiple_of((me ^ d) * size, size), size)
        x = xt_ref[place, :]
        ortho = mm(x[:, :rows], b_ref[first]) + mm(x[:, rows:], b_ref[second])
        out[...] = (weight_ref[place, :].astype(jnp.float32) - factor * ortho).astype(jnp.bfloat16)


def schulz_kernel(factor, blocks, rep_ref, me_ref, high_ref, low_ref, xt_ref, gate_ref, up_ref, *refs):
    row_refs, b_ref, outs = refs[:blocks], refs[blocks], refs[blocks + 1 : -6]
    r_ref, gram_ref, poly_ref, x_ref, weight_ref, sems = refs[-6:]
    rows = row_refs[0].shape[0]
    rep = rep_ref[0]
    x_copy = pltpu.make_async_copy(xt_ref, x_ref, sems.at[0])
    gate_copy = pltpu.make_async_copy(gate_ref, weight_ref, sems.at[1])
    up_copy = pltpu.make_async_copy(up_ref, weight_ref, sems.at[2])
    x_copy.start()
    pl.when(rep == 0)(gate_copy.start)
    pl.when(rep == 1)(up_copy.start)
    for n, row_ref in enumerate(row_refs):
        r_ref[n * rows : (n + 1) * rows] = row_ref[...]
    size = None
    for repeat in range(ITERS):
        base = r_ref[...]
        mapped = mm(high_ref[...], base) + mm(low_ref[...], base)
        if repeat == 0:
            squares = jnp.sum(base.astype(jnp.float32) * mapped)
            total = jnp.sqrt(jnp.maximum(squares, 0.0)) + epsilon
            size = 1.0 / total
        gram = mm(base, mapped.astype(jnp.bfloat16), ((0,), (0,)))
        if repeat == 0:
            gram = gram * (size * size)
        gram_ref[...] = gram.astype(jnp.bfloat16)
        square = mm(gram_ref[...], gram_ref[...])
        poly_ref[...] = (
            quintic_second * gram_ref[...].astype(jnp.float32) + quintic_third * square
        ).astype(jnp.bfloat16)
        mixed = quintic_first * base.astype(jnp.float32) + mm(base, poly_ref[...])
        if repeat == 0:
            mixed = mixed * size
        if repeat == ITERS - 1:
            b_ref[...] = mixed.astype(jnp.bfloat16)
        else:
            r_ref[...] = mixed.astype(jnp.bfloat16)
    x_copy.wait()
    pl.when(rep == 0)(gate_copy.wait)
    pl.when(rep == 1)(up_copy.wait)
    update_rows(factor, me_ref[0], x_ref, weight_ref, b_ref, False, outs)


def update_kernel(factor, rep_ref, me_ref, xt_ref, gate_ref, up_ref, b_ref, *outs):
    for rep, weight_ref in ((0, up_ref), (1, gate_ref)):

        @pl.when(rep_ref[0] == rep)
        def _():
            update_rows(factor, me_ref[0], xt_ref, weight_ref, b_ref, True, outs)


def route_kernel(line, plane, least, limit, owner_ref, place_ref, pick_ref, last_ref, branch_ref, at, to, slot, right, left):
    items = line * plane
    shift = plane.bit_length() - 1
    mine, me = place_ref[0] >> shift, place_ref[0] & (plane - 1)
    for i in range(items):
        at[i] = i // plane
        to[i] = owner_ref[i] >> shift
        slot[i] = (i % plane) ^ me
    count = jnp.int32(0)
    even = mine & 1 == 0
    for step in range(limit):
        for z in range(line):
            right[z] = -1
            left[z] = -1
        waiting = jnp.int32(0)
        for i in range(items):
            place, target = at[i], to[i]
            key = target * items + items - 1 - i
            right[place] = jnp.maximum(right[place], jnp.where(target > place, key, -1))
            key = (line - 1 - target) * items + items - 1 - i
            left[place] = jnp.maximum(left[place], jnp.where(target < place, key, -1))
            waiting = waiting | (target ^ place)
        count = jnp.where(waiting > 0, step + 1, count)

        def chosen(key):
            return items - 1 - (jnp.maximum(key, 0) & (items - 1))

        go, back = right[mine], left[mine]
        go = jnp.where(go >= 0, slot[chosen(go)], 0)
        back = jnp.where(back >= 0, slot[chosen(back)], 0)
        pick_ref[step] = jnp.where(even, go, back)
        pick_ref[limit + step] = jnp.where(even, back, go)
        for z in range(line):
            for keys, move in ((right, 1), (left, -1)):
                key = keys[z]
                item = chosen(key)
                at[item] = jnp.where(key >= 0, z + move, at[item])
                slot[item] = jnp.where(key >= 0, plane + step, slot[item])
    rest = jnp.int32(0)
    for i in range(items):
        target = to[i]
        rest = rest | (target ^ at[i])

        @pl.when(target == mine)
        def _():
            link = jnp.where(target < i // plane, mine, mine + 1)
            second = (slot[i] >= plane) & (link & 1 == 1)
            last_ref[(owner_ref[i] & (plane - 1)) ^ me] = slot[i] + jnp.where(second, limit, 0)

    branch_ref[0] = jnp.where(rest > 0, 0, jnp.maximum(count - least, 0) + 1)


def route(line, plane, least, limit, owner, place):
    table = lambda n: jax.ShapeDtypeStruct((n,), jnp.int32)
    return pl.pallas_call(
        functools.partial(route_kernel, line, plane, least, limit),
        out_shape=(table(2 * limit), table(plane), table(1)),
        in_specs=[SMEM, SMEM],
        out_specs=(SMEM, SMEM, SMEM),
        scratch_shapes=[pltpu.SMEM((n,), jnp.int32) for n in (line * plane,) * 3 + (line,) * 2],
        compiler_params=pltpu.CompilerParams(vmem_limit_bytes=MIB),
    )(owner, place)


def pick_kernel(entries, groups, table_ref, *refs):
    outs = refs[len(refs) - len(entries) :]
    for entry, group, out in zip(entries, groups, outs):
        for number, index in group:

            @pl.when(table_ref[entry] == number)
            def _():
                def copy(i, carry):
                    place = pl.ds(pl.multiple_of(i * 16, 16), 16)
                    out[place, :] = refs[index][place, :]
                    return carry

                lax.fori_loop(0, out.shape[0] // 16, copy, 0, unroll=1)


def pick(table, blocks, entries, groups, after):
    shape = jax.ShapeDtypeStruct(blocks[0].shape, blocks[0].dtype)
    return call(
        functools.partial(pick_kernel, entries, groups),
        (shape,) * len(entries),
        [SMEM] + [VMEM] * len(blocks) + [ANY] * len(after),
        (table, *blocks, *after),
        0,
        4 * blocks[0].size * len(entries),
        limit=6,
    )


def hold_kernel(*refs):
    pass


def hold(blocks, after):
    return pl.pallas_call(
        hold_kernel,
        out_shape=tuple(jax.ShapeDtypeStruct(b.shape, b.dtype) for b in blocks),
        in_specs=[ANY] * (len(blocks) + 1),
        out_specs=(ANY,) * len(blocks),
        input_output_aliases={i: i for i in range(len(blocks))},
        compiler_params=pltpu.CompilerParams(vmem_limit_bytes=MIB),
    )(*blocks, after)


def assemble_kernel(plane, rep_ref, me_ref, *refs):
    pieces, gate_ref, up_ref, sems = refs[: 2 * plane], refs[-3], refs[-2], refs[-1]
    size = pieces[0].shape[0]

    def move(outs):
        copies = []
        for n, piece in enumerate(pieces):
            start = pl.multiple_of((me_ref[0] ^ (n % plane)) * size, size)
            out = outs[n // plane].at[pl.ds(start, size), :]
            copies.append(pltpu.make_async_copy(piece, out, sems.at[n]))
        for copy in copies:
            copy.start()
        for copy in copies:
            copy.wait()

    pl.when(rep_ref[0] == 0)(lambda: move((gate_ref, up_ref)))
    pl.when(rep_ref[0] == 1)(lambda: move((up_ref, gate_ref)))


def assemble(plane, rep, me, pieces):
    rows, columns = pieces[0].shape
    shape = jax.ShapeDtypeStruct((plane * rows, columns), pieces[0].dtype)
    return pl.pallas_call(
        functools.partial(assemble_kernel, plane),
        out_shape=(shape,) * 2,
        in_specs=[SMEM, SMEM] + [VMEM] * len(pieces),
        out_specs=(ANY,) * 2,
        scratch_shapes=[pltpu.SemaphoreType.DMA((len(pieces),))],
        compiler_params=pltpu.CompilerParams(vmem_limit_bytes=8 * MIB),
        cost_estimate=pl.CostEstimate(
            flops=0, bytes_accessed=8 * plane * rows * columns, transcendentals=0
        ),
    )(rep, me, *pieces)


def across(block, d, items):
    return block if d == 0 else lax.ppermute(block, "ep", [(i, i ^ d) for i in range(items)])


def direct(steps, limit, line, plane, rep, me, owner, pick_table, last_table, spread, own, other):
    items = line * plane

    def along(block, stream):
        pairs = []
        for z in range(stream, line - 1, 2):
            for i in range(z * plane, (z + 1) * plane):
                pairs += [(i, i + plane), (i + plane, i)]
        return lax.ppermute(block, "ep", pairs)

    groups = (own, other)
    chunks = [spread]
    came = [([], []) for _ in groups]
    base = [(s, s) for s in range(plane)]
    order = sorted((1.5 * c + step, c, step) for c in range(len(groups)) for step in range(steps + 1))
    after = ()
    waits = {}
    collected = [None] * len(groups)
    for position, (_, c, step) in enumerate(order):
        first, second = came[c]
        after += waits.pop(position, ())
        if step == steps:
            from_first = [(plane + s, plane + s) for s in range(steps)]
            from_second = [(plane + limit + s, plane + steps + s) for s in range(steps)]
            found = pick(
                last_table,
                (*chunks[c], *first, *second),
                tuple(range(plane)),
                (base + from_first + from_second,) * plane,
                after,
            )
            after = found[:1]
            collected[c] = [across(block, d, items) for d, block in enumerate(found)]
            waits[position + 2] = tuple(collected[c][1:])
            continue
        from_first = [(plane + s, plane + s) for s in range(step)]
        from_second = [(plane + s, plane + step + s) for s in range(step)]
        sent = pick(
            pick_table,
            (*chunks[c], *first, *second),
            (step, limit + step),
            (base + from_second, base + from_first),
            after,
        )
        after = sent[:1]
        if step == 0 and c + 1 < len(groups):
            chunks.append(
                [
                    across(block, d, items)
                    for d, block in enumerate(hold(groups[c + 1], sent[0]))
                ]
            )
        first.append(along(sent[0], 0))
        second.append(along(sent[1], 1))
    return tuple(piece for chunk in collected for piece in chunk)


def indirect(experts, plane, rep, me, owner, own, other):
    order = jnp.arange(experts, dtype=jnp.int32)
    source = jnp.sum(
        jnp.where(owner[None, :] == order[:, None], order[None, :], 0), axis=1, dtype=jnp.int32
    )
    matrices = assemble(plane, rep, me, (*own, *other))
    results = [exchange(m.reshape(experts, -1, m.shape[1])) for m in matrices]
    results = [exchange(arrange(spread, source)) for spread in results]
    return tuple(result.reshape(-1, result.shape[2]) for result in results)


def cut(plane, rep, me, matrices):
    size = matrices[0].shape[0] // plane
    gate, up = matrices
    return tuple(
        lax.dynamic_slice_in_dim(matrix, (me[0] ^ d) * size, size)
        for matrix in (jnp.where(rep[0] == 0, gate, up), jnp.where(rep[0] == 0, up, gate))
        for d in range(plane)
    )


def arrange_kernel(index_ref, in_ref, out_ref):
    for i in range(in_ref.shape[0]):
        out_ref[i] = in_ref[index_ref[i]]


def arrange(blocks, index):
    return call(
        arrange_kernel,
        jax.ShapeDtypeStruct(blocks.shape, blocks.dtype),
        [SMEM, VMEM],
        (index, blocks),
        0,
        4 * blocks.size,
        limit=8,
    )


def exchange(blocks):
    return lax.all_to_all(blocks, "ep", split_axis=0, concat_axis=0, tiled=True)


def shards(
    dy,
    probs,
    expert_ids,
    copy_choice,
    saved_inputs,
    saved_gate,
    saved_up,
    down_weight,
    gate_weight,
    up_weight,
    new_owner,
):
    experts = lax.axis_size("ep")
    capacity = saved_inputs.shape[3]
    width = dy.shape[1]
    inner = saved_gate.shape[4]
    half = width // 2
    rows = experts * capacity
    bf16 = jnp.bfloat16
    shape = lambda *dims: jax.ShapeDtypeStruct(dims, bf16)
    rep = lax.axis_index("rep").astype(jnp.int32).reshape(1)

    plane = 1
    while 4 * plane * plane <= experts:
        plane *= 2
    line = experts // plane
    place = lax.axis_index("ep").astype(jnp.int32)
    me = (place & (plane - 1)).reshape(1)
    least, limit = plane - 1, plane + 1
    inputs = saved_inputs.reshape(rows, width)
    down = down_weight[0]
    other_inputs = from_partner(inputs)
    other_down = from_partner(down)
    high, low, transposed = call(
        inputs_kernel,
        (shape(2 * rows, 2 * rows), shape(2 * rows, 2 * rows), shape(half, 2 * rows)),
        [SMEM, VMEM, VMEM],
        (rep, inputs, other_inputs),
        2 * 3 * rows * rows * width,
        8 * rows * width,
    )
    gate_rows = saved_gate.reshape(rows, inner)
    up_rows = saved_up.reshape(rows, inner)
    if line == plane:
        pick_table, last_table, branch = route(
            line, plane, least, limit, new_owner, place.reshape(1)
        )
        tokens, top = expert_ids.shape
        choice = jnp.concatenate(
            [expert_ids.T.astype(jnp.float32), copy_choice.T.astype(jnp.float32), probs.T]
        )
        packed = call(
            pack_kernel,
            shape(tokens, half + 128),
            [SMEM, VMEM, VMEM],
            (rep, choice, dy),
            0,
            4 * tokens * width,
            scratch=(pltpu.VMEM((128, 128), jnp.float32),),
            limit=2,
        )
        along = lambda q: [
            (z * plane + i, (z ^ q) * plane + i) for z in range(line) for i in range(plane)
        ]
        column = join(
            [packed] + [lax.ppermute(packed, "ep", along(q)) for q in range(1, line)],
            (high,),
        )
        own_tokens = [column] + [
            lax.ppermute(column, "ep", [(i, i ^ d) for i in range(experts)])
            for d in range(1, plane)
        ]
        own_tokens[-1] = hold(own_tokens[-1:], pick_table)[0]
        other_tokens = [from_partner(block) for block in own_tokens]
        row_blocks = (
            call(
                functools.partial(gather_kernel, capacity, line, plane, top),
                shape(2 * rows, inner),
                [SMEM, SMEM] + [VMEM] * (6 + 2 * plane),
                (
                    rep,
                    place.reshape(1),
                    down,
                    other_down,
                    gate_rows,
                    up_rows,
                    from_partner(gate_rows),
                    from_partner(up_rows),
                    *own_tokens,
                    *other_tokens,
                ),
                2 * 2 * rows * width * (inner + experts * tokens),
                8 * rows * width,
                scratch=(
                    pltpu.VMEM((experts * tokens, half), bf16),
                    pltpu.VMEM((experts * tokens, half), bf16),
                    pltpu.VMEM((128, experts * tokens), jnp.float32),
                ),
                limit=24,
            ),
        )
    else:
        outgoing = pl.pallas_call(
            functools.partial(dispatch_kernel, capacity),
            out_shape=shape(rows, width),
            grid=(1,),
            in_specs=[SMEM]
            + [pl.BlockSpec(a.shape, lambda i: (0, 0)) for a in (expert_ids.T, copy_choice.T, probs.T, dy)],
            out_specs=pl.BlockSpec((rows, width), lambda i: (0, 0)),
            compiler_params=pltpu.CompilerParams(vmem_limit_bytes=8 * MIB),
        )(rep, expert_ids.T, copy_choice.T, probs.T, dy)
        routed = exchange(outgoing.reshape(experts, capacity, width)).reshape(rows, width)

        own_rows, partner_rows = call(
            rows_kernel,
            (shape(rows, inner), shape(rows, inner)),
            [SMEM] + [VMEM] * 5 + [ANY],
            (
                rep,
                routed,
                down,
                other_down,
                gate_rows,
                up_rows,
                high,
            ),
            2 * rows * width * inner,
            2 * inner * width,
        )
        row_blocks = (own_rows, from_partner(partner_rows))
    factor = step_scale * math.sqrt(width)
    size = half // plane
    gate, up = gate_weight[0], up_weight[0]
    own_b, *own = call(
        functools.partial(schulz_kernel, factor, len(row_blocks)),
        (shape(2 * rows, inner),) + (shape(size, inner),) * plane,
        [SMEM, SMEM, VMEM, VMEM, ANY, ANY, ANY] + [VMEM] * len(row_blocks),
        (rep, me, high, low, transposed, gate, up, *row_blocks),
        ITERS * 2 * inner * inner * (inner + 6 * rows) + 2 * half * 2 * rows * inner,
        8 * rows * inner,
        scratch=(
            pltpu.VMEM((2 * rows, inner), bf16),
            pltpu.VMEM((inner, inner), bf16),
            pltpu.VMEM((inner, inner), bf16),
            pltpu.VMEM((half, 2 * rows), bf16),
            pltpu.VMEM((half, inner), bf16),
            pltpu.SemaphoreType.DMA((3,)),
        ),
        limit=22,
    )
    other = call(
        functools.partial(update_kernel, factor),
        (shape(size, inner),) * plane,
        [SMEM, SMEM] + [VMEM] * 4,
        (rep, me, transposed, gate, up, from_partner(own_b)),
        2 * half * 2 * rows * inner,
        8 * half * inner,
    )
    if line == plane:
        spread = [across(block, d, experts) for d, block in enumerate(own)]

        def otherwise(rep, me, owner, pick_table, last_table, spread, own, other):
            return cut(plane, rep, me, indirect(experts, plane, rep, me, owner, own, other))

        branches = [
            functools.partial(direct, steps, limit, line, plane)
            for steps in range(least, limit + 1)
        ]
        pieces = lax.switch(
            branch[0],
            [otherwise] + branches,
            rep,
            me,
            new_owner,
            pick_table,
            last_table,
            spread,
            own,
            other,
        )
        gate, up = assemble(plane, rep, me, pieces)
    else:
        gate, up = indirect(experts, plane, rep, me, new_owner, own, other)
    return (gate[None], up[None])


def solution(mesh):
    in_specs = (
        P("ep", None),
        P("ep", None),
        P("ep", None),
        P("ep", None),
        P("ep", "rep", None, None, None),
        P("ep", "rep", None, None, None),
        P("ep", "rep", None, None, None),
        P("ep", None, "rep"),
        P("ep", "rep", None),
        P("ep", "rep", None),
        P(),
    )
    out_specs = (P("ep", "rep", None), P("ep", "rep", None))
    return jax.shard_map(shards, mesh=mesh, in_specs=in_specs, out_specs=out_specs, check_vma=False)
```

```python
import functools
import math

import jax
import jax.numpy as jnp
from jax import lax
from jax.experimental import pallas as pl
from jax.experimental.pallas import tpu as pltpu
from jax.sharding import PartitionSpec as P

ITERS = 2

quintic_first = 3.4445
quintic_second = -4.775
quintic_third = 2.0315
step_scale = 2.0
epsilon = 1e-07

VMEM = pl.BlockSpec(memory_space=pltpu.VMEM)
SMEM = pl.BlockSpec(memory_space=pltpu.SMEM)
ANY = pl.BlockSpec(memory_space=pl.ANY)
MIB = 1 << 20


def from_partner(block):
    return lax.ppermute(block, "rep", [(0, 1), (1, 0)])


def mm(left, right, dims=((1,), (0,))):
    return lax.dot_general(left, right, (dims, ((), ())), preferred_element_type=jnp.float32)


def call(kernel, outs, in_specs, args, flops, nbytes, scratch=(), limit=16):
    return pl.pallas_call(
        kernel,
        out_shape=outs,
        in_specs=in_specs,
        out_specs=jax.tree.map(lambda _: VMEM, outs),
        scratch_shapes=list(scratch),
        compiler_params=pltpu.CompilerParams(vmem_limit_bytes=limit * MIB),
        cost_estimate=pl.CostEstimate(flops=flops, bytes_accessed=nbytes, transcendentals=0),
    )(*args)


def dispatch_kernel(capacity, rep_ref, ids_ref, copy_ref, probs_ref, dy_ref, out_ref):
    rows, tokens = out_ref.shape[0], dy_ref.shape[0]
    own = rep_ref[0]
    expert = lax.broadcasted_iota(jnp.int32, (rows, tokens), 0) // capacity
    slot = lax.broadcasted_iota(jnp.int32, (rows, tokens), 0) % capacity
    mask = jnp.zeros((rows, tokens), jnp.float32)
    weight = jnp.zeros((rows, tokens), jnp.float32)
    for k in range(ids_ref.shape[0]):
        here = (ids_ref[k : k + 1, :] == expert) & (copy_ref[k : k + 1, :] == own)
        mask = jnp.where(here, 1.0, mask)
        weight = jnp.where(here, probs_ref[k : k + 1, :], weight)
    before = lax.broadcasted_iota(jnp.int32, (tokens, tokens), 0) < lax.broadcasted_iota(
        jnp.int32, (tokens, tokens), 1
    )
    rank = mm(mask.astype(jnp.bfloat16), jnp.where(before, 1.0, 0.0).astype(jnp.bfloat16))
    hot = (mask > 0.5) & (rank.astype(jnp.int32) == slot)
    scale = jnp.sum(jnp.where(hot, weight, 0.0), axis=1, keepdims=True)
    picked = mm(jnp.where(hot, 1.0, 0.0).astype(jnp.bfloat16), dy_ref[...])
    out_ref[...] = (picked * scale).astype(jnp.bfloat16)


def pack_kernel(rep_ref, choice_ref, dy_ref, out_ref, table):
    top, half = choice_ref.shape[0] // 3, dy_ref.shape[1] // 2
    tokens = dy_ref.shape[0]
    out_ref[:, :half] = dy_ref[:, pl.ds(pl.multiple_of(rep_ref[0] * half, half), half)]
    table[...] = jnp.zeros_like(table)
    table[: 2 * top, :tokens] = choice_ref[: 2 * top, :]
    rest = choice_ref[2 * top :, :]
    for part in range(3):
        rounded = rest.astype(jnp.bfloat16).astype(jnp.float32)
        table[(2 + part) * top : (3 + part) * top, :tokens] = rounded
        rest = rest - rounded
    out_ref[:, half:] = table[...].T[:tokens].astype(jnp.bfloat16)


def join_kernel(*refs):
    out_ref = refs[-1]
    rows = refs[0].shape[0]
    for n in range(out_ref.shape[0] // rows):
        out_ref[n * rows : (n + 1) * rows, :] = refs[n][...]


def join(blocks, after):
    rows, columns = blocks[0].shape
    return call(
        join_kernel,
        jax.ShapeDtypeStruct((len(blocks) * rows, columns), blocks[0].dtype),
        [VMEM] * len(blocks) + [ANY] * len(after),
        (*blocks, *after),
        0,
        4 * len(blocks) * rows * columns,
        limit=2,
    )


def gather_kernel(
    capacity,
    line,
    plane,
    top,
    rep_ref,
    place_ref,
    own_down_ref,
    other_down_ref,
    own_gate_ref,
    own_up_ref,
    other_gate_ref,
    other_up_ref,
    *refs,
):
    own_refs, other_refs = refs[:plane], refs[plane : 2 * plane]
    out_ref, own_dy, other_dy, table = refs[-4:]
    half, inner = own_down_ref.shape[1], own_down_ref.shape[0]
    block = own_refs[0].shape[0]
    tokens = block * plane
    rows = out_ref.shape[0] // 2
    per = block // line
    rep, place = rep_ref[0], place_ref[0]
    mine, me = place // plane, place % plane
    for d in range(plane):
        own_dy[d * block : (d + 1) * block, :] = own_refs[d][:, :half]
        other_dy[d * block : (d + 1) * block, :] = other_refs[d][:, :half]
        table[:, d * block : (d + 1) * block] = own_refs[d][:, half:].astype(jnp.float32).T
    ids = table[:top, :]
    copies = table[top : 2 * top, :]
    probs = table[2 * top : 3 * top, :] + table[3 * top : 4 * top, :] + table[4 * top : 5 * top, :]
    here = ids == place.astype(jnp.float32)
    prob = jnp.sum(jnp.where(here, probs, 0.0), axis=0, keepdims=True)
    chosen = [
        jnp.sum(
            jnp.where(here & (copies == copy.astype(jnp.float32)), 1.0, 0.0), axis=0, keepdims=True
        )
        for copy in (rep, 1 - rep)
    ]
    first = lax.broadcasted_iota(jnp.int32, (tokens, tokens), 0)
    second = lax.broadcasted_iota(jnp.int32, (tokens, tokens), 1)
    before = jnp.where((first // per == second // per) & (first < second), 1.0, 0.0)
    both = jnp.concatenate(chosen + [jnp.zeros((6, tokens), jnp.float32)], axis=0)
    rank = mm(both.astype(jnp.bfloat16), before.astype(jnp.bfloat16)).astype(jnp.int32)
    number = lax.broadcasted_iota(jnp.int32, (1, tokens), 1) // per
    source = ((number % line) ^ mine) * plane + ((number // line) ^ me)
    row = lax.broadcasted_iota(jnp.int32, (rows, tokens), 0)
    hot = jnp.concatenate(
        [
            (row == source * capacity + rank[c : c + 1]) & (chosen[c] > 0.5)
            for c in range(2)
        ],
        axis=0,
    )
    scale = jnp.sum(jnp.where(hot, prob, 0.0), axis=1, keepdims=True)
    hot = jnp.where(hot, 1.0, 0.0).astype(jnp.bfloat16)
    routed = (mm(hot, own_dy[...]) * scale).astype(jnp.bfloat16)
    hidden = mm(routed, own_down_ref[...], ((1,), (1,)))
    routed = (mm(hot, other_dy[...]) * scale).astype(jnp.bfloat16)
    hidden += mm(routed, other_down_ref[...], ((1,), (1,)))
    hidden = hidden / math.sqrt(inner)
    for c, (gate_ref, up_ref) in enumerate(
        ((own_gate_ref, own_up_ref), (other_gate_ref, other_up_ref))
    ):
        part = slice(c * rows, (c + 1) * rows)
        gate = gate_ref[...].astype(jnp.float32)
        sigmoid = 1.0 / (1.0 + jnp.exp(-gate))

        @pl.when(rep == 0)
        def _():
            up = up_ref[...].astype(jnp.float32)
            out_ref[part, :] = (
                hidden[part] * up * sigmoid * (1.0 + gate * (1.0 - sigmoid))
            ).astype(jnp.bfloat16)

        @pl.when(rep == 1)
        def _():
            out_ref[part, :] = (hidden[part] * gate * sigmoid).astype(jnp.bfloat16)


def inputs_kernel(rep_ref, own_ref, other_ref, high_ref, low_ref, xt_ref):
    half = xt_ref.shape[0]
    rows = own_ref.shape[0]
    own, other = own_ref[...], other_ref[...]

    def store(first, second, block):
        high = block.astype(jnp.bfloat16)
        high_ref[first, second] = high
        low_ref[first, second] = (block - high.astype(jnp.float32)).astype(jnp.bfloat16)

    begin, end = slice(0, rows), slice(rows, None)
    store(begin, begin, mm(own, own, ((1,), (1,))))
    store(end, end, mm(other, other, ((1,), (1,))))
    cross = mm(own, other, ((1,), (1,)))
    store(begin, end, cross)
    store(end, begin, cross.T)
    start = pl.multiple_of(rep_ref[0] * half, half)
    xt_ref[:, :rows] = own_ref[:, pl.ds(start, half)].T
    xt_ref[:, rows:] = other_ref[:, pl.ds(start, half)].T


def rows_kernel(rep_ref, routed_ref, own_down_ref, other_down_ref, gate_ref, up_ref, *refs):
    own_ref, partner_ref = refs[-2:]
    half = own_down_ref.shape[1]
    inner = own_down_ref.shape[0]
    rep = rep_ref[0]
    first = pl.multiple_of(rep * half, half)
    second = pl.multiple_of((1 - rep) * half, half)
    hidden = mm(routed_ref[:, pl.ds(first, half)], own_down_ref[...], ((1,), (1,)))
    hidden += mm(routed_ref[:, pl.ds(second, half)], other_down_ref[...], ((1,), (1,)))
    hidden = hidden / math.sqrt(inner)
    gate = gate_ref[...].astype(jnp.float32)
    up = up_ref[...].astype(jnp.float32)
    sigmoid = 1.0 / (1.0 + jnp.exp(-gate))
    gate_rows = (hidden * up * sigmoid * (1.0 + gate * (1.0 - sigmoid))).astype(jnp.bfloat16)
    up_rows = (hidden * gate * sigmoid).astype(jnp.bfloat16)

    @pl.when(rep == 0)
    def _():
        own_ref[...] = gate_rows
        partner_ref[...] = up_rows

    @pl.when(rep == 1)
    def _():
        own_ref[...] = up_rows
        partner_ref[...] = gate_rows


def update_rows(factor, me, xt_ref, weight_ref, b_ref, swapped, outs):
    rows = b_ref.shape[0] // 2
    begin, end = slice(0, rows), slice(rows, None)
    first, second = (end, begin) if swapped else (begin, end)
    for d, out in enumerate(outs):
        size = out.shape[0]
        place = pl.ds(pl.multiple_of((me ^ d) * size, size), size)
        x = xt_ref[place, :]
        ortho = mm(x[:, :rows], b_ref[first]) + mm(x[:, rows:], b_ref[second])
        out[...] = (weight_ref[place, :].astype(jnp.float32) - factor * ortho).astype(jnp.bfloat16)


def schulz_kernel(factor, blocks, rep_ref, me_ref, high_ref, low_ref, xt_ref, gate_ref, up_ref, *refs):
    row_refs, b_ref, outs = refs[:blocks], refs[blocks], refs[blocks + 1 : -6]
    r_ref, gram_ref, poly_ref, x_ref, weight_ref, sems = refs[-6:]
    rows = row_refs[0].shape[0]
    rep = rep_ref[0]
    x_copy = pltpu.make_async_copy(xt_ref, x_ref, sems.at[0])
    gate_copy = pltpu.make_async_copy(gate_ref, weight_ref, sems.at[1])
    up_copy = pltpu.make_async_copy(up_ref, weight_ref, sems.at[2])
    x_copy.start()
    pl.when(rep == 0)(gate_copy.start)
    pl.when(rep == 1)(up_copy.start)
    for n, row_ref in enumerate(row_refs):
        r_ref[n * rows : (n + 1) * rows] = row_ref[...]
    size = None
    for repeat in range(ITERS):
        base = r_ref[...]
        mapped = mm(high_ref[...], base) + mm(low_ref[...], base)
        if repeat == 0:
            squares = jnp.sum(base.astype(jnp.float32) * mapped)
            total = jnp.sqrt(jnp.maximum(squares, 0.0)) + epsilon
            size = 1.0 / total
        gram = mm(base, mapped.astype(jnp.bfloat16), ((0,), (0,)))
        if repeat == 0:
            gram = gram * (size * size)
        gram_ref[...] = gram.astype(jnp.bfloat16)
        square = mm(gram_ref[...], gram_ref[...])
        poly_ref[...] = (
            quintic_second * gram_ref[...].astype(jnp.float32) + quintic_third * square
        ).astype(jnp.bfloat16)
        mixed = quintic_first * base.astype(jnp.float32) + mm(base, poly_ref[...])
        if repeat == 0:
            mixed = mixed * size
        if repeat == ITERS - 1:
            b_ref[...] = mixed.astype(jnp.bfloat16)
        else:
            r_ref[...] = mixed.astype(jnp.bfloat16)
    x_copy.wait()
    pl.when(rep == 0)(gate_copy.wait)
    pl.when(rep == 1)(up_copy.wait)
    update_rows(factor, me_ref[0], x_ref, weight_ref, b_ref, False, outs)


def update_kernel(factor, rep_ref, me_ref, xt_ref, gate_ref, up_ref, b_ref, *outs):
    for rep, weight_ref in ((0, up_ref), (1, gate_ref)):

        @pl.when(rep_ref[0] == rep)
        def _():
            update_rows(factor, me_ref[0], xt_ref, weight_ref, b_ref, True, outs)


def route_kernel(line, plane, least, limit, owner_ref, place_ref, pick_ref, last_ref, branch_ref, at, to, slot, right, left):
    items = line * plane
    shift = plane.bit_length() - 1
    mine, me = place_ref[0] >> shift, place_ref[0] & (plane - 1)
    for i in range(items):
        at[i] = i // plane
        to[i] = owner_ref[i] >> shift
        slot[i] = (i % plane) ^ me
    count = jnp.int32(0)
    even = mine & 1 == 0
    for step in range(limit):
        for z in range(line):
            right[z] = -1
            left[z] = -1
        waiting = jnp.int32(0)
        for i in range(items):
            place, target = at[i], to[i]
            key = target * items + items - 1 - i
            right[place] = jnp.maximum(right[place], jnp.where(target > place, key, -1))
            key = (line - 1 - target) * items + items - 1 - i
            left[place] = jnp.maximum(left[place], jnp.where(target < place, key, -1))
            waiting = waiting | (target ^ place)
        count = jnp.where(waiting > 0, step + 1, count)

        def chosen(key):
            return items - 1 - (jnp.maximum(key, 0) & (items - 1))

        go, back = right[mine], left[mine]
        go = jnp.where(go >= 0, slot[chosen(go)], 0)
        back = jnp.where(back >= 0, slot[chosen(back)], 0)
        pick_ref[step] = jnp.where(even, go, back)
        pick_ref[limit + step] = jnp.where(even, back, go)
        for z in range(line):
            for keys, move in ((right, 1), (left, -1)):
                key = keys[z]
                item = chosen(key)
                at[item] = jnp.where(key >= 0, z + move, at[item])
                slot[item] = jnp.where(key >= 0, plane + step, slot[item])
    rest = jnp.int32(0)
    for i in range(items):
        target = to[i]
        rest = rest | (target ^ at[i])

        @pl.when(target == mine)
        def _():
            link = jnp.where(target < i // plane, mine, mine + 1)
            second = (slot[i] >= plane) & (link & 1 == 1)
            last_ref[(owner_ref[i] & (plane - 1)) ^ me] = slot[i] + jnp.where(second, limit, 0)

    branch_ref[0] = jnp.where(rest > 0, 0, jnp.maximum(count - least, 0) + 1)


def route(line, plane, least, limit, owner, place):
    table = lambda n: jax.ShapeDtypeStruct((n,), jnp.int32)
    return pl.pallas_call(
        functools.partial(route_kernel, line, plane, least, limit),
        out_shape=(table(2 * limit), table(plane), table(1)),
        in_specs=[SMEM, SMEM],
        out_specs=(SMEM, SMEM, SMEM),
        scratch_shapes=[pltpu.SMEM((n,), jnp.int32) for n in (line * plane,) * 3 + (line,) * 2],
        compiler_params=pltpu.CompilerParams(vmem_limit_bytes=MIB),
    )(owner, place)


def pick_kernel(entries, groups, table_ref, *refs):
    outs = refs[len(refs) - len(entries) :]
    for entry, group, out in zip(entries, groups, outs):
        for number, index in group:

            @pl.when(table_ref[entry] == number)
            def _():
                def copy(i, carry):
                    place = pl.ds(pl.multiple_of(i * 16, 16), 16)
                    out[place, :] = refs[index][place, :]
                    return carry

                lax.fori_loop(0, out.shape[0] // 16, copy, 0, unroll=1)


def pick(table, blocks, entries, groups, after):
    shape = jax.ShapeDtypeStruct(blocks[0].shape, blocks[0].dtype)
    return call(
        functools.partial(pick_kernel, entries, groups),
        (shape,) * len(entries),
        [SMEM] + [VMEM] * len(blocks) + [ANY] * len(after),
        (table, *blocks, *after),
        0,
        4 * blocks[0].size * len(entries),
        limit=6,
    )


def hold_kernel(*refs):
    pass


def hold(blocks, after):
    return pl.pallas_call(
        hold_kernel,
        out_shape=tuple(jax.ShapeDtypeStruct(b.shape, b.dtype) for b in blocks),
        in_specs=[ANY] * (len(blocks) + 1),
        out_specs=(ANY,) * len(blocks),
        input_output_aliases={i: i for i in range(len(blocks))},
        compiler_params=pltpu.CompilerParams(vmem_limit_bytes=MIB),
    )(*blocks, after)


def assemble_kernel(plane, which, rep_ref, me_ref, *refs):
    pieces, gate_ref, up_ref, sems = refs[:plane], refs[-3], refs[-2], refs[-1]
    size = pieces[0].shape[0]

    def move(out):
        copies = []
        for d, piece in enumerate(pieces):
            start = pl.multiple_of((me_ref[0] ^ d) * size, size)
            copies.append(
                pltpu.make_async_copy(piece, out.at[pl.ds(start, size), :], sems.at[d])
            )
        for copy in copies:
            copy.start()
        for copy in copies:
            copy.wait()

    pl.when(rep_ref[0] == which)(lambda: move(gate_ref))
    pl.when(rep_ref[0] != which)(lambda: move(up_ref))


def assemble(plane, rep, me, own, other):
    rows, columns = own[0].shape
    shape = jax.ShapeDtypeStruct((plane * rows, columns), own[0].dtype)
    matrices = ()
    for which, pieces in enumerate((own, other)):
        matrices = pl.pallas_call(
            functools.partial(assemble_kernel, plane, which),
            out_shape=(shape,) * 2,
            in_specs=[SMEM, SMEM] + [VMEM] * plane + [ANY] * len(matrices),
            out_specs=(ANY,) * 2,
            input_output_aliases={2 + plane + n: n for n in range(len(matrices))},
            scratch_shapes=[pltpu.SemaphoreType.DMA((plane,))],
            compiler_params=pltpu.CompilerParams(vmem_limit_bytes=4 * MIB),
            cost_estimate=pl.CostEstimate(
                flops=0, bytes_accessed=4 * plane * rows * columns, transcendentals=0
            ),
        )(rep, me, *pieces, *matrices)
    return matrices


def across(block, d, items):
    return block if d == 0 else lax.ppermute(block, "ep", [(i, i ^ d) for i in range(items)])


def direct(steps, limit, line, plane, rep, me, owner, pick_table, last_table, spread, own, other):
    items = line * plane

    def along(block, stream):
        pairs = []
        for z in range(stream, line - 1, 2):
            for i in range(z * plane, (z + 1) * plane):
                pairs += [(i, i + plane), (i + plane, i)]
        return lax.ppermute(block, "ep", pairs)

    groups = (own, other)
    chunks = [spread]
    came = [([], []) for _ in groups]
    base = [(s, s) for s in range(plane)]
    order = sorted((1.5 * c + step, c, step) for c in range(len(groups)) for step in range(steps + 1))
    after = ()
    waits = {}
    collected = [None] * len(groups)
    for position, (_, c, step) in enumerate(order):
        first, second = came[c]
        after += waits.pop(position, ())
        if step == steps:
            from_first = [(plane + s, plane + s) for s in range(steps)]
            from_second = [(plane + limit + s, plane + steps + s) for s in range(steps)]
            found = pick(
                last_table,
                (*chunks[c], *first, *second),
                tuple(range(plane)),
                (base + from_first + from_second,) * plane,
                after,
            )
            after = found[:1]
            if c + 1 == len(groups):
                collected[c] = found
                continue
            collected[c] = [across(block, d, items) for d, block in enumerate(found)]
            waits[position + 2] = tuple(collected[c][1:])
            continue
        from_first = [(plane + s, plane + s) for s in range(step)]
        from_second = [(plane + s, plane + step + s) for s in range(step)]
        sent = pick(
            pick_table,
            (*chunks[c], *first, *second),
            (step, limit + step),
            (base + from_second, base + from_first),
            after,
        )
        after = sent[:1]
        if step == 0 and c + 1 < len(groups):
            chunks.append(
                [
                    across(block, d, items)
                    for d, block in enumerate(hold(groups[c + 1], sent[0]))
                ]
            )
        first.append(along(sent[0], 0))
        second.append(along(sent[1], 1))
    return tuple(piece for chunk in collected for piece in chunk)


def indirect(experts, plane, rep, me, owner, own, other):
    order = jnp.arange(experts, dtype=jnp.int32)
    source = jnp.sum(
        jnp.where(owner[None, :] == order[:, None], order[None, :], 0), axis=1, dtype=jnp.int32
    )
    matrices = assemble(plane, rep, me, own, other)
    results = [exchange(m.reshape(experts, -1, m.shape[1])) for m in matrices]
    results = [exchange(arrange(spread, source)) for spread in results]
    return tuple(result.reshape(-1, result.shape[2]) for result in results)


def cut(plane, rep, me, matrices):
    size = matrices[0].shape[0] // plane
    gate, up = matrices
    return tuple(
        lax.dynamic_slice_in_dim(matrix, (me[0] ^ d) * size, size)
        for matrix in (jnp.where(rep[0] == 0, gate, up), jnp.where(rep[0] == 0, up, gate))
        for d in range(plane)
    )


def arrange_kernel(index_ref, in_ref, out_ref):
    for i in range(in_ref.shape[0]):
        out_ref[i] = in_ref[index_ref[i]]


def arrange(blocks, index):
    return call(
        arrange_kernel,
        jax.ShapeDtypeStruct(blocks.shape, blocks.dtype),
        [SMEM, VMEM],
        (index, blocks),
        0,
        4 * blocks.size,
        limit=8,
    )


def exchange(blocks):
    return lax.all_to_all(blocks, "ep", split_axis=0, concat_axis=0, tiled=True)


def shards(
    dy,
    probs,
    expert_ids,
    copy_choice,
    saved_inputs,
    saved_gate,
    saved_up,
    down_weight,
    gate_weight,
    up_weight,
    new_owner,
):
    experts = lax.axis_size("ep")
    capacity = saved_inputs.shape[3]
    width = dy.shape[1]
    inner = saved_gate.shape[4]
    half = width // 2
    rows = experts * capacity
    bf16 = jnp.bfloat16
    shape = lambda *dims: jax.ShapeDtypeStruct(dims, bf16)
    rep = lax.axis_index("rep").astype(jnp.int32).reshape(1)

    plane = 1
    while 4 * plane * plane <= experts:
        plane *= 2
    line = experts // plane
    place = lax.axis_index("ep").astype(jnp.int32)
    me = (place & (plane - 1)).reshape(1)
    least, limit = plane - 1, plane + 2
    inputs = saved_inputs.reshape(rows, width)
    down = down_weight[0]
    other_inputs = from_partner(inputs)
    other_down = from_partner(down)
    high, low, transposed = call(
        inputs_kernel,
        (shape(2 * rows, 2 * rows), shape(2 * rows, 2 * rows), shape(half, 2 * rows)),
        [SMEM, VMEM, VMEM],
        (rep, inputs, other_inputs),
        2 * 3 * rows * rows * width,
        8 * rows * width,
    )
    gate_rows = saved_gate.reshape(rows, inner)
    up_rows = saved_up.reshape(rows, inner)
    if line == plane:
        pick_table, last_table, branch = route(
            line, plane, least, limit, new_owner, place.reshape(1)
        )
        tokens, top = expert_ids.shape
        choice = jnp.concatenate(
            [expert_ids.T.astype(jnp.float32), copy_choice.T.astype(jnp.float32), probs.T]
        )
        packed = call(
            pack_kernel,
            shape(tokens, half + 128),
            [SMEM, VMEM, VMEM],
            (rep, choice, dy),
            0,
            4 * tokens * width,
            scratch=(pltpu.VMEM((128, 128), jnp.float32),),
            limit=2,
        )
        along = lambda q: [
            (z * plane + i, (z ^ q) * plane + i) for z in range(line) for i in range(plane)
        ]
        column = join(
            [packed] + [lax.ppermute(packed, "ep", along(q)) for q in range(1, line)],
            (high,),
        )
        own_tokens = [column] + [
            lax.ppermute(column, "ep", [(i, i ^ d) for i in range(experts)])
            for d in range(1, plane)
        ]
        own_tokens[-1] = hold(own_tokens[-1:], pick_table)[0]
        other_tokens = [from_partner(block) for block in own_tokens]
        row_blocks = (
            call(
                functools.partial(gather_kernel, capacity, line, plane, top),
                shape(2 * rows, inner),
                [SMEM, SMEM] + [VMEM] * (6 + 2 * plane),
                (
                    rep,
                    place.reshape(1),
                    down,
                    other_down,
                    gate_rows,
                    up_rows,
                    from_partner(gate_rows),
                    from_partner(up_rows),
                    *own_tokens,
                    *other_tokens,
                ),
                2 * 2 * rows * width * (inner + experts * tokens),
                8 * rows * width,
                scratch=(
                    pltpu.VMEM((experts * tokens, half), bf16),
                    pltpu.VMEM((experts * tokens, half), bf16),
                    pltpu.VMEM((128, experts * tokens), jnp.float32),
                ),
                limit=24,
            ),
        )
    else:
        outgoing = pl.pallas_call(
            functools.partial(dispatch_kernel, capacity),
            out_shape=shape(rows, width),
            grid=(1,),
            in_specs=[SMEM]
            + [pl.BlockSpec(a.shape, lambda i: (0, 0)) for a in (expert_ids.T, copy_choice.T, probs.T, dy)],
            out_specs=pl.BlockSpec((rows, width), lambda i: (0, 0)),
            compiler_params=pltpu.CompilerParams(vmem_limit_bytes=8 * MIB),
        )(rep, expert_ids.T, copy_choice.T, probs.T, dy)
        routed = exchange(outgoing.reshape(experts, capacity, width)).reshape(rows, width)

        own_rows, partner_rows = call(
            rows_kernel,
            (shape(rows, inner), shape(rows, inner)),
            [SMEM] + [VMEM] * 5 + [ANY],
            (
                rep,
                routed,
                down,
                other_down,
                gate_rows,
                up_rows,
                high,
            ),
            2 * rows * width * inner,
            2 * inner * width,
        )
        row_blocks = (own_rows, from_partner(partner_rows))
    factor = step_scale * math.sqrt(width)
    size = half // plane
    gate, up = gate_weight[0], up_weight[0]
    own_b, *own = call(
        functools.partial(schulz_kernel, factor, len(row_blocks)),
        (shape(2 * rows, inner),) + (shape(size, inner),) * plane,
        [SMEM, SMEM, VMEM, VMEM, ANY, ANY, ANY] + [VMEM] * len(row_blocks),
        (rep, me, high, low, transposed, gate, up, *row_blocks),
        ITERS * 2 * inner * inner * (inner + 6 * rows) + 2 * half * 2 * rows * inner,
        8 * rows * inner,
        scratch=(
            pltpu.VMEM((2 * rows, inner), bf16),
            pltpu.VMEM((inner, inner), bf16),
            pltpu.VMEM((inner, inner), bf16),
            pltpu.VMEM((half, 2 * rows), bf16),
            pltpu.VMEM((half, inner), bf16),
            pltpu.SemaphoreType.DMA((3,)),
        ),
        limit=22,
    )
    other = call(
        functools.partial(update_kernel, factor),
        (shape(size, inner),) * plane,
        [SMEM, SMEM] + [VMEM] * 4,
        (rep, me, transposed, gate, up, from_partner(own_b)),
        2 * half * 2 * rows * inner,
        8 * half * inner,
    )
    if line == plane:
        spread = [across(block, d, experts) for d, block in enumerate(own)]

        def otherwise(rep, me, owner, pick_table, last_table, spread, own, other):
            pieces = cut(plane, rep, me, indirect(experts, plane, rep, me, owner, own, other))
            back = [across(block, d, experts) for d, block in enumerate(pieces[plane:])]
            return (*pieces[:plane], *back)

        branches = [
            functools.partial(direct, steps, limit, line, plane)
            for steps in range(least, limit + 1)
        ]
        pieces = lax.switch(
            branch[0],
            [otherwise] + branches,
            rep,
            me,
            new_owner,
            pick_table,
            last_table,
            spread,
            own,
            other,
        )
        other = [across(block, d, experts) for d, block in enumerate(pieces[plane:])]
        gate, up = assemble(plane, rep, me, pieces[:plane], other)
    else:
        gate, up = indirect(experts, plane, rep, me, new_owner, own, other)
    return (gate[None], up[None])


def solution(mesh):
    in_specs = (
        P("ep", None),
        P("ep", None),
        P("ep", None),
        P("ep", None),
        P("ep", "rep", None, None, None),
        P("ep", "rep", None, None, None),
        P("ep", "rep", None, None, None),
        P("ep", None, "rep"),
        P("ep", "rep", None),
        P("ep", "rep", None),
        P(),
    )
    out_specs = (P("ep", "rep", None), P("ep", "rep", None))
    return jax.shard_map(shards, mesh=mesh, in_specs=in_specs, out_specs=out_specs, check_vma=False)
```

```python
import functools
import math

import jax
import jax.numpy as jnp
from jax import lax
from jax.experimental import pallas as pl
from jax.experimental.pallas import tpu as pltpu
from jax.sharding import PartitionSpec as P

ITERS = 2

quintic_first = 3.4445
quintic_second = -4.775
quintic_third = 2.0315
step_scale = 2.0
epsilon = 1e-07

VMEM = pl.BlockSpec(memory_space=pltpu.VMEM)
SMEM = pl.BlockSpec(memory_space=pltpu.SMEM)
ANY = pl.BlockSpec(memory_space=pl.ANY)
MIB = 1 << 20


def from_partner(block):
    return lax.ppermute(block, "rep", [(0, 1), (1, 0)])


def mm(left, right, dims=((1,), (0,))):
    return lax.dot_general(left, right, (dims, ((), ())), preferred_element_type=jnp.float32)


def call(kernel, outs, in_specs, args, flops, nbytes, scratch=(), limit=16):
    return pl.pallas_call(
        kernel,
        out_shape=outs,
        in_specs=in_specs,
        out_specs=jax.tree.map(lambda _: VMEM, outs),
        scratch_shapes=list(scratch),
        compiler_params=pltpu.CompilerParams(vmem_limit_bytes=limit * MIB),
        cost_estimate=pl.CostEstimate(flops=flops, bytes_accessed=nbytes, transcendentals=0),
    )(*args)


def dispatch_kernel(capacity, rep_ref, ids_ref, copy_ref, probs_ref, dy_ref, out_ref):
    rows, tokens = out_ref.shape[0], dy_ref.shape[0]
    own = rep_ref[0]
    expert = lax.broadcasted_iota(jnp.int32, (rows, tokens), 0) // capacity
    slot = lax.broadcasted_iota(jnp.int32, (rows, tokens), 0) % capacity
    mask = jnp.zeros((rows, tokens), jnp.float32)
    weight = jnp.zeros((rows, tokens), jnp.float32)
    for k in range(ids_ref.shape[0]):
        here = (ids_ref[k : k + 1, :] == expert) & (copy_ref[k : k + 1, :] == own)
        mask = jnp.where(here, 1.0, mask)
        weight = jnp.where(here, probs_ref[k : k + 1, :], weight)
    before = lax.broadcasted_iota(jnp.int32, (tokens, tokens), 0) < lax.broadcasted_iota(
        jnp.int32, (tokens, tokens), 1
    )
    rank = mm(mask.astype(jnp.bfloat16), jnp.where(before, 1.0, 0.0).astype(jnp.bfloat16))
    hot = (mask > 0.5) & (rank.astype(jnp.int32) == slot)
    scale = jnp.sum(jnp.where(hot, weight, 0.0), axis=1, keepdims=True)
    picked = mm(jnp.where(hot, 1.0, 0.0).astype(jnp.bfloat16), dy_ref[...])
    out_ref[...] = (picked * scale).astype(jnp.bfloat16)


def pack_kernel(rep_ref, choice_ref, dy_ref, out_ref, table):
    top, half = choice_ref.shape[0] // 3, dy_ref.shape[1] // 2
    tokens = dy_ref.shape[0]
    out_ref[:, :half] = dy_ref[:, pl.ds(pl.multiple_of(rep_ref[0] * half, half), half)]
    table[...] = jnp.zeros_like(table)
    table[: 2 * top, :tokens] = choice_ref[: 2 * top, :]
    rest = choice_ref[2 * top :, :]
    for part in range(3):
        rounded = rest.astype(jnp.bfloat16).astype(jnp.float32)
        table[(2 + part) * top : (3 + part) * top, :tokens] = rounded
        rest = rest - rounded
    out_ref[:, half:] = table[...].T[:tokens].astype(jnp.bfloat16)


def join_kernel(*refs):
    out_ref = refs[-1]
    rows = refs[0].shape[0]
    for n in range(out_ref.shape[0] // rows):
        out_ref[n * rows : (n + 1) * rows, :] = refs[n][...]


def join(blocks, after):
    rows, columns = blocks[0].shape
    return call(
        join_kernel,
        jax.ShapeDtypeStruct((len(blocks) * rows, columns), blocks[0].dtype),
        [VMEM] * len(blocks) + [ANY] * len(after),
        (*blocks, *after),
        0,
        4 * len(blocks) * rows * columns,
        limit=2,
    )


def gather_kernel(
    capacity,
    line,
    plane,
    top,
    rep_ref,
    place_ref,
    own_down_ref,
    other_down_ref,
    own_gate_ref,
    own_up_ref,
    other_gate_ref,
    other_up_ref,
    *refs,
):
    own_refs, other_refs = refs[:plane], refs[plane : 2 * plane]
    out_ref, own_dy, other_dy, table = refs[-4:]
    half, inner = own_down_ref.shape[1], own_down_ref.shape[0]
    block = own_refs[0].shape[0]
    tokens = block * plane
    rows = out_ref.shape[0] // 2
    per = block // line
    rep, place = rep_ref[0], place_ref[0]
    mine, me = place // plane, place % plane
    for d in range(plane):
        own_dy[d * block : (d + 1) * block, :] = own_refs[d][:, :half]
        other_dy[d * block : (d + 1) * block, :] = other_refs[d][:, :half]
        table[:, d * block : (d + 1) * block] = own_refs[d][:, half:].astype(jnp.float32).T
    ids = table[:top, :]
    copies = table[top : 2 * top, :]
    probs = table[2 * top : 3 * top, :] + table[3 * top : 4 * top, :] + table[4 * top : 5 * top, :]
    here = ids == place.astype(jnp.float32)
    prob = jnp.sum(jnp.where(here, probs, 0.0), axis=0, keepdims=True)
    chosen = [
        jnp.sum(
            jnp.where(here & (copies == copy.astype(jnp.float32)), 1.0, 0.0), axis=0, keepdims=True
        )
        for copy in (rep, 1 - rep)
    ]
    first = lax.broadcasted_iota(jnp.int32, (tokens, tokens), 0)
    second = lax.broadcasted_iota(jnp.int32, (tokens, tokens), 1)
    before = jnp.where((first // per == second // per) & (first < second), 1.0, 0.0)
    both = jnp.concatenate(chosen + [jnp.zeros((6, tokens), jnp.float32)], axis=0)
    rank = mm(both.astype(jnp.bfloat16), before.astype(jnp.bfloat16)).astype(jnp.int32)
    number = lax.broadcasted_iota(jnp.int32, (1, tokens), 1) // per
    source = ((number % line) ^ mine) * plane + ((number // line) ^ me)
    row = lax.broadcasted_iota(jnp.int32, (rows, tokens), 0)
    hot = jnp.concatenate(
        [
            (row == source * capacity + rank[c : c + 1]) & (chosen[c] > 0.5)
            for c in range(2)
        ],
        axis=0,
    )
    scale = jnp.sum(jnp.where(hot, prob, 0.0), axis=1, keepdims=True)
    hot = jnp.where(hot, 1.0, 0.0).astype(jnp.bfloat16)
    routed = (mm(hot, own_dy[...]) * scale).astype(jnp.bfloat16)
    hidden = mm(routed, own_down_ref[...], ((1,), (1,)))
    routed = (mm(hot, other_dy[...]) * scale).astype(jnp.bfloat16)
    hidden += mm(routed, other_down_ref[...], ((1,), (1,)))
    hidden = hidden / math.sqrt(inner)
    for c, (gate_ref, up_ref) in enumerate(
        ((own_gate_ref, own_up_ref), (other_gate_ref, other_up_ref))
    ):
        part = slice(c * rows, (c + 1) * rows)
        gate = gate_ref[...].astype(jnp.float32)
        sigmoid = 1.0 / (1.0 + jnp.exp(-gate))

        @pl.when(rep == 0)
        def _():
            up = up_ref[...].astype(jnp.float32)
            out_ref[part, :] = (
                hidden[part] * up * sigmoid * (1.0 + gate * (1.0 - sigmoid))
            ).astype(jnp.bfloat16)

        @pl.when(rep == 1)
        def _():
            out_ref[part, :] = (hidden[part] * gate * sigmoid).astype(jnp.bfloat16)


def inputs_kernel(rep_ref, own_ref, other_ref, high_ref, low_ref, xt_ref):
    half = xt_ref.shape[0]
    rows = own_ref.shape[0]
    own, other = own_ref[...], other_ref[...]

    def store(first, second, block):
        high = block.astype(jnp.bfloat16)
        high_ref[first, second] = high
        low_ref[first, second] = (block - high.astype(jnp.float32)).astype(jnp.bfloat16)

    begin, end = slice(0, rows), slice(rows, None)
    store(begin, begin, mm(own, own, ((1,), (1,))))
    store(end, end, mm(other, other, ((1,), (1,))))
    cross = mm(own, other, ((1,), (1,)))
    store(begin, end, cross)
    store(end, begin, cross.T)
    start = pl.multiple_of(rep_ref[0] * half, half)
    xt_ref[:, :rows] = own_ref[:, pl.ds(start, half)].T
    xt_ref[:, rows:] = other_ref[:, pl.ds(start, half)].T


def rows_kernel(rep_ref, routed_ref, own_down_ref, other_down_ref, gate_ref, up_ref, *refs):
    own_ref, partner_ref = refs[-2:]
    half = own_down_ref.shape[1]
    inner = own_down_ref.shape[0]
    rep = rep_ref[0]
    first = pl.multiple_of(rep * half, half)
    second = pl.multiple_of((1 - rep) * half, half)
    hidden = mm(routed_ref[:, pl.ds(first, half)], own_down_ref[...], ((1,), (1,)))
    hidden += mm(routed_ref[:, pl.ds(second, half)], other_down_ref[...], ((1,), (1,)))
    hidden = hidden / math.sqrt(inner)
    gate = gate_ref[...].astype(jnp.float32)
    up = up_ref[...].astype(jnp.float32)
    sigmoid = 1.0 / (1.0 + jnp.exp(-gate))
    gate_rows = (hidden * up * sigmoid * (1.0 + gate * (1.0 - sigmoid))).astype(jnp.bfloat16)
    up_rows = (hidden * gate * sigmoid).astype(jnp.bfloat16)

    @pl.when(rep == 0)
    def _():
        own_ref[...] = gate_rows
        partner_ref[...] = up_rows

    @pl.when(rep == 1)
    def _():
        own_ref[...] = up_rows
        partner_ref[...] = gate_rows


def update_rows(factor, me, xt_ref, weight_ref, b_ref, swapped, outs):
    rows = b_ref.shape[0] // 2
    begin, end = slice(0, rows), slice(rows, None)
    first, second = (end, begin) if swapped else (begin, end)
    for d, out in enumerate(outs):
        size = out.shape[0]
        place = pl.ds(pl.multiple_of((me ^ d) * size, size), size)
        x = xt_ref[place, :]
        ortho = mm(x[:, :rows], b_ref[first]) + mm(x[:, rows:], b_ref[second])
        out[...] = (weight_ref[place, :].astype(jnp.float32) - factor * ortho).astype(jnp.bfloat16)


def schulz_kernel(factor, blocks, rep_ref, me_ref, high_ref, low_ref, xt_ref, gate_ref, up_ref, *refs):
    row_refs, b_ref, outs = refs[:blocks], refs[blocks], refs[blocks + 1 : -6]
    r_ref, gram_ref, poly_ref, x_ref, weight_ref, sems = refs[-6:]
    rows = row_refs[0].shape[0]
    rep = rep_ref[0]
    x_copy = pltpu.make_async_copy(xt_ref, x_ref, sems.at[0])
    gate_copy = pltpu.make_async_copy(gate_ref, weight_ref, sems.at[1])
    up_copy = pltpu.make_async_copy(up_ref, weight_ref, sems.at[2])
    x_copy.start()
    pl.when(rep == 0)(gate_copy.start)
    pl.when(rep == 1)(up_copy.start)
    for n, row_ref in enumerate(row_refs):
        r_ref[n * rows : (n + 1) * rows] = row_ref[...]
    size = None
    for repeat in range(ITERS):
        base = r_ref[...]
        mapped = mm(high_ref[...], base) + mm(low_ref[...], base)
        if repeat == 0:
            squares = jnp.sum(base.astype(jnp.float32) * mapped)
            total = jnp.sqrt(jnp.maximum(squares, 0.0)) + epsilon
            size = 1.0 / total
        gram = mm(base, mapped.astype(jnp.bfloat16), ((0,), (0,)))
        if repeat == 0:
            gram = gram * (size * size)
        gram_ref[...] = gram.astype(jnp.bfloat16)
        square = mm(gram_ref[...], gram_ref[...])
        poly_ref[...] = (
            quintic_second * gram_ref[...].astype(jnp.float32) + quintic_third * square
        ).astype(jnp.bfloat16)
        mixed = quintic_first * base.astype(jnp.float32) + mm(base, poly_ref[...])
        if repeat == 0:
            mixed = mixed * size
        if repeat == ITERS - 1:
            b_ref[...] = mixed.astype(jnp.bfloat16)
        else:
            r_ref[...] = mixed.astype(jnp.bfloat16)
    x_copy.wait()
    pl.when(rep == 0)(gate_copy.wait)
    pl.when(rep == 1)(up_copy.wait)
    update_rows(factor, me_ref[0], x_ref, weight_ref, b_ref, False, outs)


def update_kernel(factor, rep_ref, me_ref, xt_ref, gate_ref, up_ref, b_ref, *outs):
    for rep, weight_ref in ((0, up_ref), (1, gate_ref)):

        @pl.when(rep_ref[0] == rep)
        def _():
            update_rows(factor, me_ref[0], xt_ref, weight_ref, b_ref, True, outs)


def route_kernel(line, plane, least, limit, owner_ref, place_ref, pick_ref, last_ref, branch_ref, at, to, slot, right, left):
    items = line * plane
    shift = plane.bit_length() - 1
    mine, me = place_ref[0] >> shift, place_ref[0] & (plane - 1)
    for i in range(items):
        at[i] = i // plane
        to[i] = owner_ref[i] >> shift
        slot[i] = (i % plane) ^ me
    count = jnp.int32(0)
    even = mine & 1 == 0
    for step in range(limit):
        for z in range(line):
            right[z] = -1
            left[z] = -1
        waiting = jnp.int32(0)
        for i in range(items):
            place, target = at[i], to[i]
            key = target * items + items - 1 - i
            right[place] = jnp.maximum(right[place], jnp.where(target > place, key, -1))
            key = (line - 1 - target) * items + items - 1 - i
            left[place] = jnp.maximum(left[place], jnp.where(target < place, key, -1))
            waiting = waiting | (target ^ place)
        count = jnp.where(waiting > 0, step + 1, count)

        def chosen(key):
            return items - 1 - (jnp.maximum(key, 0) & (items - 1))

        go, back = right[mine], left[mine]
        go = jnp.where(go >= 0, slot[chosen(go)], 0)
        back = jnp.where(back >= 0, slot[chosen(back)], 0)
        pick_ref[step] = jnp.where(even, go, back)
        pick_ref[limit + step] = jnp.where(even, back, go)
        for z in range(line):
            for keys, move in ((right, 1), (left, -1)):
                key = keys[z]
                item = chosen(key)
                at[item] = jnp.where(key >= 0, z + move, at[item])
                slot[item] = jnp.where(key >= 0, plane + step, slot[item])
    rest = jnp.int32(0)
    for i in range(items):
        target = to[i]
        rest = rest | (target ^ at[i])

        @pl.when(target == mine)
        def _():
            link = jnp.where(target < i // plane, mine, mine + 1)
            second = (slot[i] >= plane) & (link & 1 == 1)
            last_ref[(owner_ref[i] & (plane - 1)) ^ me] = slot[i] + jnp.where(second, limit, 0)

    branch_ref[0] = jnp.where(rest > 0, 0, jnp.maximum(count - least, 0) + 1)


def route(line, plane, least, limit, owner, place):
    table = lambda n: jax.ShapeDtypeStruct((n,), jnp.int32)
    return pl.pallas_call(
        functools.partial(route_kernel, line, plane, least, limit),
        out_shape=(table(2 * limit), table(plane), table(1)),
        in_specs=[SMEM, SMEM],
        out_specs=(SMEM, SMEM, SMEM),
        scratch_shapes=[pltpu.SMEM((n,), jnp.int32) for n in (line * plane,) * 3 + (line,) * 2],
        compiler_params=pltpu.CompilerParams(vmem_limit_bytes=MIB),
    )(owner, place)


def pick_kernel(entries, groups, table_ref, *refs):
    outs = refs[len(refs) - len(entries) :]
    for entry, group, out in zip(entries, groups, outs):
        for number, index in group:

            @pl.when(table_ref[entry] == number)
            def _():
                def copy(i, carry):
                    place = pl.ds(pl.multiple_of(i * 16, 16), 16)
                    out[place, :] = refs[index][place, :]
                    return carry

                lax.fori_loop(0, out.shape[0] // 16, copy, 0, unroll=1)


def pick(table, blocks, entries, groups, after):
    shape = jax.ShapeDtypeStruct(blocks[0].shape, blocks[0].dtype)
    return call(
        functools.partial(pick_kernel, entries, groups),
        (shape,) * len(entries),
        [SMEM] + [VMEM] * len(blocks) + [ANY] * len(after),
        (table, *blocks, *after),
        0,
        4 * blocks[0].size * len(entries),
        limit=6,
    )


def hold_kernel(*refs):
    pass


def hold(blocks, after):
    return pl.pallas_call(
        hold_kernel,
        out_shape=tuple(jax.ShapeDtypeStruct(b.shape, b.dtype) for b in blocks),
        in_specs=[ANY] * (len(blocks) + 1),
        out_specs=(ANY,) * len(blocks),
        input_output_aliases={i: i for i in range(len(blocks))},
        compiler_params=pltpu.CompilerParams(vmem_limit_bytes=MIB),
    )(*blocks, after)


def assemble_kernel(plane, which, rep_ref, me_ref, *refs):
    pieces, gate_ref, up_ref, sems = refs[:plane], refs[-3], refs[-2], refs[-1]
    size = pieces[0].shape[0]

    def move(out):
        copies = []
        for d, piece in enumerate(pieces):
            start = pl.multiple_of((me_ref[0] ^ d) * size, size)
            copies.append(
                pltpu.make_async_copy(piece, out.at[pl.ds(start, size), :], sems.at[d])
            )
        for copy in copies:
            copy.start()
        for copy in copies:
            copy.wait()

    pl.when(rep_ref[0] == which)(lambda: move(gate_ref))
    pl.when(rep_ref[0] != which)(lambda: move(up_ref))


def assemble(plane, rep, me, own, other):
    rows, columns = own[0].shape
    shape = jax.ShapeDtypeStruct((plane * rows, columns), own[0].dtype)
    matrices = ()
    for which, pieces in enumerate((own, other)):
        matrices = pl.pallas_call(
            functools.partial(assemble_kernel, plane, which),
            out_shape=(shape,) * 2,
            in_specs=[SMEM, SMEM] + [VMEM] * plane + [ANY] * len(matrices),
            out_specs=(ANY,) * 2,
            input_output_aliases={2 + plane + n: n for n in range(len(matrices))},
            scratch_shapes=[pltpu.SemaphoreType.DMA((plane,))],
            compiler_params=pltpu.CompilerParams(vmem_limit_bytes=4 * MIB),
            cost_estimate=pl.CostEstimate(
                flops=0, bytes_accessed=4 * plane * rows * columns, transcendentals=0
            ),
        )(rep, me, *pieces, *matrices)
    return matrices


def across(block, d, items):
    return block if d == 0 else lax.ppermute(block, "ep", [(i, i ^ d) for i in range(items)])


def direct(steps, limit, line, plane, rep, me, owner, pick_table, last_table, spread, own, other):
    items = line * plane

    def along(block, stream):
        pairs = []
        for z in range(stream, line - 1, 2):
            for i in range(z * plane, (z + 1) * plane):
                pairs += [(i, i + plane), (i + plane, i)]
        return lax.ppermute(block, "ep", pairs)

    groups = (own, other)
    chunks = [spread]
    came = [([], []) for _ in groups]
    base = [(s, s) for s in range(plane)]
    order = sorted((1.5 * c + step, c, step) for c in range(len(groups)) for step in range(steps + 1))
    after = ()
    waits = {}
    collected = [None] * len(groups)
    for position, (_, c, step) in enumerate(order):
        first, second = came[c]
        after += waits.pop(position, ())
        if step == steps:
            from_first = [(plane + s, plane + s) for s in range(steps)]
            from_second = [(plane + limit + s, plane + steps + s) for s in range(steps)]
            found = pick(
                last_table,
                (*chunks[c], *first, *second),
                tuple(range(plane)),
                (base + from_first + from_second,) * plane,
                after,
            )
            after = found[:1]
            if c + 1 == len(groups):
                collected[c] = found
                continue
            collected[c] = [across(block, d, items) for d, block in enumerate(found)]
            waits[position + 2] = tuple(collected[c][1:])
            continue
        from_first = [(plane + s, plane + s) for s in range(step)]
        from_second = [(plane + s, plane + step + s) for s in range(step)]
        sent = pick(
            pick_table,
            (*chunks[c], *first, *second),
            (step, limit + step),
            (base + from_second, base + from_first),
            after,
        )
        after = sent[:1]
        if step == 0 and c + 1 < len(groups):
            chunks.append(
                [
                    across(block, d, items)
                    for d, block in enumerate(hold(groups[c + 1], sent[0]))
                ]
            )
        first.append(along(sent[0], 0))
        second.append(along(sent[1], 1))
    return tuple(piece for chunk in collected for piece in chunk)


def indirect(experts, plane, rep, me, owner, own, other):
    order = jnp.arange(experts, dtype=jnp.int32)
    source = jnp.sum(
        jnp.where(owner[None, :] == order[:, None], order[None, :], 0), axis=1, dtype=jnp.int32
    )
    matrices = assemble(plane, rep, me, own, other)
    results = [exchange(m.reshape(experts, -1, m.shape[1])) for m in matrices]
    results = [exchange(arrange(spread, source)) for spread in results]
    return tuple(result.reshape(-1, result.shape[2]) for result in results)


def cut(plane, rep, me, matrices):
    size = matrices[0].shape[0] // plane
    gate, up = matrices
    return tuple(
        lax.dynamic_slice_in_dim(matrix, (me[0] ^ d) * size, size)
        for matrix in (jnp.where(rep[0] == 0, gate, up), jnp.where(rep[0] == 0, up, gate))
        for d in range(plane)
    )


def arrange_kernel(index_ref, in_ref, out_ref):
    for i in range(in_ref.shape[0]):
        out_ref[i] = in_ref[index_ref[i]]


def arrange(blocks, index):
    return call(
        arrange_kernel,
        jax.ShapeDtypeStruct(blocks.shape, blocks.dtype),
        [SMEM, VMEM],
        (index, blocks),
        0,
        4 * blocks.size,
        limit=8,
    )


def exchange(blocks):
    return lax.all_to_all(blocks, "ep", split_axis=0, concat_axis=0, tiled=True)


def shards(
    dy,
    probs,
    expert_ids,
    copy_choice,
    saved_inputs,
    saved_gate,
    saved_up,
    down_weight,
    gate_weight,
    up_weight,
    new_owner,
):
    experts = lax.axis_size("ep")
    capacity = saved_inputs.shape[3]
    width = dy.shape[1]
    inner = saved_gate.shape[4]
    half = width // 2
    rows = experts * capacity
    bf16 = jnp.bfloat16
    shape = lambda *dims: jax.ShapeDtypeStruct(dims, bf16)
    rep = lax.axis_index("rep").astype(jnp.int32).reshape(1)

    plane = 1
    while 4 * plane * plane <= experts:
        plane *= 2
    line = experts // plane
    place = lax.axis_index("ep").astype(jnp.int32)
    me = (place & (plane - 1)).reshape(1)
    least, limit = plane - 1, plane + 2
    inputs = saved_inputs.reshape(rows, width)
    down = down_weight[0]
    other_inputs = from_partner(inputs)
    other_down = from_partner(down)
    high, low, transposed = call(
        inputs_kernel,
        (shape(2 * rows, 2 * rows), shape(2 * rows, 2 * rows), shape(half, 2 * rows)),
        [SMEM, VMEM, VMEM],
        (rep, inputs, other_inputs),
        2 * 3 * rows * rows * width,
        8 * rows * width,
    )
    gate_rows = saved_gate.reshape(rows, inner)
    up_rows = saved_up.reshape(rows, inner)
    if line == plane:
        pick_table, last_table, branch = route(
            line, plane, least, limit, new_owner, place.reshape(1)
        )
        tokens, top = expert_ids.shape
        choice = jnp.concatenate(
            [expert_ids.T.astype(jnp.float32), copy_choice.T.astype(jnp.float32), probs.T]
        )
        packed = call(
            pack_kernel,
            shape(tokens, half + 128),
            [SMEM, VMEM, VMEM],
            (rep, choice, dy),
            0,
            4 * tokens * width,
            scratch=(pltpu.VMEM((128, 128), jnp.float32),),
            limit=2,
        )
        along = lambda q: [
            (z * plane + i, (z ^ q) * plane + i) for z in range(line) for i in range(plane)
        ]
        column = join(
            [packed] + [lax.ppermute(packed, "ep", along(q)) for q in range(1, line)],
            (high,),
        )
        own_tokens = [column] + [
            lax.ppermute(column, "ep", [(i, i ^ d) for i in range(experts)])
            for d in range(1, plane)
        ]
        own_tokens[1] = hold(own_tokens[1:2], pick_table)[0]
        other_tokens = [from_partner(block) for block in own_tokens]
        row_blocks = (
            call(
                functools.partial(gather_kernel, capacity, line, plane, top),
                shape(2 * rows, inner),
                [SMEM, SMEM] + [VMEM] * (6 + 2 * plane),
                (
                    rep,
                    place.reshape(1),
                    down,
                    other_down,
                    gate_rows,
                    up_rows,
                    from_partner(gate_rows),
                    from_partner(up_rows),
                    *own_tokens,
                    *other_tokens,
                ),
                2 * 2 * rows * width * (inner + experts * tokens),
                8 * rows * width,
                scratch=(
                    pltpu.VMEM((experts * tokens, half), bf16),
                    pltpu.VMEM((experts * tokens, half), bf16),
                    pltpu.VMEM((128, experts * tokens), jnp.float32),
                ),
                limit=24,
            ),
        )
    else:
        outgoing = pl.pallas_call(
            functools.partial(dispatch_kernel, capacity),
            out_shape=shape(rows, width),
            grid=(1,),
            in_specs=[SMEM]
            + [pl.BlockSpec(a.shape, lambda i: (0, 0)) for a in (expert_ids.T, copy_choice.T, probs.T, dy)],
            out_specs=pl.BlockSpec((rows, width), lambda i: (0, 0)),
            compiler_params=pltpu.CompilerParams(vmem_limit_bytes=8 * MIB),
        )(rep, expert_ids.T, copy_choice.T, probs.T, dy)
        routed = exchange(outgoing.reshape(experts, capacity, width)).reshape(rows, width)

        own_rows, partner_rows = call(
            rows_kernel,
            (shape(rows, inner), shape(rows, inner)),
            [SMEM] + [VMEM] * 5 + [ANY],
            (
                rep,
                routed,
                down,
                other_down,
                gate_rows,
                up_rows,
                high,
            ),
            2 * rows * width * inner,
            2 * inner * width,
        )
        row_blocks = (own_rows, from_partner(partner_rows))
    factor = step_scale * math.sqrt(width)
    size = half // plane
    gate, up = gate_weight[0], up_weight[0]
    own_b, *own = call(
        functools.partial(schulz_kernel, factor, len(row_blocks)),
        (shape(2 * rows, inner),) + (shape(size, inner),) * plane,
        [SMEM, SMEM, VMEM, VMEM, ANY, ANY, ANY] + [VMEM] * len(row_blocks),
        (rep, me, high, low, transposed, gate, up, *row_blocks),
        ITERS * 2 * inner * inner * (inner + 6 * rows) + 2 * half * 2 * rows * inner,
        8 * rows * inner,
        scratch=(
            pltpu.VMEM((2 * rows, inner), bf16),
            pltpu.VMEM((inner, inner), bf16),
            pltpu.VMEM((inner, inner), bf16),
            pltpu.VMEM((half, 2 * rows), bf16),
            pltpu.VMEM((half, inner), bf16),
            pltpu.SemaphoreType.DMA((3,)),
        ),
        limit=22,
    )
    other = call(
        functools.partial(update_kernel, factor),
        (shape(size, inner),) * plane,
        [SMEM, SMEM] + [VMEM] * 4,
        (rep, me, transposed, gate, up, from_partner(own_b)),
        2 * half * 2 * rows * inner,
        8 * half * inner,
    )
    if line == plane:
        spread = [across(block, d, experts) for d, block in enumerate(own)]

        def otherwise(rep, me, owner, pick_table, last_table, spread, own, other):
            pieces = cut(plane, rep, me, indirect(experts, plane, rep, me, owner, own, other))
            back = [across(block, d, experts) for d, block in enumerate(pieces[plane:])]
            return (*pieces[:plane], *back)

        branches = [
            functools.partial(direct, steps, limit, line, plane)
            for steps in range(least, limit + 1)
        ]
        pieces = lax.switch(
            branch[0],
            [otherwise] + branches,
            rep,
            me,
            new_owner,
            pick_table,
            last_table,
            spread,
            own,
            other,
        )
        other = [across(block, d, experts) for d, block in enumerate(pieces[plane:])]
        gate, up = assemble(plane, rep, me, pieces[:plane], other)
    else:
        gate, up = indirect(experts, plane, rep, me, new_owner, own, other)
    return (gate[None], up[None])


def solution(mesh):
    in_specs = (
        P("ep", None),
        P("ep", None),
        P("ep", None),
        P("ep", None),
        P("ep", "rep", None, None, None),
        P("ep", "rep", None, None, None),
        P("ep", "rep", None, None, None),
        P("ep", None, "rep"),
        P("ep", "rep", None),
        P("ep", "rep", None),
        P(),
    )
    out_specs = (P("ep", "rep", None), P("ep", "rep", None))
    return jax.shard_map(shards, mesh=mesh, in_specs=in_specs, out_specs=out_specs, check_vma=False)
```
